32 devices in a mesh: dp: 4 (over y, x), fsdp: 8 (over z, core).
Axes of the slice: x: 2, y: 2, z: 4, core: 2. Of those that a mesh axis runs over, the one named last changes fastest.
Arguments:
- tokens: bfloat16 [16384, 1024], P(('dp', 'fsdp')), may hold values from -6 to 6
- cotangent: bfloat16 [16384, 1024], P(('dp', 'fsdp')), may hold values from -6 to 6
- lengths: int32 [32, 4], P(('dp', 'fsdp')), may hold values from 1 to 256, 512 in all within a row
- scale_codes: int32 [32, 4], P(('dp', 'fsdp')), may hold values from 0 to 3
- w_qkv: bfloat16 [1024, 3072], P(('dp', 'fsdp')), may hold values from -0.1875 to 0.1875
- w_out: bfloat16 [1024, 1024], P(('dp', 'fsdp')), may hold values from -1.5 to 1.5
- w_up: bfloat16 [1024, 4096], P(('dp', 'fsdp')), may hold values from -0.1875 to 0.1875
- w_down: bfloat16 [4096, 1024], P(('dp', 'fsdp')), may hold values from -0.09375 to 0.09375
- ln1_gain: bfloat16 [1024], P(('dp', 'fsdp')), may hold values from 0.5 to 1.5
- ln1_shift: bfloat16 [1024], P(('dp', 'fsdp')), may hold values from -3 to 3
- bias_query: bfloat16 [1024], P(('dp', 'fsdp')), may hold values from -3 to 3
- bias_value: bfloat16 [1024], P(('dp', 'fsdp')), may hold values from -3 to 3
- bias_out: bfloat16 [1024], P(('dp', 'fsdp')), may hold values from -3 to 3
- ln2_gain: bfloat16 [1024], P(('dp', 'fsdp')), may hold values from 0.5 to 1.5
- ln2_shift: bfloat16 [1024], P(('dp', 'fsdp')), may hold values from -3 to 3
- bias_up: bfloat16 [4096], P(('dp', 'fsdp')), may hold values from -3 to 3
- bias_down: bfloat16 [1024], P(('dp', 'fsdp')), may hold values from -3 to 3
Outputs:
- output: bfloat16 [16384, 1024], P(('dp', 'fsdp'))
- grad_tokens: bfloat16 [16384, 1024], P(('dp', 'fsdp'))
- grad_w_qkv: float32 [1024, 3072], P(('dp', 'fsdp'))
- grad_w_out: float32 [1024, 1024], P(('dp', 'fsdp'))
- grad_w_up: float32 [1024, 4096], P(('dp', 'fsdp'))
- grad_w_down: float32 [4096, 1024], P(('dp', 'fsdp'))
- grad_ln1_gain: float32 [1024], P(('dp', 'fsdp'))
- grad_ln1_shift: float32 [1024], P(('dp', 'fsdp'))
- grad_bias_query: float32 [1024], P(('dp', 'fsdp'))
- grad_bias_value: float32 [1024], P(('dp', 'fsdp'))
- grad_bias_out: float32 [1024], P(('dp', 'fsdp'))
- grad_ln2_gain: float32 [1024], P(('dp', 'fsdp'))
- grad_ln2_shift: float32 [1024], P(('dp', 'fsdp'))
- grad_bias_up: float32 [4096], P(('dp', 'fsdp'))
- grad_bias_down: float32 [1024], P(('dp', 'fsdp'))
The draws below stay inside these ranges and needn't reach their ends.
Inputs may be any that keep to these rules, and one draw needn't show every extreme that they name: Each device's row of 4 image lengths sums to 512, and its longest image has exactly 256 patches.
All inputs are finite; a program needn't handle non-finite values.
Results may differ from the reference program's by a relative error of at most 0.012.
Values may be sent and summed in bfloat16 or wider, within the bound.
A program may use at most 192 MiB of HBM per device.

```python
import math
import jax
import jax.numpy as jnp
import numpy as np
from jax import lax

D = 1024
HEADS = 16
HEAD_DIM = 64
FF = 4096
ROWS_DEV = 512
MOST_LEN = 256
ITEMS_DEV = 4
TOKENS = 16384
N_DP = 4
N_FSDP = 8


def with_ends(values, rng, least, largest):
    spot = [jax.random.randint(jax.random.fold_in(rng, axis), (), 0, length) for axis, length in enumerate(values.shape)]
    main_axis = values.shape.index(max(values.shape))
    next_to = spot[:main_axis] + [(spot[main_axis] + 1) % values.shape[main_axis]] + spot[main_axis + 1:]
    return values.at[tuple(spot)].set(least).at[tuple(next_to)].set(largest)


def strengthened(drawn, rng, source, target, blocks, factor):
    def block_of(position):
        return (jnp.arange(drawn.shape[position]) // (drawn.shape[position] // blocks)).reshape((-1,) + (1,) * (drawn.ndim - 1 - position))

    first = jax.random.permutation(rng, blocks)[block_of(target)]
    far = (block_of(target) + blocks // 2) % blocks
    return jnp.where((block_of(source) == first) | (block_of(source) == far), factor * drawn, drawn)


def block_levels(rng, extent, pieces, least, largest):
    factor_of, own = 1.0, jax.random.fold_in(rng, 6)
    for axis_at, blocks in pieces:
        steps = jnp.exp(jax.random.uniform(jax.random.fold_in(own, axis_at), (blocks,), jnp.float32, least / len(pieces), largest / len(pieces)))
        factor_of = factor_of * jnp.repeat(steps, extent[axis_at] // blocks).reshape([-1 if axis == axis_at else 1 for axis in range(len(extent))])
    return factor_of


def split_up(amount, total, limit, slope):
    portions = [(1 << 20) // math.isqrt(rank ** slope) + 1 for rank in range(2, amount + 1)]
    rest, holding = total - limit - (amount - 1), [1] * (amount - 1)
    while rest > 0:
        movable = [i for i in range(amount - 1) if holding[i] < limit]
        pool, left = sum([portions[i] for i in movable]), rest
        for i in movable:
            extra = min(limit - holding[i], max(1, left * portions[i] // pool), rest)
            holding[i] = holding[i] + extra
            rest = rest - extra
    return np.array([limit] + holding)


def ragged_sizes(stream_key, count, total, most, slope):
    if count == 2:
        one = jax.random.randint(stream_key, (), max(1, total - most), min(most, total - 1) + 1)
        return jnp.stack([one, total - one])
    tallies = jnp.asarray(split_up(count, total, most, slope), jnp.int32)
    pairs = (count - 1) // 2
    source_of, sink = tallies[1:1 + 2 * pairs:2], tallies[2:2 + 2 * pairs:2]
    room = jnp.minimum(source_of - 1, most - sink)
    shifted = jax.random.randint(jax.random.fold_in(stream_key, 1), (pairs,), 0, 1 << 20) % (room + 1)
    tallies = tallies.at[1:1 + 2 * pairs:2].set(source_of - shifted).at[2:2 + 2 * pairs:2].set(sink + shifted)
    return tallies[jax.random.permutation(jax.random.fold_in(stream_key, 2), count)]


def bell_draw(key, dims, scale, limit, cuts=(), held_as=jnp.bfloat16):
    level = block_levels(key, dims, cuts, -0.22, 0.18) if cuts else 1.0
    array = jax.random.normal(key, dims, jnp.float32) * scale * level
    return jnp.minimum(jnp.maximum(array, -limit), limit).astype(held_as)


def heavy_noise(stream_key, shape, scale, reach, pieces, heavy, kind=jnp.bfloat16):
    drawn = scale * jax.random.normal(stream_key, shape, jnp.float32)
    if pieces:
        drawn = drawn * block_levels(stream_key, shape, pieces, -0.22, 0.18)
    return jnp.clip(strengthened(drawn, jax.random.fold_in(stream_key, 3), *heavy), -reach, reach).astype(kind)


def setup_inputs(seed: int = 0) -> dict:
    splits = jax.random.split(jax.random.key(seed), 18)
    return {
        "tokens": heavy_noise(splits[0], (TOKENS, D), 1.0, 6.0, ((0, 32),), (0, 1, 32, 2.75)),
        "cotangent": heavy_noise(splits[1], (TOKENS, D), 1.0, 6.0, ((0, 32),), (0, 1, 32, 2.75)),
        "lengths": jax.vmap(lambda own: ragged_sizes(own, ITEMS_DEV, ROWS_DEV, MOST_LEN, 2))(jax.random.split(splits[2], (N_DP * N_FSDP))).reshape((N_DP * N_FSDP, ITEMS_DEV)).astype(jnp.int32),
        "scale_codes": with_ends(jax.random.randint(splits[3], (N_DP * N_FSDP, ITEMS_DEV), 0, 4), jax.random.fold_in(splits[3], 1), 0, 3).astype(jnp.int32),
        "w_qkv": bell_draw(splits[4], (D, 3 * D), D ** -0.5, 0.1875, ((0, 32),)),
        "w_out": bell_draw(splits[5], (D, D), (D // 64) ** -0.5, 1.5, ((0, 32),)),
        "w_up": bell_draw(splits[6], (D, FF), D ** -0.5, 0.1875, ((0, 32),)),
        "w_down": bell_draw(splits[7], (FF, D), FF ** -0.5, 0.09375, ((0, 32),)),
        "ln1_gain": jnp.clip(1.0 + 0.1 * jax.random.normal(splits[8], (D,), jnp.float32), 0.5, 1.5).astype(jnp.bfloat16),
        "ln1_shift": bell_draw(splits[9], (D,), 0.5, 3.0, ((0, 32),)),
        "bias_query": bell_draw(splits[10], (D,), 0.5, 3.0, ((0, 32),)),
        "bias_value": bell_draw(splits[11], (D,), 0.5, 3.0, ((0, 32),)),
        "bias_out": bell_draw(splits[12], (D,), 0.5, 3.0, ((0, 32),)),
        "ln2_gain": jnp.clip(1.0 + 0.1 * jax.random.normal(splits[13], (D,), jnp.float32), 0.5, 1.5).astype(jnp.bfloat16),
        "ln2_shift": bell_draw(splits[14], (D,), 0.5, 3.0, ((0, 32),)),
        "bias_up": bell_draw(splits[15], (FF,), 0.5, 3.0, ((0, 32),)),
        "bias_down": bell_draw(splits[16], (D,), 0.5, 3.0, ((0, 32),)),
    }


@jax.custom_vjp
def low(v):
    return lax.optimization_barrier(v.astype(jnp.bfloat16)).astype(jnp.float32)

@jax.custom_vjp
def low_back(v):
    return v

def low_keep(v):
    return (low(v), None)

def low_pass(kept, grad):
    return (grad,)

def back_keep(v):
    return (v, None)

def back_low(kept, grad):
    return (low(grad),)
low.defvjp(low_keep, low_pass)
low_back.defvjp(back_keep, back_low)

def both_low(values):
    return low(low_back(values))

def matmul(left, right):
    return jnp.dot(left, right, precision=lax.Precision.HIGHEST)

def layer_norm(values, gain, shift):
    centred = values - lax.optimization_barrier(jnp.mean(values, axis=-1, keepdims=True))
    variance = lax.optimization_barrier(jnp.mean(centred * centred, axis=-1, keepdims=True))
    return centred * lax.rsqrt(variance + 1e-06) * gain + shift

def row_tables(length_row, code_row, row_count, feat_width):
    item_ends = jnp.cumsum(length_row).astype(jnp.int32)
    item_starts = (item_ends - length_row).astype(jnp.int32)
    row_index = jnp.arange(row_count, dtype=jnp.int32)
    member = ((row_index[:, None] >= item_starts[None, :]) & (row_index[:, None] < item_ends[None, :])).astype(jnp.int32)
    item_ids = jnp.arange(length_row.shape[0], dtype=jnp.int32)
    segment = lax.optimization_barrier(jnp.sum(member * item_ids[None, :], axis=1)).astype(jnp.int32)
    place = (row_index - lax.optimization_barrier(jnp.sum(member * item_starts[None, :], axis=1))).astype(jnp.int32)
    row_code = lax.optimization_barrier(jnp.sum(member * code_row[None, :], axis=1)).astype(jnp.int32)
    half_width = feat_width // 2
    frequency = jnp.exp(jnp.arange(half_width, dtype=jnp.float32) * (-math.log(10000.0) / half_width))
    gsd_ratio = 0.5 * (row_code.astype(jnp.float32) + 1.0)
    phase_angle = (place.astype(jnp.float32) * gsd_ratio)[:, None] * frequency[None, :]
    return (segment, jnp.concatenate([jnp.sin(phase_angle), jnp.cos(phase_angle)], axis=1))

def layer_block(rows_in, length_row, code_row, params):
    w_qkv, w_out, w_up, w_down, ln1_gain, ln1_shift, bias_query, bias_value, bias_out, ln2_gain, ln2_shift, bias_up, bias_down = params
    row_count, model_width = rows_in.shape
    head_width = model_width // HEADS
    score_scale = 1.0 / math.sqrt(HEAD_DIM)
    segment, encoding = row_tables(length_row, code_row, row_count, model_width)
    start = rows_in + encoding
    normed_one = low(layer_norm(start, ln1_gain, ln1_shift))
    qkv_bias = jnp.concatenate([bias_query, jnp.zeros_like(bias_query), bias_value])
    projected = both_low(matmul(normed_one, w_qkv) + qkv_bias)

    def split_heads(block):
        return block.reshape(row_count, HEADS, head_width).transpose(1, 0, 2)
    queries = split_heads(projected[:, :model_width])
    keys_all = split_heads(projected[:, model_width:2 * model_width])
    values_all = split_heads(projected[:, 2 * model_width:])
    scores = jnp.einsum('hqd,hkd->hqk', queries, keys_all, precision=lax.Precision.HIGHEST) * score_scale
    scores = low_back(scores)
    same_item = segment[:, None] == segment[None, :]
    scores = jnp.where(same_item[None], scores, -1e+30)
    weights = low(jax.nn.softmax(scores, axis=-1))
    attended = jnp.einsum('hqk,hkd->hqd', weights, values_all, precision=lax.Precision.HIGHEST)
    attended = both_low(attended.transpose(1, 0, 2).reshape(row_count, model_width))
    middle = start + low_back(matmul(attended, w_out) + bias_out)
    normed_two = low(layer_norm(middle, ln2_gain, ln2_shift))
    hidden_pre = low_back(matmul(normed_two, w_up) + bias_up)
    activated = low(jax.nn.gelu(hidden_pre, approximate=False))
    return middle + low_back(matmul(activated, w_down) + bias_down)

def reference(tokens, cotangent, lengths, scale_codes, w_qkv, w_out, w_up, w_down, ln1_gain, ln1_shift, bias_query, bias_value, bias_out, ln2_gain, ln2_shift, bias_up, bias_down):
    params = tuple((initial.astype(jnp.float32) for initial in (w_qkv, w_out, w_up, w_down, ln1_gain, ln1_shift, bias_query, bias_value, bias_out, ln2_gain, ln2_shift, bias_up, bias_down)))
    block_count = N_DP * N_FSDP
    blocks = tokens.astype(jnp.float32).reshape(block_count, ROWS_DEV, D)

    def forward(block_rows, weight_set):

        def one_block(operands):
            rows_in, length_row, code_row = operands
            return layer_block(rows_in, length_row, code_row, weight_set)
        return lax.map(jax.checkpoint(one_block), (block_rows, lengths, scale_codes))
    result, pull = jax.vjp(forward, blocks, params)
    grad_blocks, grad_params = pull(cotangent.astype(jnp.float32).reshape(block_count, ROWS_DEV, D))
    return (result.reshape(TOKENS, D).astype(jnp.bfloat16), grad_blocks.reshape(TOKENS, D).astype(jnp.bfloat16), grad_params[0], grad_params[1], grad_params[2], grad_params[3], grad_params[4], grad_params[5], grad_params[6], grad_params[7], grad_params[8], grad_params[9], grad_params[10], grad_params[11], grad_params[12])
```

```python
import functools
import math

import jax
import jax.numpy as jnp
from jax import lax
from jax.experimental import pallas as pl
from jax.experimental.pallas import tpu as pltpu
from jax.sharding import PartitionSpec as P

HEADS = 16
HEAD_DIM = 64


EPSILON = 1e-06


def contract(left, right, left_dim, right_dim):
    return lax.dot_general(
        left, right, (((left_dim,), (right_dim,)), ((), ())), preferred_element_type=jnp.float32
    )


def layer_norm(values, gain, shift):
    centred = values - jnp.mean(values, axis=-1, keepdims=True)
    variance = jnp.mean(centred * centred, axis=-1, keepdims=True)
    return centred * lax.rsqrt(variance + EPSILON) * gain + shift


def gelu_exact(values):
    return jax.nn.gelu(values, approximate=False)


def row_tables(length_row, code_row, row_count, feat_width):
    items = jnp.arange(length_row.shape[0], dtype=jnp.int32)
    item_starts = jnp.sum(
        jnp.where(items[None, :] < items[:, None], length_row[None, :], 0), axis=1
    )
    item_ends = item_starts + length_row
    row_index = jnp.arange(row_count, dtype=jnp.int32)
    member = (
        (row_index[:, None] >= item_starts[None, :]) & (row_index[:, None] < item_ends[None, :])
    ).astype(jnp.int32)
    item_ids = jnp.arange(length_row.shape[0], dtype=jnp.int32)
    segment = jnp.sum(member * item_ids[None, :], axis=1)
    place = row_index - jnp.sum(member * item_starts[None, :], axis=1)
    row_code = jnp.sum(member * code_row[None, :], axis=1)
    half_width = feat_width // 2
    frequency = jnp.exp(
        jnp.arange(half_width, dtype=jnp.float32) * (-math.log(10000.0) / half_width)
    )
    gsd_ratio = 0.5 * (row_code.astype(jnp.float32) + 1.0)
    phase_angle = (place.astype(jnp.float32) * gsd_ratio)[:, None] * frequency[None, :]
    return (segment, jnp.concatenate([jnp.sin(phase_angle), jnp.cos(phase_angle)], axis=1))


PLANE = 2
CORES = 2
UNIT = 1024 * 1024
MESH = pl.DeviceIdType.MESH
ALL = slice(None)


def plain_gather(matrices, vectors):
    return tuple(lax.all_gather(v, ("dp", "fsdp"), axis=0, tiled=True) for v in matrices + vectors)


def plain_scatter(matrices, vectors):
    return tuple(
        lax.psum_scatter(v, ("dp", "fsdp"), scatter_dimension=0, tiled=True)
        for v in matrices + vectors
    )


class Place:
    def __init__(self, depth):
        dp, fsdp = lax.axis_index("dp"), lax.axis_index("fsdp")
        self.y, self.x = dp // PLANE, lax.rem(dp, PLANE)
        self.z, self.c = fsdp // CORES, lax.rem(fsdp, CORES)
        self.depth = depth
        y, x, z, c = self.y, self.x, self.z, self.c
        self.along_x = self.device(y, 1 - x, z, c)
        self.along_y = self.device(1 - y, x, z, c)
        self.other_core = self.device(y, x, z, 1 - c)
        self.ahead = [lax.rem(z + k, depth) for k in range(1, depth)]
        self.behind = [lax.rem(z + depth - k, depth) for k in range(1, depth)]

    def device(self, y, x, z, c):
        return (y * PLANE + x, z * CORES + c)

    def column(self, z):
        return self.device(self.y, self.x, z, self.c)

    def greet(self):
        partners = [self.column(q) for q in self.ahead]
        partners += [self.along_x, self.along_y, self.other_core]
        barrier = pltpu.get_barrier_semaphore()
        for partner in partners:
            pl.semaphore_signal(barrier, inc=1, device_id=partner, device_id_type=MESH)
        pl.semaphore_wait(barrier, len(partners))


class Mail:
    def __init__(self, send_sem, recv_sem):
        self.send_sem, self.recv_sem, self.sent = send_sem, recv_sem, []

    def copy(self, unit, slot, source, target, device):
        return pltpu.make_async_remote_copy(
            src_ref=source,
            dst_ref=target,
            send_sem=self.send_sem.at[unit, slot],
            recv_sem=self.recv_sem.at[unit, slot],
            device_id=device,
            device_id_type=MESH,
        )

    def send(self, unit, slot, source, target, device):
        copy = self.copy(unit, slot, source, target, device)
        copy.start()
        self.sent.append(copy)

    def arrived(self, unit, slot, target, device):
        self.copy(unit, slot, target, target, device).wait_recv()

    def finish(self):
        for copy in self.sent:
            copy.wait_send()


SLOTS = 12


def unit_list(shapes):
    units = []
    for index, (rows, columns) in enumerate(shapes):
        width = UNIT // rows
        units += [(index, first, width) for first in range(0, columns, width)]
    return units


def gather_phases(place, mail, unit, source, full, local_sem):
    y, x, z, c = place.y, place.x, place.z, place.c
    nz = place.depth - 1

    def first():
        pltpu.make_async_copy(source, full(y, x, z, c, ALL), local_sem).start()
        for k in range(nz):
            mail.send(unit, k, source, full(y, x, z, c, ALL), place.column(place.ahead[k]))

    def second():
        pltpu.make_async_copy(source, full(y, x, z, c, ALL), local_sem).wait()
        for k in range(nz):
            q = place.behind[k]
            mail.arrived(unit, k, full(y, x, q, c, ALL), place.column(q))
        mail.send(unit, 3, full(y, x, ALL, c, 0), full(y, x, ALL, c, 0), place.along_x)
        mail.send(unit, 4, full(y, x, ALL, c, 1), full(y, x, ALL, c, 1), place.along_y)

    def third():
        mail.arrived(unit, 3, full(y, 1 - x, ALL, c, 0), place.along_x)
        mail.send(unit, 5, full(y, ALL, ALL, c, 0), full(y, ALL, ALL, c, 0), place.along_y)
        mail.arrived(unit, 4, full(1 - y, x, ALL, c, 1), place.along_y)
        mail.send(unit, 6, full(ALL, x, ALL, c, 1), full(ALL, x, ALL, c, 1), place.along_x)

    def fourth():
        mail.arrived(unit, 5, full(1 - y, ALL, ALL, c, 0), place.along_y)
        mail.arrived(unit, 6, full(ALL, 1 - x, ALL, c, 1), place.along_x)
        mail.send(unit, 7, full(ALL, ALL, ALL, c, ALL), full(ALL, ALL, ALL, c, ALL), place.other_core)

    def last():
        mail.arrived(unit, 7, full(ALL, ALL, ALL, 1 - c, ALL), place.other_core)

    return first, second, third, fourth, last


def small_gather_phases(place, mail, unit, source, full, local_sem):
    y, x, z, c = place.y, place.x, place.z, place.c
    nz = place.depth - 1

    def first():
        pltpu.make_async_copy(source, full.at[y, x, z, c], local_sem).start()
        for k in range(nz):
            mail.send(unit, k, source, full.at[y, x, z, c], place.column(place.ahead[k]))

    def second():
        pltpu.make_async_copy(source, full.at[y, x, z, c], local_sem).wait()
        for k in range(nz):
            q = place.behind[k]
            mail.arrived(unit, k, full.at[y, x, q, c], place.column(q))
        mail.send(unit, 3, full.at[y, x, :, c], full.at[y, x, :, c], place.along_x)

    def third():
        mail.arrived(unit, 3, full.at[y, 1 - x, :, c], place.along_x)
        mail.send(unit, 5, full.at[y, :, :, c], full.at[y, :, :, c], place.along_y)

    def fourth():
        mail.arrived(unit, 5, full.at[1 - y, :, :, c], place.along_y)
        mail.send(unit, 7, full.at[:, :, :, c], full.at[:, :, :, c], place.other_core)

    def last():
        mail.arrived(unit, 7, full.at[:, :, :, 1 - c], place.other_core)

    return first, second, third, fourth, last


def gather_kernel(depth, units, count, *refs):
    sources, small = refs[:count], refs[count]
    fulls, small_full = refs[count + 1 : 2 * count + 1], refs[2 * count + 1]
    send_sem, recv_sem, local_sem = refs[2 * count + 2 :]
    place, mail = Place(depth), Mail(send_sem, recv_sem)
    place.greet()
    steps = [small_gather_phases(place, mail, 0, small, small_full, local_sem.at[0])]
    for unit, (index, first, width) in enumerate(units, 1):
        span = pl.ds(first, width)

        def view(*at, ref=fulls[index], span=span):
            return ref.at[at + (ALL, span)]

        steps.append(
            gather_phases(
                place, mail, unit, sources[index].at[:, :, span], view, local_sem.at[unit]
            )
        )
    for turn in range(len(steps) + 4):
        for phase in range(5):
            if 0 <= turn - phase < len(steps):
                steps[turn - phase][phase]()
    mail.finish()


def grid_gather(mesh):
    depth = mesh.shape["fsdp"] // CORES
    grid = (PLANE, PLANE, depth, CORES)
    devices = mesh.size

    def gather(matrices, vectors):
        count = len(matrices)
        halves = [m.reshape(2, m.shape[0] // 2, m.shape[1]) for m in matrices]
        units = unit_list([(m.shape[0] * devices, m.shape[1]) for m in matrices])
        flat = jnp.concatenate([vectors[-1], *vectors[:-1]]).astype(jnp.float32)
        small = jnp.pad(flat, (0, 1024 - flat.size)).reshape(8, 128)
        outs = pl.pallas_call(
            functools.partial(gather_kernel, depth, units, count),
            out_shape=[jax.ShapeDtypeStruct(grid + h.shape, h.dtype) for h in halves]
            + [jax.ShapeDtypeStruct(grid + small.shape, small.dtype)],
            in_specs=[pl.BlockSpec(memory_space=pl.ANY)] * (count + 1),
            out_specs=[pl.BlockSpec(memory_space=pl.ANY)] * (count + 1),
            scratch_shapes=[
                pltpu.SemaphoreType.DMA((len(units) + 1, SLOTS)),
                pltpu.SemaphoreType.DMA((len(units) + 1, SLOTS)),
                pltpu.SemaphoreType.DMA((len(units) + 1,)),
            ],
            compiler_params=pltpu.CompilerParams(collective_id=0, has_side_effects=True),
        )(*halves, small)
        fulls = [o.reshape(-1, o.shape[-1]) for o in outs[:count]]
        table = outs[count].reshape(devices, -1)
        wide = vectors[-1].shape[0]
        narrow = vectors[0].shape[0]
        spread = [
            table[:, wide + narrow * k : wide + narrow * (k + 1)].reshape(-1).astype(jnp.bfloat16)
            for k in range(len(vectors) - 1)
        ]
        return (*fulls, *spread, table[:, :wide].reshape(-1).astype(jnp.bfloat16))

    return gather


def scatter_kernel(depth, units, count, *refs):
    parts, small = refs[:count], refs[count]
    outs, small_out = refs[count + 1 : 2 * count + 1], refs[2 * count + 1]
    (core_in, own, wide_in, near_in, column_in, result, small_core, small_own, small_wide, small_near,
     small_column, small_result, send_sem, recv_sem, local_sem) = refs[2 * count + 2 :]
    place, mail = Place(depth), Mail(send_sem, recv_sem)
    y, x, z, c = place.y, place.x, place.z, place.c
    place.greet()
    nz = depth - 1
    steps = []

    def small_steps():
        unit = 0

        def first():
            mail.send(unit, 7, small.at[:, :, :, 1 - c], small_core, place.other_core)
            pltpu.make_async_copy(small.at[:, :, :, c], small_own, local_sem.at[unit]).start()

        def second():
            mail.arrived(unit, 7, small_core, place.other_core)
            pltpu.make_async_copy(small.at[:, :, :, c], small_own, local_sem.at[unit]).wait()
            small_own[...] += small_core[...]
            mail.send(unit, 5, small_own.at[1 - y], small_wide, place.along_y)

        def third():
            mail.arrived(unit, 5, small_wide, place.along_y)
            small_own[y] += small_wide[...]
            mail.send(unit, 3, small_own.at[y, 1 - x], small_near, place.along_x)

        def fourth():
            mail.arrived(unit, 3, small_near, place.along_x)
            small_own[y, x] += small_near[...]
            for k in range(nz):
                q = place.ahead[k]
                mail.send(unit, k, small_own.at[y, x, q], small_column.at[k], place.column(q))

        def last():
            total = small_own[y, x, z]
            for k in range(nz):
                mail.arrived(unit, k, small_column.at[k], place.column(place.behind[k]))
                total = total + small_column[k]
            small_result[...] = total
            pltpu.make_async_copy(small_result, small_out, local_sem.at[unit]).start()

        def ended():
            pltpu.make_async_copy(small_result, small_out, local_sem.at[unit]).wait()

        return first, second, third, fourth, last, ended

    def unit_steps(unit, index, at):
        _, start, width = units[unit - 1]
        span = pl.ds(start, width)
        part = parts[index]
        rows = part.shape[-2]
        shape = (PLANE, PLANE, depth, 2, rows, width)
        other = part.at[:, :, :, 1 - c, :, :, span]
        mine = part.at[:, :, :, c, :, :, span]
        inbox, held = core_in[index].at[at], own[index].at[at]
        wide, near, column = wide_in[index].at[at], near_in[index].at[at], column_in[index].at[at]
        final = result[index].at[at]
        target = outs[index].at[:, :, span]
        local = pltpu.make_async_copy(mine, held, local_sem.at[unit])
        outward = pltpu.make_async_copy(final, target, local_sem.at[unit])

        def first():
            mail.send(unit, 7, other, inbox, place.other_core)
            local.start()

        def second():
            mail.arrived(unit, 7, inbox, place.other_core)
            local.wait()
            for a in range(PLANE):
                for b in range(PLANE):
                    held[a, b] = held[a, b] + inbox[a, b]
            mail.send(unit, 5, held.at[1 - y, :, :, 0], wide.at[0], place.along_y)
            mail.send(unit, 6, held.at[:, 1 - x, :, 1], wide.at[1], place.along_x)

        def third():
            mail.arrived(unit, 5, wide.at[0], place.along_y)
            mail.arrived(unit, 6, wide.at[1], place.along_x)
            for b in range(PLANE):
                held[y, b, :, 0] = held[y, b, :, 0] + wide[0, b]
                held[b, x, :, 1] = held[b, x, :, 1] + wide[1, b]
            mail.send(unit, 3, held.at[y, 1 - x, :, 0], near.at[0], place.along_x)
            mail.send(unit, 4, held.at[1 - y, x, :, 1], near.at[1], place.along_y)

        def fourth():
            mail.arrived(unit, 3, near.at[0], place.along_x)
            mail.arrived(unit, 4, near.at[1], place.along_y)
            for h in range(2):
                held[y, x, :, h] = held[y, x, :, h] + near[h]
            for k in range(nz):
                q = place.ahead[k]
                mail.send(unit, k, held.at[y, x, q], column.at[k], place.column(q))

        def last():
            total = held[y, x, z].astype(jnp.float32)
            for k in range(nz):
                mail.arrived(unit, k, column.at[k], place.column(place.behind[k]))
                total = total + column[k].astype(jnp.float32)
            final[...] = total
            outward.start()

        def ended():
            outward.wait()

        return first, second, third, fourth, last, ended

    seen = [0] * count
    for unit, (index, _, _) in enumerate(units, 1):
        steps.append(unit_steps(unit, index, seen[index]))
        seen[index] += 1
    steps.append(small_steps())
    for turn in range(len(steps) + 5):
        for phase in range(6):
            if 0 <= turn - phase < len(steps):
                steps[turn - phase][phase]()
    mail.finish()


def grid_scatter(mesh):
    depth = mesh.shape["fsdp"] // CORES
    grid = (PLANE, PLANE, depth, CORES)
    devices = mesh.size

    def scatter(matrices, vectors):
        count = len(matrices)
        shapes = [m.shape for m in matrices]
        units = unit_list(shapes)[::-1]
        parts = [
            m.astype(jnp.bfloat16).reshape(grid + (2, m.shape[0] // devices // 2, m.shape[1]))
            for m in matrices
        ]
        wide, narrow = vectors[-1].size // devices, vectors[0].size // devices
        table = jnp.concatenate(
            [vectors[-1].reshape(devices, wide)] + [v.reshape(devices, narrow) for v in vectors[:-1]],
            axis=1,
        )
        table = jnp.pad(table, ((0, 0), (0, 1024 - table.shape[1]))).reshape(grid + (8, 128))
        amounts = [sum(u[0] == index for u in units) for index in range(count)]
        sizes = [(rows // devices // 2, UNIT // rows) for rows, _ in shapes]

        def buffers(*lead, dtype=jnp.bfloat16):
            return [pltpu.VMEM((n, *lead, *size), dtype) for n, size in zip(amounts, sizes)]

        def small(*lead):
            return pltpu.VMEM((*lead, 8, 128), jnp.float32)

        total = len(units) + 1
        outs = pl.pallas_call(
            functools.partial(scatter_kernel, depth, units, count),
            out_shape=[
                jax.ShapeDtypeStruct((2, rows // devices // 2, columns), jnp.float32)
                for rows, columns in shapes
            ]
            + [jax.ShapeDtypeStruct((8, 128), jnp.float32)],
            in_specs=[pl.BlockSpec(memory_space=pl.ANY)] * (count + 1),
            out_specs=[pl.BlockSpec(memory_space=pl.ANY)] * (count + 1),
            scratch_shapes=[
                buffers(PLANE, PLANE, depth, 2),
                buffers(PLANE, PLANE, depth, 2),
                buffers(2, PLANE, depth),
                buffers(2, depth),
                buffers(depth - 1, 2),
                buffers(2, dtype=jnp.float32),
                small(PLANE, PLANE, depth),
                small(PLANE, PLANE, depth),
                small(PLANE, depth),
                small(depth),
                small(depth - 1),
                small(),
                pltpu.SemaphoreType.DMA((total, SLOTS)),
                pltpu.SemaphoreType.DMA((total, SLOTS)),
                pltpu.SemaphoreType.DMA((total,)),
            ],
            compiler_params=pltpu.CompilerParams(
                collective_id=1, has_side_effects=True, vmem_limit_bytes=56 << 20
            ),
        )(*parts, table)
        spread = outs[count].reshape(-1)
        return (
            *(o.reshape(-1, o.shape[-1]) for o in outs[:count]),
            *(spread[wide + narrow * k : wide + narrow * (k + 1)] for k in range(len(vectors) - 1)),
            spread[:wide],
        )

    return scatter


def body(
    gather,
    scatter,
    tokens,
    cotangent,
    lengths,
    scale_codes,
    w_qkv,
    w_out,
    w_up,
    w_down,
    ln1_gain,
    ln1_shift,
    bias_query,
    bias_value,
    bias_out,
    ln2_gain,
    ln2_shift,
    bias_up,
    bias_down,
):
    gathered = gather(
        (w_qkv, w_out, w_up, w_down),
        (
            ln1_gain,
            ln1_shift,
            bias_query,
            bias_value,
            bias_out,
            ln2_gain,
            ln2_shift,
            bias_down,
            bias_up,
        ),
    )
    (
        full_qkv,
        full_out,
        full_up,
        full_down,
        gain_first,
        shift_first,
        query_bias,
        value_bias,
        out_bias,
        gain_second,
        shift_second,
        down_bias,
        up_bias,
    ) = gathered
    gain_one = gain_first.astype(jnp.float32)
    shift_one = shift_first.astype(jnp.float32)
    gain_two = gain_second.astype(jnp.float32)
    shift_two = shift_second.astype(jnp.float32)
    row_count, model_width = tokens.shape
    head_width = model_width // HEADS
    score_scale = 1.0 / math.sqrt(HEAD_DIM)
    segment, encoding = row_tables(lengths[0], scale_codes[0], row_count, model_width)
    same_item = segment[:, None] == segment[None, :]
    start = tokens.astype(jnp.float32) + encoding
    normed_one = layer_norm(start, gain_one, shift_one).astype(jnp.bfloat16)
    qkv_bias = jnp.concatenate([query_bias, jnp.zeros_like(query_bias), value_bias]).astype(
        jnp.float32
    )
    projected = (
        jnp.dot(normed_one, full_qkv, preferred_element_type=jnp.float32) + qkv_bias
    ).astype(jnp.bfloat16)

    def split_heads(block):
        return block.reshape(row_count, HEADS, head_width).transpose(1, 0, 2)

    def join_heads(block):
        return block.transpose(1, 0, 2).reshape(row_count, model_width)

    query_heads = split_heads(projected[:, :model_width])
    key_heads = split_heads(projected[:, model_width : 2 * model_width])
    value_heads = split_heads(projected[:, 2 * model_width :])

    def forward_head(operands):
        query_head, key_head, value_head = operands
        scores = contract(query_head, key_head, 1, 1) * score_scale
        scores = jnp.where(same_item, scores, -1e30)
        top_score = jnp.max(scores, axis=1, keepdims=True)
        expon = jnp.exp(scores - top_score)
        total = jnp.sum(expon, axis=1, keepdims=True)
        weights_low = (expon / total).astype(jnp.bfloat16)
        result = jnp.dot(weights_low, value_head, preferred_element_type=jnp.float32)
        return (result, (top_score + jnp.log(total))[:, 0])

    attended_heads, log_totals = lax.map(forward_head, (query_heads, key_heads, value_heads))
    attended = join_heads(attended_heads).astype(jnp.bfloat16)
    middle = (
        start
        + jnp.dot(attended, full_out, preferred_element_type=jnp.float32)
        + out_bias.astype(jnp.float32)
    )
    normed_two = layer_norm(middle, gain_two, shift_two).astype(jnp.bfloat16)
    hidden_pre = jnp.dot(normed_two, full_up, preferred_element_type=jnp.float32) + up_bias.astype(
        jnp.float32
    )
    activated = gelu_exact(hidden_pre).astype(jnp.bfloat16)
    feed_out = jnp.dot(activated, full_down, preferred_element_type=jnp.float32) + down_bias.astype(
        jnp.float32
    )
    output = (middle + feed_out).astype(jnp.bfloat16)
    back_qkv, back_out, back_up, back_down = full_qkv, full_out, full_up, full_down
    grad_output = cotangent.astype(jnp.float32)
    grad_down_bias = jnp.sum(grad_output, axis=0)
    grad_down = contract(activated, cotangent, 0, 0)
    grad_act = contract(cotangent, back_down, 1, 1)
    gelu_value, gelu_pull = jax.vjp(gelu_exact, hidden_pre)
    grad_hidden = gelu_pull(grad_act)[0].astype(jnp.bfloat16)
    grad_up_bias = jnp.sum(grad_hidden.astype(jnp.float32), axis=0)
    grad_up = contract(normed_two, grad_hidden, 0, 0)
    grad_normed_two = contract(grad_hidden, back_up, 1, 1)
    norm_value, second_pull = jax.vjp(layer_norm, middle, gain_two, shift_two)
    grad_middle_part, grad_gain_two, grad_shift_two = second_pull(grad_normed_two)
    grad_middle = grad_output + grad_middle_part
    branch_grad = grad_middle.astype(jnp.bfloat16)
    grad_out_bias = jnp.sum(branch_grad.astype(jnp.float32), axis=0)
    grad_out_weight = contract(attended, branch_grad, 0, 0)
    grad_attended = contract(branch_grad, back_out, 1, 1).astype(jnp.bfloat16)
    grad_heads = split_heads(grad_attended)

    def backward_head(operands):
        query_head, key_head, value_head, grad_head, log_total = operands
        scores = contract(query_head, key_head, 1, 1) * score_scale
        weights = jnp.where(same_item, jnp.exp(scores - log_total[:, None]), 0.0)
        weights_low = weights.astype(jnp.bfloat16)
        grad_weights = contract(grad_head, value_head, 1, 1)
        grad_value = contract(weights_low, grad_head, 0, 0)
        grad_scores = weights * (
            grad_weights - jnp.sum(weights * grad_weights, axis=1, keepdims=True)
        )
        grad_scores_low = grad_scores.astype(jnp.bfloat16)
        grad_query = (
            jnp.dot(grad_scores_low, key_head, preferred_element_type=jnp.float32) * score_scale
        )
        grad_key = contract(grad_scores_low, query_head, 0, 0) * score_scale
        return (grad_query, grad_key, grad_value)

    grad_query_heads, grad_key_heads, grad_value_heads = lax.map(
        backward_head, (query_heads, key_heads, value_heads, grad_heads, log_totals)
    )
    grad_projected = jnp.concatenate(
        [join_heads(grad_query_heads), join_heads(grad_key_heads), join_heads(grad_value_heads)],
        axis=1,
    ).astype(jnp.bfloat16)
    grad_query_bias = jnp.sum(grad_projected[:, :model_width].astype(jnp.float32), axis=0)
    grad_value_bias = jnp.sum(grad_projected[:, 2 * model_width :].astype(jnp.float32), axis=0)
    grad_qkv = contract(normed_one, grad_projected, 0, 0)
    grad_normed_one = contract(grad_projected, back_qkv, 1, 1)
    first_value, first_pull = jax.vjp(layer_norm, start, gain_one, shift_one)
    grad_start_part, grad_gain_one, grad_shift_one = first_pull(grad_normed_one)
    grad_tokens = (grad_middle + grad_start_part).astype(jnp.bfloat16)
    every_grad = scatter(
        (grad_qkv, grad_out_weight, grad_up, grad_down),
        (
            grad_gain_one,
            grad_shift_one,
            grad_query_bias,
            grad_value_bias,
            grad_out_bias,
            grad_gain_two,
            grad_shift_two,
            grad_down_bias,
            grad_up_bias,
        ),
    )
    (
        shard_qkv,
        shard_out,
        shard_up,
        shard_down,
        shard_gain_one,
        shard_shift_one,
        shard_query_bias,
        shard_value_bias,
        shard_out_bias,
        shard_gain_two,
        shard_shift_two,
        shard_down_bias,
        shard_up_bias,
    ) = every_grad
    return (
        output,
        grad_tokens,
        shard_qkv,
        shard_out,
        shard_up,
        shard_down,
        shard_gain_one,
        shard_shift_one,
        shard_query_bias,
        shard_value_bias,
        shard_out_bias,
        shard_gain_two,
        shard_shift_two,
        shard_up_bias,
        shard_down_bias,
    )


def solution(mesh):
    placed = (
        P(("dp", "fsdp"), None),
        P(("dp", "fsdp"), None),
        P(("dp", "fsdp"), None),
        P(("dp", "fsdp"), None),
        P(("dp", "fsdp"), None),
        P(("dp", "fsdp"), None),
        P(("dp", "fsdp"), None),
        P(("dp", "fsdp"), None),
        P(("dp", "fsdp")),
        P(("dp", "fsdp")),
        P(("dp", "fsdp")),
        P(("dp", "fsdp")),
        P(("dp", "fsdp")),
        P(("dp", "fsdp")),
        P(("dp", "fsdp")),
        P(("dp", "fsdp")),
        P(("dp", "fsdp")),
    )
    gather, scatter = plain_gather, plain_scatter
    if mesh.shape["dp"] == PLANE * PLANE and mesh.shape["fsdp"] % CORES == 0 and mesh.shape["fsdp"] <= 8:
        gather, scatter = grid_gather(mesh), grid_scatter(mesh)
    return jax.shard_map(
        functools.partial(body, gather, scatter),
        mesh=mesh,
        in_specs=placed,
        out_specs=(
            P(("dp", "fsdp"), None),
            P(("dp", "fsdp"), None),
            P(("dp", "fsdp"), None),
            P(("dp", "fsdp"), None),
            P(("dp", "fsdp"), None),
            P(("dp", "fsdp"), None),
            P(("dp", "fsdp")),
            P(("dp", "fsdp")),
            P(("dp", "fsdp")),
            P(("dp", "fsdp")),
            P(("dp", "fsdp")),
            P(("dp", "fsdp")),
            P(("dp", "fsdp")),
            P(("dp", "fsdp")),
            P(("dp", "fsdp")),
        ),
        check_vma=False,
    )
```

```python
import functools
import math

import jax
import jax.numpy as jnp
from jax import lax
from jax.experimental import pallas as pl
from jax.experimental.pallas import tpu as pltpu
from jax.sharding import PartitionSpec as P

HEADS = 16
HEAD_DIM = 64


EPSILON = 1e-06


def contract(left, right, left_dim, right_dim):
    return lax.dot_general(
        left, right, (((left_dim,), (right_dim,)), ((), ())), preferred_element_type=jnp.float32
    )


def layer_norm(values, gain, shift):
    centred = values - jnp.mean(values, axis=-1, keepdims=True)
    variance = jnp.mean(centred * centred, axis=-1, keepdims=True)
    return centred * lax.rsqrt(variance + EPSILON) * gain + shift


def gelu_exact(values):
    return jax.nn.gelu(values, approximate=False)


def row_tables(length_row, code_row, row_count, feat_width):
    items = jnp.arange(length_row.shape[0], dtype=jnp.int32)
    item_starts = jnp.sum(
        jnp.where(items[None, :] < items[:, None], length_row[None, :], 0), axis=1
    )
    item_ends = item_starts + length_row
    row_index = jnp.arange(row_count, dtype=jnp.int32)
    member = (
        (row_index[:, None] >= item_starts[None, :]) & (row_index[:, None] < item_ends[None, :])
    ).astype(jnp.int32)
    item_ids = jnp.arange(length_row.shape[0], dtype=jnp.int32)
    segment = jnp.sum(member * item_ids[None, :], axis=1)
    place = row_index - jnp.sum(member * item_starts[None, :], axis=1)
    row_code = jnp.sum(member * code_row[None, :], axis=1)
    half_width = feat_width // 2
    frequency = jnp.exp(
        jnp.arange(half_width, dtype=jnp.float32) * (-math.log(10000.0) / half_width)
    )
    gsd_ratio = 0.5 * (row_code.astype(jnp.float32) + 1.0)
    phase_angle = (place.astype(jnp.float32) * gsd_ratio)[:, None] * frequency[None, :]
    return (segment, jnp.concatenate([jnp.sin(phase_angle), jnp.cos(phase_angle)], axis=1))


def body(
    tokens,
    cotangent,
    lengths,
    scale_codes,
    w_qkv,
    w_out,
    w_up,
    w_down,
    ln1_gain,
    ln1_shift,
    bias_query,
    bias_value,
    bias_out,
    ln2_gain,
    ln2_shift,
    bias_up,
    bias_down,
):
    gathered = (
        lax.all_gather(w_qkv, ("dp", "fsdp"), axis=0, tiled=True),
        lax.all_gather(w_out, ("dp", "fsdp"), axis=0, tiled=True),
        lax.all_gather(w_up, ("dp", "fsdp"), axis=0, tiled=True),
        lax.all_gather(w_down, ("dp", "fsdp"), axis=0, tiled=True),
        lax.all_gather(ln1_gain, ("dp", "fsdp"), axis=0, tiled=True),
        lax.all_gather(ln1_shift, ("dp", "fsdp"), axis=0, tiled=True),
        lax.all_gather(bias_query, ("dp", "fsdp"), axis=0, tiled=True),
        lax.all_gather(bias_value, ("dp", "fsdp"), axis=0, tiled=True),
        lax.all_gather(bias_out, ("dp", "fsdp"), axis=0, tiled=True),
        lax.all_gather(ln2_gain, ("dp", "fsdp"), axis=0, tiled=True),
        lax.all_gather(ln2_shift, ("dp", "fsdp"), axis=0, tiled=True),
        lax.all_gather(bias_up, ("dp", "fsdp"), axis=0, tiled=True),
        lax.all_gather(bias_down, ("dp", "fsdp"), axis=0, tiled=True),
    )
    (
        full_qkv,
        full_out,
        full_up,
        full_down,
        gain_first,
        shift_first,
        query_bias,
        value_bias,
        out_bias,
        gain_second,
        shift_second,
        up_bias,
        down_bias,
    ) = gathered
    gain_one = gain_first.astype(jnp.float32)
    shift_one = shift_first.astype(jnp.float32)
    gain_two = gain_second.astype(jnp.float32)
    shift_two = shift_second.astype(jnp.float32)
    row_count, model_width = tokens.shape
    head_width = model_width // HEADS
    score_scale = 1.0 / math.sqrt(HEAD_DIM)
    segment, encoding = row_tables(lengths[0], scale_codes[0], row_count, model_width)
    same_item = segment[:, None] == segment[None, :]
    start = tokens.astype(jnp.float32) + encoding
    normed_one = layer_norm(start, gain_one, shift_one).astype(jnp.bfloat16)
    qkv_bias = jnp.concatenate([query_bias, jnp.zeros_like(query_bias), value_bias]).astype(
        jnp.float32
    )
    projected = (
        jnp.dot(normed_one, full_qkv, preferred_element_type=jnp.float32) + qkv_bias
    ).astype(jnp.bfloat16)

    def split_heads(block):
        return block.reshape(row_count, HEADS, head_width).transpose(1, 0, 2)

    def join_heads(block):
        return block.transpose(1, 0, 2).reshape(row_count, model_width)

    query_heads = split_heads(projected[:, :model_width])
    key_heads = split_heads(projected[:, model_width : 2 * model_width])
    value_heads = split_heads(projected[:, 2 * model_width :])

    def forward_head(operands):
        query_head, key_head, value_head = operands
        scores = contract(query_head, key_head, 1, 1) * score_scale
        scores = jnp.where(same_item, scores, -1e30)
        top_score = jnp.max(scores, axis=1, keepdims=True)
        expon = jnp.exp(scores - top_score)
        total = jnp.sum(expon, axis=1, keepdims=True)
        weights_low = (expon / total).astype(jnp.bfloat16)
        result = jnp.dot(weights_low, value_head, preferred_element_type=jnp.float32)
        return (result, (top_score + jnp.log(total))[:, 0])

    attended_heads, log_totals = lax.map(forward_head, (query_heads, key_heads, value_heads))
    attended = join_heads(attended_heads).astype(jnp.bfloat16)
    middle = (
        start
        + jnp.dot(attended, full_out, preferred_element_type=jnp.float32)
        + out_bias.astype(jnp.float32)
    )
    normed_two = layer_norm(middle, gain_two, shift_two).astype(jnp.bfloat16)
    hidden_pre = jnp.dot(normed_two, full_up, preferred_element_type=jnp.float32) + up_bias.astype(
        jnp.float32
    )
    activated = gelu_exact(hidden_pre).astype(jnp.bfloat16)
    feed_out = jnp.dot(activated, full_down, preferred_element_type=jnp.float32) + down_bias.astype(
        jnp.float32
    )
    output = (middle + feed_out).astype(jnp.bfloat16)
    back_qkv, back_out, back_up, back_down = (
        lax.all_gather(w_qkv, ("dp", "fsdp"), axis=0, tiled=True),
        lax.all_gather(w_out, ("dp", "fsdp"), axis=0, tiled=True),
        lax.all_gather(w_up, ("dp", "fsdp"), axis=0, tiled=True),
        lax.all_gather(w_down, ("dp", "fsdp"), axis=0, tiled=True),
    )
    grad_output = cotangent.astype(jnp.float32)
    grad_down_bias = jnp.sum(grad_output, axis=0)
    grad_down = contract(activated, cotangent, 0, 0)
    grad_act = contract(cotangent, back_down, 1, 1)
    gelu_value, gelu_pull = jax.vjp(gelu_exact, hidden_pre)
    grad_hidden = gelu_pull(grad_act)[0].astype(jnp.bfloat16)
    grad_up_bias = jnp.sum(grad_hidden.astype(jnp.float32), axis=0)
    grad_up = contract(normed_two, grad_hidden, 0, 0)
    grad_normed_two = contract(grad_hidden, back_up, 1, 1)
    norm_value, second_pull = jax.vjp(layer_norm, middle, gain_two, shift_two)
    grad_middle_part, grad_gain_two, grad_shift_two = second_pull(grad_normed_two)
    grad_middle = grad_output + grad_middle_part
    branch_grad = grad_middle.astype(jnp.bfloat16)
    grad_out_bias = jnp.sum(branch_grad.astype(jnp.float32), axis=0)
    grad_out_weight = contract(attended, branch_grad, 0, 0)
    grad_attended = contract(branch_grad, back_out, 1, 1).astype(jnp.bfloat16)
    grad_heads = split_heads(grad_attended)

    def backward_head(operands):
        query_head, key_head, value_head, grad_head, log_total = operands
        scores = contract(query_head, key_head, 1, 1) * score_scale
        weights = jnp.where(same_item, jnp.exp(scores - log_total[:, None]), 0.0)
        weights_low = weights.astype(jnp.bfloat16)
        grad_weights = contract(grad_head, value_head, 1, 1)
        grad_value = contract(weights_low, grad_head, 0, 0)
        grad_scores = weights * (
            grad_weights - jnp.sum(weights * grad_weights, axis=1, keepdims=True)
        )
        grad_scores_low = grad_scores.astype(jnp.bfloat16)
        grad_query = (
            jnp.dot(grad_scores_low, key_head, preferred_element_type=jnp.float32) * score_scale
        )
        grad_key = contract(grad_scores_low, query_head, 0, 0) * score_scale
        return (grad_query, grad_key, grad_value)

    grad_query_heads, grad_key_heads, grad_value_heads = lax.map(
        backward_head, (query_heads, key_heads, value_heads, grad_heads, log_totals)
    )
    grad_projected = jnp.concatenate(
        [join_heads(grad_query_heads), join_heads(grad_key_heads), join_heads(grad_value_heads)],
        axis=1,
    ).astype(jnp.bfloat16)
    grad_query_bias = jnp.sum(grad_projected[:, :model_width].astype(jnp.float32), axis=0)
    grad_value_bias = jnp.sum(grad_projected[:, 2 * model_width :].astype(jnp.float32), axis=0)
    grad_qkv = contract(normed_one, grad_projected, 0, 0)
    grad_normed_one = contract(grad_projected, back_qkv, 1, 1)
    first_value, first_pull = jax.vjp(layer_norm, start, gain_one, shift_one)
    grad_start_part, grad_gain_one, grad_shift_one = first_pull(grad_normed_one)
    grad_tokens = (grad_middle + grad_start_part).astype(jnp.bfloat16)
    every_grad = (
        lax.psum_scatter(grad_qkv, ("dp", "fsdp"), scatter_dimension=0, tiled=True),
        lax.psum_scatter(grad_out_weight, ("dp", "fsdp"), scatter_dimension=0, tiled=True),
        lax.psum_scatter(grad_up, ("dp", "fsdp"), scatter_dimension=0, tiled=True),
        lax.psum_scatter(grad_down, ("dp", "fsdp"), scatter_dimension=0, tiled=True),
        lax.psum_scatter(grad_gain_one, ("dp", "fsdp"), scatter_dimension=0, tiled=True),
        lax.psum_scatter(grad_shift_one, ("dp", "fsdp"), scatter_dimension=0, tiled=True),
        lax.psum_scatter(grad_query_bias, ("dp", "fsdp"), scatter_dimension=0, tiled=True),
        lax.psum_scatter(grad_value_bias, ("dp", "fsdp"), scatter_dimension=0, tiled=True),
        lax.psum_scatter(grad_out_bias, ("dp", "fsdp"), scatter_dimension=0, tiled=True),
        lax.psum_scatter(grad_gain_two, ("dp", "fsdp"), scatter_dimension=0, tiled=True),
        lax.psum_scatter(grad_shift_two, ("dp", "fsdp"), scatter_dimension=0, tiled=True),
        lax.psum_scatter(grad_up_bias, ("dp", "fsdp"), scatter_dimension=0, tiled=True),
        lax.psum_scatter(grad_down_bias, ("dp", "fsdp"), scatter_dimension=0, tiled=True),
    )
    (
        shard_qkv,
        shard_out,
        shard_up,
        shard_down,
        shard_gain_one,
        shard_shift_one,
        shard_query_bias,
        shard_value_bias,
        shard_out_bias,
        shard_gain_two,
        shard_shift_two,
        shard_up_bias,
        shard_down_bias,
    ) = every_grad
    return (
        output,
        grad_tokens,
        shard_qkv,
        shard_out,
        shard_up,
        shard_down,
        shard_gain_one,
        shard_shift_one,
        shard_query_bias,
        shard_value_bias,
        shard_out_bias,
        shard_gain_two,
        shard_shift_two,
        shard_up_bias,
        shard_down_bias,
    )


PLANE = 2
CORES = 2
UNIT = 1024 * 1024
MESH = pl.DeviceIdType.MESH
ALL = slice(None)


class Place:
    def __init__(self, depth):
        dp, fsdp = lax.axis_index("dp"), lax.axis_index("fsdp")
        self.y, self.x = dp // PLANE, lax.rem(dp, PLANE)
        self.z, self.c = fsdp // CORES, lax.rem(fsdp, CORES)
        self.depth = depth
        y, x, z, c = self.y, self.x, self.z, self.c
        self.along_x = self.device(y, 1 - x, z, c)
        self.along_y = self.device(1 - y, x, z, c)
        self.other_core = self.device(y, x, z, 1 - c)
        self.ahead = [lax.rem(z + k, depth) for k in range(1, depth)]
        self.behind = [lax.rem(z + depth - k, depth) for k in range(1, depth)]

    def device(self, y, x, z, c):
        return (y * PLANE + x, z * CORES + c)

    def column(self, z):
        return self.device(self.y, self.x, z, self.c)

    def greet(self):
        partners = [self.column(q) for q in self.ahead]
        partners += [self.along_x, self.along_y, self.other_core]
        barrier = pltpu.get_barrier_semaphore()
        for partner in partners:
            pl.semaphore_signal(barrier, inc=1, device_id=partner, device_id_type=MESH)
        pl.semaphore_wait(barrier, len(partners))


class Mail:
    def __init__(self, send_sem, recv_sem):
        self.send_sem, self.recv_sem, self.sent = send_sem, recv_sem, []

    def copy(self, unit, slot, source, target, device):
        return pltpu.make_async_remote_copy(
            src_ref=source,
            dst_ref=target,
            send_sem=self.send_sem.at[unit, slot],
            recv_sem=self.recv_sem.at[unit, slot],
            device_id=device,
            device_id_type=MESH,
        )

    def send(self, unit, slot, source, target, device):
        copy = self.copy(unit, slot, source, target, device)
        copy.start()
        self.sent.append(copy)

    def arrived(self, unit, slot, target, device):
        self.copy(unit, slot, target, target, device).wait_recv()

    def finish(self):
        for copy in self.sent:
            copy.wait_send()


SLOTS = 12


def unit_list(shapes):
    units = []
    for index, (rows, columns) in enumerate(shapes):
        width = UNIT // rows
        units += [(index, first, width) for first in range(0, columns, width)]
    return units


def gather_phases(place, mail, unit, source, full, local_sem):
    y, x, z, c = place.y, place.x, place.z, place.c
    nz = place.depth - 1

    def first():
        pltpu.make_async_copy(source, full(y, x, z, c, ALL), local_sem).start()
        for k in range(nz):
            mail.send(unit, k, source, full(y, x, z, c, ALL), place.column(place.ahead[k]))

    def second():
        pltpu.make_async_copy(source, full(y, x, z, c, ALL), local_sem).wait()
        for k in range(nz):
            q = place.behind[k]
            mail.arrived(unit, k, full(y, x, q, c, ALL), place.column(q))
        mail.send(unit, 3, full(y, x, ALL, c, 0), full(y, x, ALL, c, 0), place.along_x)
        mail.send(unit, 4, full(y, x, ALL, c, 1), full(y, x, ALL, c, 1), place.along_y)

    def third():
        mail.arrived(unit, 3, full(y, 1 - x, ALL, c, 0), place.along_x)
        mail.send(unit, 5, full(y, ALL, ALL, c, 0), full(y, ALL, ALL, c, 0), place.along_y)
        mail.arrived(unit, 4, full(1 - y, x, ALL, c, 1), place.along_y)
        mail.send(unit, 6, full(ALL, x, ALL, c, 1), full(ALL, x, ALL, c, 1), place.along_x)

    def fourth():
        mail.arrived(unit, 5, full(1 - y, ALL, ALL, c, 0), place.along_y)
        mail.arrived(unit, 6, full(ALL, 1 - x, ALL, c, 1), place.along_x)
        mail.send(unit, 7, full(ALL, ALL, ALL, c, ALL), full(ALL, ALL, ALL, c, ALL), place.other_core)

    def last():
        mail.arrived(unit, 7, full(ALL, ALL, ALL, 1 - c, ALL), place.other_core)

    return first, second, third, fourth, last


def small_gather_phases(place, mail, unit, source, full, local_sem):
    y, x, z, c = place.y, place.x, place.z, place.c
    nz = place.depth - 1

    def first():
        pltpu.make_async_copy(source, full.at[y, x, z, c], local_sem).start()
        for k in range(nz):
            mail.send(unit, k, source, full.at[y, x, z, c], place.column(place.ahead[k]))

    def second():
        pltpu.make_async_copy(source, full.at[y, x, z, c], local_sem).wait()
        for k in range(nz):
            q = place.behind[k]
            mail.arrived(unit, k, full.at[y, x, q, c], place.column(q))
        mail.send(unit, 3, full.at[y, x, :, c], full.at[y, x, :, c], place.along_x)

    def third():
        mail.arrived(unit, 3, full.at[y, 1 - x, :, c], place.along_x)
        mail.send(unit, 5, full.at[y, :, :, c], full.at[y, :, :, c], place.along_y)

    def fourth():
        mail.arrived(unit, 5, full.at[1 - y, :, :, c], place.along_y)
        mail.send(unit, 7, full.at[:, :, :, c], full.at[:, :, :, c], place.other_core)

    def last():
        mail.arrived(unit, 7, full.at[:, :, :, 1 - c], place.other_core)

    return first, second, third, fourth, last


def scatter_kernel(depth, units, count, *refs):
    parts, small = refs[:count], refs[count]
    outs, small_out = refs[count + 1 : 2 * count + 1], refs[2 * count + 1]
    (core_in, own, wide_in, near_in, column_in, result, small_core, small_own, small_wide, small_near,
     small_column, small_result, send_sem, recv_sem, local_sem) = refs[2 * count + 2 :]
    place, mail = Place(depth), Mail(send_sem, recv_sem)
    y, x, z, c = place.y, place.x, place.z, place.c
    place.greet()
    nz = depth - 1
    steps = []

    def small_steps():
        unit = 0

        def first():
            mail.send(unit, 7, small.at[:, :, :, 1 - c], small_core, place.other_core)
            pltpu.make_async_copy(small.at[:, :, :, c], small_own, local_sem.at[unit]).start()

        def second():
            mail.arrived(unit, 7, small_core, place.other_core)
            pltpu.make_async_copy(small.at[:, :, :, c], small_own, local_sem.at[unit]).wait()
            small_own[...] += small_core[...]
            mail.send(unit, 5, small_own.at[1 - y], small_wide, place.along_y)

        def third():
            mail.arrived(unit, 5, small_wide, place.along_y)
            small_own[y] += small_wide[...]
            mail.send(unit, 3, small_own.at[y, 1 - x], small_near, place.along_x)

        def fourth():
            mail.arrived(unit, 3, small_near, place.along_x)
            small_own[y, x] += small_near[...]
            for k in range(nz):
                q = place.ahead[k]
                mail.send(unit, k, small_own.at[y, x, q], small_column.at[k], place.column(q))

        def last():
            total = small_own[y, x, z]
            for k in range(nz):
                mail.arrived(unit, k, small_column.at[k], place.column(place.behind[k]))
                total = total + small_column[k]
            small_result[...] = total
            pltpu.make_async_copy(small_result, small_out, local_sem.at[unit]).start()

        def ended():
            pltpu.make_async_copy(small_result, small_out, local_sem.at[unit]).wait()

        return first, second, third, fourth, last, ended

    def unit_steps(unit, index, at):
        _, start, width = units[unit - 1]
        span = pl.ds(start, width)
        part = parts[index]
        rows = part.shape[-2]
        shape = (PLANE, PLANE, depth, 2, rows, width)
        other = part.at[:, :, :, 1 - c, :, :, span]
        mine = part.at[:, :, :, c, :, :, span]
        inbox, held = core_in[index].at[at], own[index].at[at]
        wide, near, column = wide_in[index].at[at], near_in[index].at[at], column_in[index].at[at]
        final = result[index].at[at]
        target = outs[index].at[:, :, span]
        local = pltpu.make_async_copy(mine, held, local_sem.at[unit])
        outward = pltpu.make_async_copy(final, target, local_sem.at[unit])

        def first():
            mail.send(unit, 7, other, inbox, place.other_core)
            local.start()

        def second():
            mail.arrived(unit, 7, inbox, place.other_core)
            local.wait()
            for a in range(PLANE):
                for b in range(PLANE):
                    held[a, b] = held[a, b] + inbox[a, b]
            mail.send(unit, 5, held.at[1 - y, :, :, 0], wide.at[0], place.along_y)
            mail.send(unit, 6, held.at[:, 1 - x, :, 1], wide.at[1], place.along_x)

        def third():
            mail.arrived(unit, 5, wide.at[0], place.along_y)
            mail.arrived(unit, 6, wide.at[1], place.along_x)
            for b in range(PLANE):
                held[y, b, :, 0] = held[y, b, :, 0] + wide[0, b]
                held[b, x, :, 1] = held[b, x, :, 1] + wide[1, b]
            mail.send(unit, 3, held.at[y, 1 - x, :, 0], near.at[0], place.along_x)
            mail.send(unit, 4, held.at[1 - y, x, :, 1], near.at[1], place.along_y)

        def fourth():
            mail.arrived(unit, 3, near.at[0], place.along_x)
            mail.arrived(unit, 4, near.at[1], place.along_y)
            for h in range(2):
                held[y, x, :, h] = held[y, x, :, h] + near[h]
            for k in range(nz):
                q = place.ahead[k]
                mail.send(unit, k, held.at[y, x, q], column.at[k], place.column(q))

        def last():
            total = held[y, x, z].astype(jnp.float32)
            for k in range(nz):
                mail.arrived(unit, k, column.at[k], place.column(place.behind[k]))
                total = total + column[k].astype(jnp.float32)
            final[...] = total
            outward.start()

        def ended():
            outward.wait()

        return first, second, third, fourth, last, ended

    seen = [0] * count
    for unit, (index, _, _) in enumerate(units, 1):
        steps.append(unit_steps(unit, index, seen[index]))
        seen[index] += 1
    steps.append(small_steps())
    for turn in range(len(steps) + 5):
        for phase in range(6):
            if 0 <= turn - phase < len(steps):
                steps[turn - phase][phase]()
    mail.finish()


def grid_scatter(mesh):
    depth = mesh.shape["fsdp"] // CORES
    grid = (PLANE, PLANE, depth, CORES)
    devices = mesh.size

    def scatter(matrices, vectors):
        count = len(matrices)
        shapes = [m.shape for m in matrices]
        units = unit_list(shapes)[::-1]
        parts = [
            m.astype(jnp.bfloat16).reshape(grid + (2, m.shape[0] // devices // 2, m.shape[1]))
            for m in matrices
        ]
        wide, narrow = vectors[-1].size // devices, vectors[0].size // devices
        table = jnp.concatenate(
            [vectors[-1].reshape(devices, wide)] + [v.reshape(devices, narrow) for v in vectors[:-1]],
            axis=1,
        )
        table = jnp.pad(table, ((0, 0), (0, 1024 - table.shape[1]))).reshape(grid + (8, 128))
        amounts = [sum(u[0] == index for u in units) for index in range(count)]
        sizes = [(rows // devices // 2, UNIT // rows) for rows, _ in shapes]

        def buffers(*lead, dtype=jnp.bfloat16):
            return [pltpu.VMEM((n, *lead, *size), dtype) for n, size in zip(amounts, sizes)]

        def small(*lead):
            return pltpu.VMEM((*lead, 8, 128), jnp.float32)

        total = len(units) + 1
        outs = pl.pallas_call(
            functools.partial(scatter_kernel, depth, units, count),
            out_shape=[
                jax.ShapeDtypeStruct((2, rows // devices // 2, columns), jnp.float32)
                for rows, columns in shapes
            ]
            + [jax.ShapeDtypeStruct((8, 128), jnp.float32)],
            in_specs=[pl.BlockSpec(memory_space=pl.ANY)] * (count + 1),
            out_specs=[pl.BlockSpec(memory_space=pl.ANY)] * (count + 1),
            scratch_shapes=[
                buffers(PLANE, PLANE, depth, 2),
                buffers(PLANE, PLANE, depth, 2),
                buffers(2, PLANE, depth),
                buffers(2, depth),
                buffers(depth - 1, 2),
                buffers(2, dtype=jnp.float32),
                small(PLANE, PLANE, depth),
                small(PLANE, PLANE, depth),
                small(PLANE, depth),
                small(depth),
                small(depth - 1),
                small(),
                pltpu.SemaphoreType.DMA((total, SLOTS)),
                pltpu.SemaphoreType.DMA((total, SLOTS)),
                pltpu.SemaphoreType.DMA((total,)),
            ],
            compiler_params=pltpu.CompilerParams(
                collective_id=1, has_side_effects=True, vmem_limit_bytes=56 << 20
            ),
        )(*parts, table)
        spread = outs[count].reshape(-1)
        return (
            *(o.reshape(-1, o.shape[-1]) for o in outs[:count]),
            *(spread[wide + narrow * k : wide + narrow * (k + 1)] for k in range(len(vectors) - 1)),
            spread[:wide],
        )

    return scatter


def by_rows(left, right):
    return contract(left, right, 1, 1)


def by_columns(left, right):
    return contract(left, right, 0, 0)


def plain(left, right):
    return jnp.dot(left, right, preferred_element_type=jnp.float32)


class Table:
    GAIN_ONE, SHIFT_ONE, QUERY, VALUE, OUT, GAIN_TWO, SHIFT_TWO, DOWN = range(8)

    def __init__(self, packed, narrow, wide):
        self.packed, self.narrow, self.wide = packed, narrow, wide

    def expand(self, devices):
        y_count, x_count, z_count, c_count = self.packed.shape[:4]

        def tile(d):
            d, c = divmod(d, c_count)
            d, z = divmod(d, z_count)
            y, x = divmod(d, x_count)
            return self.packed[y, x, z, c]

        group = lax.broadcasted_iota(jnp.int32, (8, 128), 1) // 32
        for base in range(0, devices, 4):
            tiles = [tile(base + i) for i in range(4)]
            for i in range(4):
                self.wide[:, pl.ds(128 * (base + i), 128)] = tiles[i][0:1, :]
            for q in range(4):
                mixed = jnp.zeros((8, 128), jnp.float32)
                for i in range(4):
                    turned = tiles[i] if i == q else pltpu.roll(tiles[i], 32 * ((i - q) % 4), 1)
                    mixed = jnp.where(group == i, turned, mixed)
                self.narrow[q, :, pl.ds(32 * base, 128)] = mixed

    def __getitem__(self, index):
        return self.narrow[index % 4, 1 + index // 4 : 2 + index // 4, :]


def row_facts(lengths, codes, row):
    begin = jnp.int32(0)
    segment = jnp.zeros(row.shape, jnp.int32)
    first = jnp.zeros(row.shape, jnp.int32)
    code = jnp.full(row.shape, codes[0, 0], jnp.int32)
    for item in range(1, lengths.shape[1]):
        begin = begin + lengths[0, item - 1]
        inside = row >= begin
        segment = jnp.where(inside, item, segment)
        first = jnp.where(inside, begin, first)
        code = jnp.where(inside, codes[0, item], code)
    return segment, (row - first).astype(jnp.float32) * (0.5 * (code.astype(jnp.float32) + 1.0))


def fill_mask(lengths, codes, mask):
    rows = mask.shape[0]
    across, _ = row_facts(lengths, codes, lax.broadcasted_iota(jnp.int32, (1, rows), 1))
    for base in range(0, rows, 128):
        down, _ = row_facts(lengths, codes, lax.broadcasted_iota(jnp.int32, (128, 1), 0) + base)
        mask[base : base + 128, :] = jnp.where(down == across, 0.0, -1e30)


def head_half(rows, which):
    lane = lax.broadcasted_iota(jnp.int32, (rows, 2 * HEAD_DIM), 1)
    return (lane >= HEAD_DIM) if which else (lane < HEAD_DIM)


def pair_span(pair, offset):
    return pl.ds(pl.multiple_of(offset + pair * 2 * HEAD_DIM, 2 * HEAD_DIM), 2 * HEAD_DIM)


def attend(first_pair, last_pair, projected, mask, attended):
    rows, width = attended.shape
    zero = jnp.zeros((), jnp.bfloat16)
    scale = jnp.asarray(1.0 / math.sqrt(HEAD_DIM), jnp.bfloat16)

    def one_pair(pair, carry):
        query = projected[:, pair_span(pair, 0)] * scale
        key = projected[:, pair_span(pair, width)]
        value = projected[:, pair_span(pair, 2 * width)]
        results = []
        for which in range(2):
            scores = by_rows(jnp.where(head_half(rows, which), query, zero), key) + mask[...]
            top = jnp.max(scores, axis=1, keepdims=True)
            expon = jnp.exp(scores - top)
            total = jnp.sum(expon, axis=1, keepdims=True)
            weights = (expon * (1.0 / total)).astype(jnp.bfloat16)
            results.append(plain(weights, value))
        mixed = jnp.where(head_half(rows, 0), results[0], results[1])
        attended[:, pair_span(pair, 0)] = mixed.astype(jnp.bfloat16)
        return carry

    lax.fori_loop(first_pair, last_pair, one_pair, 0)


CHUNK = 64


def over_rows(rows, step):
    def one(index, carry):
        step(pl.ds(pl.multiple_of(index * CHUNK, CHUNK), CHUNK), index * CHUNK)
        return carry

    lax.fori_loop(0, rows // CHUNK, one, 0)


def normalised(values):
    centred = values - jnp.mean(values, axis=-1, keepdims=True)
    variance = jnp.mean(centred * centred, axis=-1, keepdims=True)
    scale = lax.rsqrt(variance + EPSILON)
    return centred * scale, scale


def forward_kernel(depth, units, *refs):
    (s_qkv, s_out, s_up, s_down, small, tokens, lengths, codes) = refs[:8]
    (f_qkv, f_out, f_up, f_down, o_narrow, o_projected, o_attended, o_start, o_middle, o_activated, o_slope, o_output) = refs[8:20]
    (packed, narrow, wide, start, normed, projected, attended, middle, activated, slope, output, mask, square, tall,
     send_sem, recv_sem, local_sem, load_sem, store_sem) = refs[20:]
    place, mail = Place(depth), Mail(send_sem, recv_sem)
    rows, width = start.shape
    table = Table(packed, narrow, wide)
    place.greet()
    sources, fulls = (s_qkv, s_out, s_up, s_down), (f_qkv, f_out, f_up, f_down)

    steps, loads = [], []
    small_step = small_gather_phases(place, mail, 0, small, packed, local_sem.at[0])
    seen = [0, 0]
    for unit, (index, first, columns) in enumerate(units, 1):
        span = pl.ds(first, columns)

        def view(*at, ref=fulls[index], span=span):
            return ref.at[at + (ALL, span)]

        steps.append(
            gather_phases(
                place, mail, unit, sources[index].at[:, :, span], view, local_sem.at[unit]
            )
        )
        kind = 1 if index == 3 else 0
        buffer = (square, tall)[kind]
        loads.append(
            (
                pltpu.make_async_copy(
                    fulls[index].at[:, :, :, :, :, :, span],
                    buffer.at[seen[kind] % 2],
                    load_sem.at[unit],
                ),
                buffer,
                seen[kind] % 2,
            )
        )
        seen[kind] += 1
    stores = []

    def store(source, target):
        copy = pltpu.make_async_copy(source, target, store_sem.at[len(stores)])
        copy.start()
        stores.append(copy)

    def weights(unit, columns):
        _, buffer, at = loads[unit]
        block = buffer[at, :, :, :, :, :, :, columns]
        return block.reshape(-1, block.shape[-1])

    def prepare():
        def chunk(span, base):
            row = lax.broadcasted_iota(jnp.int32, (CHUNK, 1), 0) + base
            _, factor = row_facts(lengths, codes, row)
            lane = lax.broadcasted_iota(jnp.int32, (1, width // 2), 1).astype(jnp.float32)
            phase = factor * jnp.exp(lane * (-math.log(10000.0) / (width // 2)))
            low, high = pl.ds(0, width // 2), pl.ds(width // 2, width // 2)
            start[span, low] = tokens[span, low].astype(jnp.float32) + jnp.sin(phase)
            start[span, high] = tokens[span, high].astype(jnp.float32) + jnp.cos(phase)

        over_rows(rows, chunk)
        store(start, o_start)
        fill_mask(lengths, codes, mask)

    def norm(values, gain, shift):
        def chunk(span, base):
            normed[span, :] = (normalised(values[span, :])[0] * table[gain] + table[shift]).astype(jnp.bfloat16)

        over_rows(rows, chunk)

    def norm_one():
        table.expand(PLANE * PLANE * depth * CORES)
        store(narrow, o_narrow)
        norm(start, Table.GAIN_ONE, Table.SHIFT_ONE)

    def project(unit, bias):
        tile = 512
        for first in range(0, width, tile):
            value = plain(normed[...], weights(unit, pl.ds(first, tile)))
            if bias is not None:
                value = value + table[bias][:, first : first + tile]
            projected[:, pl.ds(unit * width + first, tile)] = value.astype(jnp.bfloat16)

    def project_out(unit):
        tile = 512
        for first in range(0, width, tile):
            span = pl.ds(first, tile)
            value = plain(attended[...], weights(unit, span)) + table[Table.OUT][:, first : first + tile]
            middle[:, span] = start[:, span] + value
        store(middle, o_middle)
        norm(middle, Table.GAIN_TWO, Table.SHIFT_TWO)

    def rise(unit, number):
        tile = 256

        def one(index, carry):
            at = pl.multiple_of(index * tile, tile)
            there = pl.ds(pl.multiple_of(number * width + at, tile), tile)
            pre = plain(normed[...], weights(unit, pl.ds(at, tile))) + wide[:, there]
            normal = 0.5 * (1.0 + lax.erf(pre * math.sqrt(0.5)))
            density = jnp.exp(pre * pre * -0.5) * (1.0 / math.sqrt(2.0 * math.pi))
            activated[:, there] = (pre * normal).astype(jnp.bfloat16)
            slope[:, there] = (normal + pre * density).astype(jnp.bfloat16)
            return carry

        lax.fori_loop(0, width // tile, one, 0)
        there = pl.ds(number * width, width)
        store(activated.at[:, there], o_activated.at[:, there])
        store(slope.at[:, there], o_slope.at[:, there])

    def fall(unit, number, columns):
        span = pl.ds(number * columns, columns)
        value = plain(activated[...], weights(unit, ALL)) + table[Table.DOWN][:, number * columns : (number + 1) * columns]
        output[:, span] = (middle[:, span] + value).astype(jnp.bfloat16)
        store(output.at[:, span], o_output.at[:, span])

    pairs = width // (2 * HEAD_DIM)
    total = len(units)
    for turn in range(total + 4):
        for phase in range(5):
            unit = turn - phase
            if unit == 0:
                small_step[phase]()
            if 0 <= unit < total:
                steps[unit][phase]()
                if phase == 4:
                    loads[unit][0].start()
        if turn == 0:
            prepare()
        unit = turn - 4
        if unit < 0:
            continue
        index, first, columns = units[unit]
        if unit == 0:
            norm_one()
        if unit == 3:
            attend(pairs // 2, pairs, projected, mask, attended)
            store(attended, o_attended)
        loads[unit][0].wait()
        if index == 0:
            project(unit, (Table.QUERY, None, Table.VALUE)[unit])
            if unit == 2:
                store(projected, o_projected)
                attend(0, pairs // 2, projected, mask, attended)
        elif index == 1:
            project_out(unit)
        elif index == 2:
            rise(unit, first // columns)
        else:
            fall(unit, first // columns, columns)
    for copy in stores:
        copy.wait()
    mail.finish()


def run_forward(mesh, tokens, lengths, codes, matrices, vectors):
    depth = mesh.shape["fsdp"] // CORES
    grid = (PLANE, PLANE, depth, CORES)
    rows, width = tokens.shape
    hidden = matrices[2].shape[1]
    halves = [m.reshape(2, m.shape[0] // 2, m.shape[1]) for m in matrices]
    units = unit_list([(m.shape[0] * mesh.size, m.shape[1]) for m in matrices])
    flat = jnp.concatenate([vectors[-1], *vectors[:-1]]).astype(jnp.float32)
    small = jnp.pad(flat, (0, 1024 - flat.size)).reshape(8, 128)
    low, full = jnp.bfloat16, jnp.float32

    def shaped(*shape, dtype=low):
        return jax.ShapeDtypeStruct(shape, dtype)

    anywhere = pl.BlockSpec(memory_space=pl.ANY)
    vmem = pl.BlockSpec(memory_space=pltpu.VMEM)
    smem = pl.BlockSpec(memory_space=pltpu.SMEM)
    count = len(units) + 1
    square = UNIT // width
    tall = UNIT // hidden
    return pl.pallas_call(
        functools.partial(forward_kernel, depth, units),
        out_shape=[shaped(*grid, *h.shape) for h in halves]
        + [
            shaped(4, 8, width, dtype=full),
            shaped(rows, 3 * width),
            shaped(rows, width),
            shaped(rows, width, dtype=full),
            shaped(rows, width, dtype=full),
            shaped(rows, hidden),
            shaped(rows, hidden),
            shaped(rows, width),
        ],
        in_specs=[anywhere] * 5 + [vmem, smem, smem],
        out_specs=[anywhere] * 12,
        scratch_shapes=[
            pltpu.VMEM((*grid, 8, 128), full),
            pltpu.VMEM((4, 8, width), full),
            pltpu.VMEM((1, hidden), full),
            pltpu.VMEM((rows, width), full),
            pltpu.VMEM((rows, width), low),
            pltpu.VMEM((rows, 3 * width), low),
            pltpu.VMEM((rows, width), low),
            pltpu.VMEM((rows, width), full),
            pltpu.VMEM((rows, hidden), low),
            pltpu.VMEM((rows, hidden), low),
            pltpu.VMEM((rows, width), low),
            pltpu.VMEM((rows, rows), full),
            pltpu.VMEM((2, *grid, 2, width // mesh.size // 2, square), low),
            pltpu.VMEM((2, *grid, 2, hidden // mesh.size // 2, tall), low),
            pltpu.SemaphoreType.DMA((count, SLOTS)),
            pltpu.SemaphoreType.DMA((count, SLOTS)),
            pltpu.SemaphoreType.DMA((count,)),
            pltpu.SemaphoreType.DMA((count,)),
            pltpu.SemaphoreType.DMA((24,)),
        ],
        compiler_params=pltpu.CompilerParams(
            collective_id=0, has_side_effects=True, vmem_limit_bytes=58 << 20
        ),
    )(*halves, small, tokens, lengths, codes)


def attend_back_kernel(projected, mask, grad_attended, grad_projected, weights_low, grad_low):
    rows, width = grad_attended.shape
    zero = jnp.zeros((), jnp.bfloat16)
    scale = 1.0 / math.sqrt(HEAD_DIM)

    def one_pair(pair, carry):
        query, key, value = (projected[:, pair_span(pair, k * width)] for k in range(3))
        grad = grad_attended[:, pair_span(pair, 0)]
        scaled = query * jnp.asarray(scale, jnp.bfloat16)
        g_query, g_key, g_value = [], [], []
        for which in range(2):
            keep = head_half(rows, which)
            scores = by_rows(jnp.where(keep, key, zero), scaled) + mask[...]
            expon = jnp.exp(scores - jnp.max(scores, axis=0, keepdims=True))
            weights = expon * (1.0 / jnp.sum(expon, axis=0, keepdims=True))
            weights_low[which] = weights.astype(jnp.bfloat16)
            slopes = by_rows(jnp.where(keep, value, zero), grad)
            level = jnp.sum(weights * slopes, axis=0, keepdims=True)
            grad_low[which] = (weights * (slopes - level)).astype(jnp.bfloat16)
            g_value.append(plain(weights_low[which], grad))
            g_key.append(plain(grad_low[which], query))
            g_query.append(by_columns(grad_low[which], key))
        keep = head_half(rows, 0)
        for k, (parts, factor) in enumerate(((g_query, scale), (g_key, scale), (g_value, 1.0))):
            mixed = jnp.where(keep, parts[0], parts[1]) * factor
            grad_projected[:, pair_span(pair, k * width)] = mixed.astype(jnp.bfloat16)
        return carry

    lax.fori_loop(0, width // (2 * HEAD_DIM), one_pair, 0)


def attend_back(projected, mask, grad_attended):
    rows = projected.shape[0]
    return pl.pallas_call(
        attend_back_kernel,
        out_shape=jax.ShapeDtypeStruct(projected.shape, jnp.bfloat16),
        scratch_shapes=[pltpu.VMEM((2, rows, rows), jnp.bfloat16)] * 2,
        compiler_params=pltpu.CompilerParams(vmem_limit_bytes=56 << 20),
    )(projected, mask, grad_attended)


def grid_body(mesh, scatter, tokens, cotangent, lengths, scale_codes, *params):
    matrices = params[:4]
    (gain_one, shift_one, bias_query, bias_value, bias_out, gain_two, shift_two, bias_up, bias_down) = params[4:]
    vectors = (gain_one, shift_one, bias_query, bias_value, bias_out, gain_two, shift_two, bias_down, bias_up)
    (f_qkv, f_out, f_up, f_down, narrow, projected, attended, start, middle, activated, slope, output) = run_forward(
        mesh, tokens, lengths, scale_codes, matrices, vectors
    )
    back_qkv, back_out, back_up, back_down = (f.reshape(-1, f.shape[-1]) for f in (f_qkv, f_out, f_up, f_down))
    g1, s1 = narrow[Table.GAIN_ONE % 4, 1], narrow[Table.SHIFT_ONE % 4, 1]
    g2, s2 = narrow[Table.GAIN_TWO % 4, 2], narrow[Table.SHIFT_TWO % 4, 2]
    normed_one, first_pull = jax.vjp(layer_norm, start, g1, s1)
    normed_two, second_pull = jax.vjp(layer_norm, middle, g2, s2)
    normed_one, normed_two = normed_one.astype(jnp.bfloat16), normed_two.astype(jnp.bfloat16)
    segment, _ = row_tables(lengths[0], scale_codes[0], tokens.shape[0], 2)
    mask = jnp.where(segment[:, None] == segment[None, :], 0.0, -1e30)
    width = tokens.shape[1]
    grad_output = cotangent.astype(jnp.float32)
    grad_down_bias = jnp.sum(grad_output, axis=0)
    grad_down = contract(activated, cotangent, 0, 0)
    grad_act = contract(cotangent, back_down, 1, 1)
    grad_hidden = (grad_act * slope.astype(jnp.float32)).astype(jnp.bfloat16)
    grad_up_bias = jnp.sum(grad_hidden.astype(jnp.float32), axis=0)
    grad_up = contract(normed_two, grad_hidden, 0, 0)
    grad_normed_two = contract(grad_hidden, back_up, 1, 1)
    grad_middle_part, grad_gain_two, grad_shift_two = second_pull(grad_normed_two)
    grad_middle = grad_output + grad_middle_part
    branch_grad = grad_middle.astype(jnp.bfloat16)
    grad_out_bias = jnp.sum(branch_grad.astype(jnp.float32), axis=0)
    grad_out_weight = contract(attended, branch_grad, 0, 0)
    grad_attended = contract(branch_grad, back_out, 1, 1).astype(jnp.bfloat16)
    grad_projected = attend_back(projected, mask, grad_attended)
    grad_query_bias = jnp.sum(grad_projected[:, :width].astype(jnp.float32), axis=0)
    grad_value_bias = jnp.sum(grad_projected[:, 2 * width :].astype(jnp.float32), axis=0)
    grad_qkv = contract(normed_one, grad_projected, 0, 0)
    grad_normed_one = contract(grad_projected, back_qkv, 1, 1)
    grad_start_part, grad_gain_one, grad_shift_one = first_pull(grad_normed_one)
    grad_tokens = (grad_middle + grad_start_part).astype(jnp.bfloat16)
    every = scatter(
        (grad_qkv, grad_out_weight, grad_up, grad_down),
        (
            grad_gain_one,
            grad_shift_one,
            grad_query_bias,
            grad_value_bias,
            grad_out_bias,
            grad_gain_two,
            grad_shift_two,
            grad_down_bias,
            grad_up_bias,
        ),
    )
    return (output, grad_tokens, *every[:-2], every[-1], every[-2])


def solution(mesh):
    placed = (
        P(("dp", "fsdp"), None),
        P(("dp", "fsdp"), None),
        P(("dp", "fsdp"), None),
        P(("dp", "fsdp"), None),
        P(("dp", "fsdp"), None),
        P(("dp", "fsdp"), None),
        P(("dp", "fsdp"), None),
        P(("dp", "fsdp"), None),
        P(("dp", "fsdp")),
        P(("dp", "fsdp")),
        P(("dp", "fsdp")),
        P(("dp", "fsdp")),
        P(("dp", "fsdp")),
        P(("dp", "fsdp")),
        P(("dp", "fsdp")),
        P(("dp", "fsdp")),
        P(("dp", "fsdp")),
    )
    per_device = body
    if mesh.shape["dp"] == PLANE * PLANE and mesh.shape["fsdp"] == 4 * CORES:
        per_device = functools.partial(grid_body, mesh, grid_scatter(mesh))
    return jax.shard_map(
        per_device,
        mesh=mesh,
        in_specs=placed,
        out_specs=(
            P(("dp", "fsdp"), None),
            P(("dp", "fsdp"), None),
            P(("dp", "fsdp"), None),
            P(("dp", "fsdp"), None),
            P(("dp", "fsdp"), None),
            P(("dp", "fsdp"), None),
            P(("dp", "fsdp")),
            P(("dp", "fsdp")),
            P(("dp", "fsdp")),
            P(("dp", "fsdp")),
            P(("dp", "fsdp")),
            P(("dp", "fsdp")),
            P(("dp", "fsdp")),
            P(("dp", "fsdp")),
            P(("dp", "fsdp")),
        ),
        check_vma=False,
    )
```

```python
import functools
import math

import jax
import jax.numpy as jnp
from jax import lax
from jax.experimental import pallas as pl
from jax.experimental.pallas import tpu as pltpu
from jax.sharding import PartitionSpec as P

HEADS = 16
HEAD_DIM = 64


EPSILON = 1e-06


def contract(left, right, left_dim, right_dim):
    return lax.dot_general(
        left, right, (((left_dim,), (right_dim,)), ((), ())), preferred_element_type=jnp.float32
    )


def layer_norm(values, gain, shift):
    centred = values - jnp.mean(values, axis=-1, keepdims=True)
    variance = jnp.mean(centred * centred, axis=-1, keepdims=True)
    return centred * lax.rsqrt(variance + EPSILON) * gain + shift


def gelu_exact(values):
    return jax.nn.gelu(values, approximate=False)


def row_tables(length_row, code_row, row_count, feat_width):
    items = jnp.arange(length_row.shape[0], dtype=jnp.int32)
    item_starts = jnp.sum(
        jnp.where(items[None, :] < items[:, None], length_row[None, :], 0), axis=1
    )
    item_ends = item_starts + length_row
    row_index = jnp.arange(row_count, dtype=jnp.int32)
    member = (
        (row_index[:, None] >= item_starts[None, :]) & (row_index[:, None] < item_ends[None, :])
    ).astype(jnp.int32)
    item_ids = jnp.arange(length_row.shape[0], dtype=jnp.int32)
    segment = jnp.sum(member * item_ids[None, :], axis=1)
    place = row_index - jnp.sum(member * item_starts[None, :], axis=1)
    row_code = jnp.sum(member * code_row[None, :], axis=1)
    half_width = feat_width // 2
    frequency = jnp.exp(
        jnp.arange(half_width, dtype=jnp.float32) * (-math.log(10000.0) / half_width)
    )
    gsd_ratio = 0.5 * (row_code.astype(jnp.float32) + 1.0)
    phase_angle = (place.astype(jnp.float32) * gsd_ratio)[:, None] * frequency[None, :]
    return (segment, jnp.concatenate([jnp.sin(phase_angle), jnp.cos(phase_angle)], axis=1))


def body(
    tokens,
    cotangent,
    lengths,
    scale_codes,
    w_qkv,
    w_out,
    w_up,
    w_down,
    ln1_gain,
    ln1_shift,
    bias_query,
    bias_value,
    bias_out,
    ln2_gain,
    ln2_shift,
    bias_up,
    bias_down,
):
    gathered = (
        lax.all_gather(w_qkv, ("dp", "fsdp"), axis=0, tiled=True),
        lax.all_gather(w_out, ("dp", "fsdp"), axis=0, tiled=True),
        lax.all_gather(w_up, ("dp", "fsdp"), axis=0, tiled=True),
        lax.all_gather(w_down, ("dp", "fsdp"), axis=0, tiled=True),
        lax.all_gather(ln1_gain, ("dp", "fsdp"), axis=0, tiled=True),
        lax.all_gather(ln1_shift, ("dp", "fsdp"), axis=0, tiled=True),
        lax.all_gather(bias_query, ("dp", "fsdp"), axis=0, tiled=True),
        lax.all_gather(bias_value, ("dp", "fsdp"), axis=0, tiled=True),
        lax.all_gather(bias_out, ("dp", "fsdp"), axis=0, tiled=True),
        lax.all_gather(ln2_gain, ("dp", "fsdp"), axis=0, tiled=True),
        lax.all_gather(ln2_shift, ("dp", "fsdp"), axis=0, tiled=True),
        lax.all_gather(bias_up, ("dp", "fsdp"), axis=0, tiled=True),
        lax.all_gather(bias_down, ("dp", "fsdp"), axis=0, tiled=True),
    )
    (
        full_qkv,
        full_out,
        full_up,
        full_down,
        gain_first,
        shift_first,
        query_bias,
        value_bias,
        out_bias,
        gain_second,
        shift_second,
        up_bias,
        down_bias,
    ) = gathered
    gain_one = gain_first.astype(jnp.float32)
    shift_one = shift_first.astype(jnp.float32)
    gain_two = gain_second.astype(jnp.float32)
    shift_two = shift_second.astype(jnp.float32)
    row_count, model_width = tokens.shape
    head_width = model_width // HEADS
    score_scale = 1.0 / math.sqrt(HEAD_DIM)
    segment, encoding = row_tables(lengths[0], scale_codes[0], row_count, model_width)
    same_item = segment[:, None] == segment[None, :]
    start = tokens.astype(jnp.float32) + encoding
    normed_one = layer_norm(start, gain_one, shift_one).astype(jnp.bfloat16)
    qkv_bias = jnp.concatenate([query_bias, jnp.zeros_like(query_bias), value_bias]).astype(
        jnp.float32
    )
    projected = (
        jnp.dot(normed_one, full_qkv, preferred_element_type=jnp.float32) + qkv_bias
    ).astype(jnp.bfloat16)

    def split_heads(block):
        return block.reshape(row_count, HEADS, head_width).transpose(1, 0, 2)

    def join_heads(block):
        return block.transpose(1, 0, 2).reshape(row_count, model_width)

    query_heads = split_heads(projected[:, :model_width])
    key_heads = split_heads(projected[:, model_width : 2 * model_width])
    value_heads = split_heads(projected[:, 2 * model_width :])

    def forward_head(operands):
        query_head, key_head, value_head = operands
        scores = contract(query_head, key_head, 1, 1) * score_scale
        scores = jnp.where(same_item, scores, -1e30)
        top_score = jnp.max(scores, axis=1, keepdims=True)
        expon = jnp.exp(scores - top_score)
        total = jnp.sum(expon, axis=1, keepdims=True)
        weights_low = (expon / total).astype(jnp.bfloat16)
        result = jnp.dot(weights_low, value_head, preferred_element_type=jnp.float32)
        return (result, (top_score + jnp.log(total))[:, 0])

    attended_heads, log_totals = lax.map(forward_head, (query_heads, key_heads, value_heads))
    attended = join_heads(attended_heads).astype(jnp.bfloat16)
    middle = (
        start
        + jnp.dot(attended, full_out, preferred_element_type=jnp.float32)
        + out_bias.astype(jnp.float32)
    )
    normed_two = layer_norm(middle, gain_two, shift_two).astype(jnp.bfloat16)
    hidden_pre = jnp.dot(normed_two, full_up, preferred_element_type=jnp.float32) + up_bias.astype(
        jnp.float32
    )
    activated = gelu_exact(hidden_pre).astype(jnp.bfloat16)
    feed_out = jnp.dot(activated, full_down, preferred_element_type=jnp.float32) + down_bias.astype(
        jnp.float32
    )
    output = (middle + feed_out).astype(jnp.bfloat16)
    back_qkv, back_out, back_up, back_down = (
        lax.all_gather(w_qkv, ("dp", "fsdp"), axis=0, tiled=True),
        lax.all_gather(w_out, ("dp", "fsdp"), axis=0, tiled=True),
        lax.all_gather(w_up, ("dp", "fsdp"), axis=0, tiled=True),
        lax.all_gather(w_down, ("dp", "fsdp"), axis=0, tiled=True),
    )
    grad_output = cotangent.astype(jnp.float32)
    grad_down_bias = jnp.sum(grad_output, axis=0)
    grad_down = contract(activated, cotangent, 0, 0)
    grad_act = contract(cotangent, back_down, 1, 1)
    gelu_value, gelu_pull = jax.vjp(gelu_exact, hidden_pre)
    grad_hidden = gelu_pull(grad_act)[0].astype(jnp.bfloat16)
    grad_up_bias = jnp.sum(grad_hidden.astype(jnp.float32), axis=0)
    grad_up = contract(normed_two, grad_hidden, 0, 0)
    grad_normed_two = contract(grad_hidden, back_up, 1, 1)
    norm_value, second_pull = jax.vjp(layer_norm, middle, gain_two, shift_two)
    grad_middle_part, grad_gain_two, grad_shift_two = second_pull(grad_normed_two)
    grad_middle = grad_output + grad_middle_part
    branch_grad = grad_middle.astype(jnp.bfloat16)
    grad_out_bias = jnp.sum(branch_grad.astype(jnp.float32), axis=0)
    grad_out_weight = contract(attended, branch_grad, 0, 0)
    grad_attended = contract(branch_grad, back_out, 1, 1).astype(jnp.bfloat16)
    grad_heads = split_heads(grad_attended)

    def backward_head(operands):
        query_head, key_head, value_head, grad_head, log_total = operands
        scores = contract(query_head, key_head, 1, 1) * score_scale
        weights = jnp.where(same_item, jnp.exp(scores - log_total[:, None]), 0.0)
        weights_low = weights.astype(jnp.bfloat16)
        grad_weights = contract(grad_head, value_head, 1, 1)
        grad_value = contract(weights_low, grad_head, 0, 0)
        grad_scores = weights * (
            grad_weights - jnp.sum(weights * grad_weights, axis=1, keepdims=True)
        )
        grad_scores_low = grad_scores.astype(jnp.bfloat16)
        grad_query = (
            jnp.dot(grad_scores_low, key_head, preferred_element_type=jnp.float32) * score_scale
        )
        grad_key = contract(grad_scores_low, query_head, 0, 0) * score_scale
        return (grad_query, grad_key, grad_value)

    grad_query_heads, grad_key_heads, grad_value_heads = lax.map(
        backward_head, (query_heads, key_heads, value_heads, grad_heads, log_totals)
    )
    grad_projected = jnp.concatenate(
        [join_heads(grad_query_heads), join_heads(grad_key_heads), join_heads(grad_value_heads)],
        axis=1,
    ).astype(jnp.bfloat16)
    grad_query_bias = jnp.sum(grad_projected[:, :model_width].astype(jnp.float32), axis=0)
    grad_value_bias = jnp.sum(grad_projected[:, 2 * model_width :].astype(jnp.float32), axis=0)
    grad_qkv = contract(normed_one, grad_projected, 0, 0)
    grad_normed_one = contract(grad_projected, back_qkv, 1, 1)
    first_value, first_pull = jax.vjp(layer_norm, start, gain_one, shift_one)
    grad_start_part, grad_gain_one, grad_shift_one = first_pull(grad_normed_one)
    grad_tokens = (grad_middle + grad_start_part).astype(jnp.bfloat16)
    every_grad = (
        lax.psum_scatter(grad_qkv, ("dp", "fsdp"), scatter_dimension=0, tiled=True),
        lax.psum_scatter(grad_out_weight, ("dp", "fsdp"), scatter_dimension=0, tiled=True),
        lax.psum_scatter(grad_up, ("dp", "fsdp"), scatter_dimension=0, tiled=True),
        lax.psum_scatter(grad_down, ("dp", "fsdp"), scatter_dimension=0, tiled=True),
        lax.psum_scatter(grad_gain_one, ("dp", "fsdp"), scatter_dimension=0, tiled=True),
        lax.psum_scatter(grad_shift_one, ("dp", "fsdp"), scatter_dimension=0, tiled=True),
        lax.psum_scatter(grad_query_bias, ("dp", "fsdp"), scatter_dimension=0, tiled=True),
        lax.psum_scatter(grad_value_bias, ("dp", "fsdp"), scatter_dimension=0, tiled=True),
        lax.psum_scatter(grad_out_bias, ("dp", "fsdp"), scatter_dimension=0, tiled=True),
        lax.psum_scatter(grad_gain_two, ("dp", "fsdp"), scatter_dimension=0, tiled=True),
        lax.psum_scatter(grad_shift_two, ("dp", "fsdp"), scatter_dimension=0, tiled=True),
        lax.psum_scatter(grad_up_bias, ("dp", "fsdp"), scatter_dimension=0, tiled=True),
        lax.psum_scatter(grad_down_bias, ("dp", "fsdp"), scatter_dimension=0, tiled=True),
    )
    (
        shard_qkv,
        shard_out,
        shard_up,
        shard_down,
        shard_gain_one,
        shard_shift_one,
        shard_query_bias,
        shard_value_bias,
        shard_out_bias,
        shard_gain_two,
        shard_shift_two,
        shard_up_bias,
        shard_down_bias,
    ) = every_grad
    return (
        output,
        grad_tokens,
        shard_qkv,
        shard_out,
        shard_up,
        shard_down,
        shard_gain_one,
        shard_shift_one,
        shard_query_bias,
        shard_value_bias,
        shard_out_bias,
        shard_gain_two,
        shard_shift_two,
        shard_up_bias,
        shard_down_bias,
    )


PLANE = 2
CORES = 2
UNIT = 1024 * 1024
MESH = pl.DeviceIdType.MESH
ALL = slice(None)


class Place:
    def __init__(self, depth):
        dp, fsdp = lax.axis_index("dp"), lax.axis_index("fsdp")
        self.y, self.x = dp // PLANE, lax.rem(dp, PLANE)
        self.z, self.c = fsdp // CORES, lax.rem(fsdp, CORES)
        self.depth = depth
        y, x, z, c = self.y, self.x, self.z, self.c
        self.along_x = self.device(y, 1 - x, z, c)
        self.along_y = self.device(1 - y, x, z, c)
        self.other_core = self.device(y, x, z, 1 - c)
        self.ahead = [lax.rem(z + k, depth) for k in range(1, depth)]
        self.behind = [lax.rem(z + depth - k, depth) for k in range(1, depth)]

    def device(self, y, x, z, c):
        return (y * PLANE + x, z * CORES + c)

    def column(self, z):
        return self.device(self.y, self.x, z, self.c)

    def greet(self):
        partners = [self.column(q) for q in self.ahead]
        partners += [self.along_x, self.along_y, self.other_core]
        barrier = pltpu.get_barrier_semaphore()
        for partner in partners:
            pl.semaphore_signal(barrier, inc=1, device_id=partner, device_id_type=MESH)
        pl.semaphore_wait(barrier, len(partners))


class Mail:
    def __init__(self, send_sem, recv_sem):
        self.send_sem, self.recv_sem, self.sent = send_sem, recv_sem, {}

    def copy(self, unit, slot, source, target, device):
        return pltpu.make_async_remote_copy(
            src_ref=source,
            dst_ref=target,
            send_sem=self.send_sem.at[unit, slot],
            recv_sem=self.recv_sem.at[unit, slot],
            device_id=device,
            device_id_type=MESH,
        )

    def send(self, unit, slot, source, target, device):
        copy = self.copy(unit, slot, source, target, device)
        copy.start()
        self.sent[unit, slot] = copy

    def arrived(self, unit, slot, target, device):
        self.copy(unit, slot, target, target, device).wait_recv()

    def settle(self, unit, slot):
        self.sent.pop((unit, slot)).wait_send()

    def finish(self):
        for at in list(self.sent):
            self.settle(*at)


SLOTS = 12


def unit_list(shapes):
    units = []
    for index, (rows, columns) in enumerate(shapes):
        width = UNIT // rows
        units += [(index, first, width) for first in range(0, columns, width)]
    return units


def gather_phases(place, mail, unit, source, full, local_sem):
    y, x, z, c = place.y, place.x, place.z, place.c
    nz = place.depth - 1

    def first():
        pltpu.make_async_copy(source, full(y, x, z, c, ALL), local_sem).start()
        for k in range(nz):
            mail.send(unit, k, source, full(y, x, z, c, ALL), place.column(place.ahead[k]))

    def second():
        pltpu.make_async_copy(source, full(y, x, z, c, ALL), local_sem).wait()
        for k in range(nz):
            q = place.behind[k]
            mail.arrived(unit, k, full(y, x, q, c, ALL), place.column(q))
        mail.send(unit, 3, full(y, x, ALL, c, 0), full(y, x, ALL, c, 0), place.along_x)
        mail.send(unit, 4, full(y, x, ALL, c, 1), full(y, x, ALL, c, 1), place.along_y)

    def third():
        mail.arrived(unit, 3, full(y, 1 - x, ALL, c, 0), place.along_x)
        mail.send(unit, 5, full(y, ALL, ALL, c, 0), full(y, ALL, ALL, c, 0), place.along_y)
        mail.arrived(unit, 4, full(1 - y, x, ALL, c, 1), place.along_y)
        mail.send(unit, 6, full(ALL, x, ALL, c, 1), full(ALL, x, ALL, c, 1), place.along_x)

    def fourth():
        mail.arrived(unit, 5, full(1 - y, ALL, ALL, c, 0), place.along_y)
        mail.arrived(unit, 6, full(ALL, 1 - x, ALL, c, 1), place.along_x)
        mail.send(unit, 7, full(ALL, ALL, ALL, c, ALL), full(ALL, ALL, ALL, c, ALL), place.other_core)

    def last():
        mail.arrived(unit, 7, full(ALL, ALL, ALL, 1 - c, ALL), place.other_core)

    return first, second, third, fourth, last


def small_gather_phases(place, mail, unit, source, full, local_sem):
    y, x, z, c = place.y, place.x, place.z, place.c
    nz = place.depth - 1

    def first():
        pltpu.make_async_copy(source, full.at[y, x, z, c], local_sem).start()
        for k in range(nz):
            mail.send(unit, k, source, full.at[y, x, z, c], place.column(place.ahead[k]))

    def second():
        pltpu.make_async_copy(source, full.at[y, x, z, c], local_sem).wait()
        for k in range(nz):
            q = place.behind[k]
            mail.arrived(unit, k, full.at[y, x, q, c], place.column(q))
        mail.send(unit, 3, full.at[y, x, :, c], full.at[y, x, :, c], place.along_x)

    def third():
        mail.arrived(unit, 3, full.at[y, 1 - x, :, c], place.along_x)
        mail.send(unit, 5, full.at[y, :, :, c], full.at[y, :, :, c], place.along_y)

    def fourth():
        mail.arrived(unit, 5, full.at[1 - y, :, :, c], place.along_y)
        mail.send(unit, 7, full.at[:, :, :, c], full.at[:, :, :, c], place.other_core)

    def last():
        mail.arrived(unit, 7, full.at[:, :, :, 1 - c], place.other_core)

    return first, second, third, fourth, last


def by_rows(left, right):
    return contract(left, right, 1, 1)


def by_columns(left, right):
    return contract(left, right, 0, 0)


def plain(left, right):
    return jnp.dot(left, right, preferred_element_type=jnp.float32)


class Table:
    GAIN_ONE, SHIFT_ONE, QUERY, VALUE, OUT, GAIN_TWO, SHIFT_TWO, DOWN = range(8)

    def __init__(self, packed, narrow, wide):
        self.packed, self.narrow, self.wide = packed, narrow, wide

    def expand(self, devices):
        y_count, x_count, z_count, c_count = self.packed.shape[:4]

        def tile(d):
            d, c = divmod(d, c_count)
            d, z = divmod(d, z_count)
            y, x = divmod(d, x_count)
            return self.packed[y, x, z, c]

        group = lax.broadcasted_iota(jnp.int32, (8, 128), 1) // 32
        for base in range(0, devices, 4):
            tiles = [tile(base + i) for i in range(4)]
            for i in range(4):
                self.wide[:, pl.ds(128 * (base + i), 128)] = tiles[i][0:1, :]
            for q in range(4):
                mixed = jnp.zeros((8, 128), jnp.float32)
                for i in range(4):
                    turned = tiles[i] if i == q else pltpu.roll(tiles[i], 32 * ((i - q) % 4), 1)
                    mixed = jnp.where(group == i, turned, mixed)
                self.narrow[q, :, pl.ds(32 * base, 128)] = mixed

    def __getitem__(self, index):
        return self.narrow[index % 4, 1 + index // 4 : 2 + index // 4, :]


def row_facts(lengths, codes, row):
    begin = jnp.int32(0)
    segment = jnp.zeros(row.shape, jnp.int32)
    first = jnp.zeros(row.shape, jnp.int32)
    code = jnp.full(row.shape, codes[0, 0], jnp.int32)
    for item in range(1, lengths.shape[1]):
        begin = begin + lengths[0, item - 1]
        inside = row >= begin
        segment = jnp.where(inside, item, segment)
        first = jnp.where(inside, begin, first)
        code = jnp.where(inside, codes[0, item], code)
    return segment, (row - first).astype(jnp.float32) * (0.5 * (code.astype(jnp.float32) + 1.0))


def fill_mask(lengths, codes, mask):
    rows = mask.shape[0]
    across, _ = row_facts(lengths, codes, lax.broadcasted_iota(jnp.int32, (1, rows), 1))
    for base in range(0, rows, 128):
        down, _ = row_facts(lengths, codes, lax.broadcasted_iota(jnp.int32, (128, 1), 0) + base)
        mask[base : base + 128, :] = jnp.where(down == across, 0.0, -1e30)


def head_half(rows, which):
    lane = lax.broadcasted_iota(jnp.int32, (rows, 2 * HEAD_DIM), 1)
    return (lane >= HEAD_DIM) if which else (lane < HEAD_DIM)


def pair_span(pair, offset):
    return pl.ds(pl.multiple_of(offset + pair * 2 * HEAD_DIM, 2 * HEAD_DIM), 2 * HEAD_DIM)


def attend(first_pair, last_pair, projected, mask, attended):
    rows, width = attended.shape
    zero = jnp.zeros((), jnp.bfloat16)
    scale = jnp.asarray(1.0 / math.sqrt(HEAD_DIM), jnp.bfloat16)

    def one_pair(pair, carry):
        query = projected[:, pair_span(pair, 0)] * scale
        key = projected[:, pair_span(pair, width)]
        value = projected[:, pair_span(pair, 2 * width)]
        results = []
        for which in range(2):
            scores = by_rows(jnp.where(head_half(rows, which), query, zero), key) + mask[...]
            top = jnp.max(scores, axis=1, keepdims=True)
            expon = jnp.exp(scores - top)
            total = jnp.sum(expon, axis=1, keepdims=True)
            weights = (expon * (1.0 / total)).astype(jnp.bfloat16)
            results.append(plain(weights, value))
        mixed = jnp.where(head_half(rows, 0), results[0], results[1])
        attended[:, pair_span(pair, 0)] = mixed.astype(jnp.bfloat16)
        return carry

    lax.fori_loop(first_pair, last_pair, one_pair, 0)


CHUNK = 64


def over_rows(rows, step):
    def one(index, carry):
        step(pl.ds(pl.multiple_of(index * CHUNK, CHUNK), CHUNK), index * CHUNK)
        return carry

    lax.fori_loop(0, rows // CHUNK, one, 0)


def normalised(values):
    centred = values - jnp.mean(values, axis=-1, keepdims=True)
    variance = jnp.mean(centred * centred, axis=-1, keepdims=True)
    scale = lax.rsqrt(variance + EPSILON)
    return centred * scale, scale


def forward_kernel(depth, units, *refs):
    (s_qkv, s_out, s_up, s_down, small, tokens, lengths, codes) = refs[:8]
    (f_qkv, f_out, f_up, f_down, o_narrow, o_projected, o_attended, o_start, o_middle, o_activated, o_slope, o_output) = refs[8:20]
    (packed, narrow, wide, start, normed, projected, attended, middle, activated, slope, output, mask, square, tall,
     send_sem, recv_sem, local_sem, load_sem, store_sem) = refs[20:]
    place, mail = Place(depth), Mail(send_sem, recv_sem)
    rows, width = start.shape
    table = Table(packed, narrow, wide)
    place.greet()
    sources, fulls = (s_qkv, s_out, s_up, s_down), (f_qkv, f_out, f_up, f_down)

    steps, loads = [], []
    small_step = small_gather_phases(place, mail, 0, small, packed, local_sem.at[0])
    seen = [0, 0]
    for unit, (index, first, columns) in enumerate(units, 1):
        span = pl.ds(first, columns)

        def view(*at, ref=fulls[index], span=span):
            return ref.at[at + (ALL, span)]

        steps.append(
            gather_phases(
                place, mail, unit, sources[index].at[:, :, span], view, local_sem.at[unit]
            )
        )
        kind = 1 if index == 3 else 0
        buffer = (square, tall)[kind]
        loads.append(
            (
                pltpu.make_async_copy(
                    fulls[index].at[:, :, :, :, :, :, span],
                    buffer.at[seen[kind] % 2],
                    load_sem.at[unit],
                ),
                buffer,
                seen[kind] % 2,
            )
        )
        seen[kind] += 1
    stores = []

    def store(source, target):
        copy = pltpu.make_async_copy(source, target, store_sem.at[len(stores)])
        copy.start()
        stores.append(copy)

    def weights(unit, columns):
        _, buffer, at = loads[unit]
        block = buffer[at, :, :, :, :, :, :, columns]
        return block.reshape(-1, block.shape[-1])

    def prepare():
        def chunk(span, base):
            row = lax.broadcasted_iota(jnp.int32, (CHUNK, 1), 0) + base
            _, factor = row_facts(lengths, codes, row)
            lane = lax.broadcasted_iota(jnp.int32, (1, width // 2), 1).astype(jnp.float32)
            phase = factor * jnp.exp(lane * (-math.log(10000.0) / (width // 2)))
            low, high = pl.ds(0, width // 2), pl.ds(width // 2, width // 2)
            start[span, low] = tokens[span, low].astype(jnp.float32) + jnp.sin(phase)
            start[span, high] = tokens[span, high].astype(jnp.float32) + jnp.cos(phase)

        over_rows(rows, chunk)
        store(start, o_start)
        fill_mask(lengths, codes, mask)

    def norm(values, gain, shift):
        def chunk(span, base):
            normed[span, :] = (normalised(values[span, :])[0] * table[gain] + table[shift]).astype(jnp.bfloat16)

        over_rows(rows, chunk)

    def norm_one():
        table.expand(PLANE * PLANE * depth * CORES)
        store(narrow, o_narrow)
        norm(start, Table.GAIN_ONE, Table.SHIFT_ONE)

    def project(unit, bias):
        tile = 512
        for first in range(0, width, tile):
            value = plain(normed[...], weights(unit, pl.ds(first, tile)))
            if bias is not None:
                value = value + table[bias][:, first : first + tile]
            projected[:, pl.ds(unit * width + first, tile)] = value.astype(jnp.bfloat16)

    def project_out(unit):
        tile = 512
        for first in range(0, width, tile):
            span = pl.ds(first, tile)
            value = plain(attended[...], weights(unit, span)) + table[Table.OUT][:, first : first + tile]
            middle[:, span] = start[:, span] + value
        store(middle, o_middle)
        norm(middle, Table.GAIN_TWO, Table.SHIFT_TWO)

    def rise(unit, number):
        tile = 256

        def one(index, carry):
            at = pl.multiple_of(index * tile, tile)
            there = pl.ds(pl.multiple_of(number * width + at, tile), tile)
            pre = plain(normed[...], weights(unit, pl.ds(at, tile))) + wide[:, there]
            normal = 0.5 * (1.0 + lax.erf(pre * math.sqrt(0.5)))
            density = jnp.exp(pre * pre * -0.5) * (1.0 / math.sqrt(2.0 * math.pi))
            activated[:, there] = (pre * normal).astype(jnp.bfloat16)
            slope[:, there] = (normal + pre * density).astype(jnp.bfloat16)
            return carry

        lax.fori_loop(0, width // tile, one, 0)
        there = pl.ds(number * width, width)
        store(activated.at[:, there], o_activated.at[:, there])
        store(slope.at[:, there], o_slope.at[:, there])

    def fall(unit, number, columns):
        span = pl.ds(number * columns, columns)
        value = plain(activated[...], weights(unit, ALL)) + table[Table.DOWN][:, number * columns : (number + 1) * columns]
        output[:, span] = (middle[:, span] + value).astype(jnp.bfloat16)
        store(output.at[:, span], o_output.at[:, span])

    pairs = width // (2 * HEAD_DIM)
    total = len(units)
    for turn in range(total + 4):
        for phase in range(5):
            unit = turn - phase
            if unit == 0:
                small_step[phase]()
            if 0 <= unit < total:
                steps[unit][phase]()
                if phase == 4:
                    loads[unit][0].start()
        if turn == 0:
            prepare()
        unit = turn - 4
        if unit < 0:
            continue
        index, first, columns = units[unit]
        if unit == 0:
            norm_one()
        if unit == 3:
            attend(pairs // 2, pairs, projected, mask, attended)
            store(attended, o_attended)
        loads[unit][0].wait()
        if index == 0:
            project(unit, (Table.QUERY, None, Table.VALUE)[unit])
            if unit == 2:
                store(projected, o_projected)
                attend(0, pairs // 2, projected, mask, attended)
        elif index == 1:
            project_out(unit)
        elif index == 2:
            rise(unit, first // columns)
        else:
            fall(unit, first // columns, columns)
    for copy in stores:
        copy.wait()
    mail.finish()


def run_forward(mesh, tokens, lengths, codes, matrices, vectors):
    depth = mesh.shape["fsdp"] // CORES
    grid = (PLANE, PLANE, depth, CORES)
    rows, width = tokens.shape
    hidden = matrices[2].shape[1]
    halves = [m.reshape(2, m.shape[0] // 2, m.shape[1]) for m in matrices]
    units = unit_list([(m.shape[0] * mesh.size, m.shape[1]) for m in matrices])
    flat = jnp.concatenate([vectors[-1], *vectors[:-1]]).astype(jnp.float32)
    small = jnp.pad(flat, (0, 1024 - flat.size)).reshape(8, 128)
    low, full = jnp.bfloat16, jnp.float32

    def shaped(*shape, dtype=low):
        return jax.ShapeDtypeStruct(shape, dtype)

    anywhere = pl.BlockSpec(memory_space=pl.ANY)
    vmem = pl.BlockSpec(memory_space=pltpu.VMEM)
    smem = pl.BlockSpec(memory_space=pltpu.SMEM)
    count = len(units) + 1
    square = UNIT // width
    tall = UNIT // hidden
    return pl.pallas_call(
        functools.partial(forward_kernel, depth, units),
        out_shape=[shaped(*grid, *h.shape) for h in halves]
        + [
            shaped(4, 8, width, dtype=full),
            shaped(rows, 3 * width),
            shaped(rows, width),
            shaped(rows, width, dtype=full),
            shaped(rows, width, dtype=full),
            shaped(rows, hidden),
            shaped(rows, hidden),
            shaped(rows, width),
        ],
        in_specs=[anywhere] * 5 + [vmem, smem, smem],
        out_specs=[anywhere] * 12,
        scratch_shapes=[
            pltpu.VMEM((*grid, 8, 128), full),
            pltpu.VMEM((4, 8, width), full),
            pltpu.VMEM((1, hidden), full),
            pltpu.VMEM((rows, width), full),
            pltpu.VMEM((rows, width), low),
            pltpu.VMEM((rows, 3 * width), low),
            pltpu.VMEM((rows, width), low),
            pltpu.VMEM((rows, width), full),
            pltpu.VMEM((rows, hidden), low),
            pltpu.VMEM((rows, hidden), low),
            pltpu.VMEM((rows, width), low),
            pltpu.VMEM((rows, rows), full),
            pltpu.VMEM((2, *grid, 2, width // mesh.size // 2, square), low),
            pltpu.VMEM((2, *grid, 2, hidden // mesh.size // 2, tall), low),
            pltpu.SemaphoreType.DMA((count, SLOTS)),
            pltpu.SemaphoreType.DMA((count, SLOTS)),
            pltpu.SemaphoreType.DMA((count,)),
            pltpu.SemaphoreType.DMA((count,)),
            pltpu.SemaphoreType.DMA((24,)),
        ],
        compiler_params=pltpu.CompilerParams(
            collective_id=0, has_side_effects=True, vmem_limit_bytes=58 << 20
        ),
    )(*halves, small, tokens, lengths, codes)


def attend_back(first_pair, last_pair, projected, mask, grad_attended, sums, weights_low, grad_low):
    rows, width = grad_attended.shape
    zero = jnp.zeros((), jnp.bfloat16)
    scale = 1.0 / math.sqrt(HEAD_DIM)

    def one_pair(pair, carry):
        query, key, value = (projected[:, pair_span(pair, k * width)] for k in range(3))
        grad = grad_attended[:, pair_span(pair, 0)]
        scaled = query * jnp.asarray(scale, jnp.bfloat16)
        g_query, g_key, g_value = [], [], []
        for which in range(2):
            keep = head_half(rows, which)
            scores = by_rows(jnp.where(keep, key, zero), scaled) + mask[...]
            expon = jnp.exp(scores - jnp.max(scores, axis=0, keepdims=True))
            weights = expon * (1.0 / jnp.sum(expon, axis=0, keepdims=True))
            weights_low[which] = weights.astype(jnp.bfloat16)
            slopes = by_rows(jnp.where(keep, value, zero), grad)
            level = jnp.sum(weights * slopes, axis=0, keepdims=True)
            grad_low[which] = (weights * (slopes - level)).astype(jnp.bfloat16)
            g_value.append(plain(weights_low[which], grad))
            g_key.append(plain(grad_low[which], query))
            g_query.append(by_columns(grad_low[which], key))
        keep = head_half(rows, 0)
        for k, (parts, factor) in enumerate(((g_query, scale), (g_key, scale), (g_value, 1.0))):
            mixed = (jnp.where(keep, parts[0], parts[1]) * factor).astype(jnp.bfloat16)
            projected[:, pair_span(pair, k * width)] = mixed
            if k != 1:
                slot = Table.QUERY if k == 0 else Table.VALUE
                total = jnp.sum(mixed.astype(jnp.float32), axis=0, keepdims=True)
                sums[slot % 4, 1 + slot // 4 : 2 + slot // 4, pair_span(pair, 0)] = total
        return carry

    lax.fori_loop(first_pair, last_pair, one_pair, 0)


INBOXES = 6
HELD = 4
TILE = 256


def backward_kernel(depth, units, *refs):
    (f_qkv, f_out, f_up, f_down, narrow, a_projected, a_attended, a_start, a_middle, a_activated, a_slope, cotangent,
     lengths, codes) = refs[:14]
    (o_qkv, o_out, o_up, o_down, o_small, o_tokens) = refs[14:20]
    (inbox, wide_in, near_in, column_in, r_square, r_tall, parts, s_part, s_core, s_wide, s_near, s_column, s_result,
     first_big, hidden_grad, slope, rows_up, rows_down, stream, grad_middle, grad_normed, normed, branch, grad_attended,
     weights_low, grad_low, mask, sums, wide_sums, tokens_out,
     send_sem, recv_sem, load_sem, store_sem, free_sem) = refs[20:]
    place, mail = Place(depth), Mail(send_sem, recv_sem)
    y, x, z, c = place.y, place.x, place.z, place.c
    nz = depth - 1
    rows, width = cotangent.shape
    hidden = hidden_grad.shape[1]
    table = Table(None, narrow, None)
    outs = (o_qkv, o_out, o_up, o_down)
    low, full = jnp.bfloat16, jnp.float32
    place.greet()
    stores = []

    def load(number, source, target):
        return pltpu.make_async_copy(source, target, load_sem.at[number])

    def store(source, target):
        copy = pltpu.make_async_copy(source, target, store_sem.at[len(stores)])
        copy.start()
        stores.append(copy)

    corners = [(a, b) for a in range(PLANE) for b in range(PLANE)]
    half = depth // 2
    get_activated = load(0, a_activated, first_big)
    get_middle = load(1, a_middle, stream)
    get_projected = load(2, a_projected, first_big.at[:, pl.ds(0, 3 * width)])
    get_attended = load(3, a_attended, first_big.at[:, pl.ds(3 * width, width)])
    get_start = load(4, a_start, stream)
    eighth = hidden // 8
    get_down = [
        load(8 + n, f_down.at[a, b, pl.ds(half * k, half)], rows_down.at[n % 2])
        for n, (a, b, k) in enumerate((a, b, k) for a, b in corners for k in range(2))
    ]
    get_slope = [
        load(16 + n, a_slope.at[:, pl.ds(eighth * n, eighth)], slope.at[n % 2]) for n in range(8)
    ]
    get_up = [load(24 + n, f_up.at[a, b], rows_up.at[n % 2]) for n, (a, b) in enumerate(corners)]
    get_out = [
        load(28 + n, f_out.at[a, b], rows_up.at[0, :, :, :, :, pl.ds(n * width, width)])
        for n, (a, b) in enumerate(corners)
    ]
    get_qkv = [
        load(32 + n, f_qkv.at[a, b], rows_up.at[(n + 1) % 2, :, :, :, :, pl.ds(0, 3 * width)])
        for n, (a, b) in enumerate(corners)
    ]

    def flat(block):
        return block.reshape(-1, block.shape[-1])

    def tally(slot, values):
        at = (slot % 4, pl.ds(1 + slot // 4, 1), ALL)
        sums[at] = sums[at] + jnp.sum(values, axis=0, keepdims=True)

    def square_part(unit, left, left_at, right, right_at):
        for k in range(width // TILE):
            span = pl.ds(right_at + TILE * k, TILE)
            value = by_columns(left[:, pl.ds(left_at, width)], right[:, span]).astype(low)
            shape = parts.shape[1:6] + (parts.shape[7], TILE)
            parts[unit % HELD, :, :, :, :, :, k] = value.reshape(shape)

    def tall_part(unit, number):
        def one(corner, carry):
            left = first_big[:, pl.ds(pl.multiple_of(corner * width, width), width)]
            value = by_columns(left, cotangent[:, pl.ds(TILE * number, TILE)]).astype(low)
            parts[unit % HELD, corner // PLANE, corner % PLANE] = value.reshape(parts.shape[3:])
            return carry

        lax.fori_loop(0, PLANE * PLANE, one, 0)

    def hidden_step(n):
        get_down[n].wait()
        get_slope[n].wait()
        span = pl.ds(eighth * n, eighth)
        value = by_rows(cotangent[...], flat(rows_down[n % 2])) * slope[n % 2].astype(full)
        value = value.astype(low)
        hidden_grad[:, span] = value
        wide_sums[:, span] = jnp.sum(value.astype(full), axis=0, keepdims=True)
        if n + 2 < 8:
            get_down[n + 2].start()
            get_slope[n + 2].start()

    def up_step(n):
        get_up[n].wait()
        grad_normed[:, pl.ds(TILE * n, TILE)] = by_rows(hidden_grad[...], flat(rows_up[n % 2]))
        if n + 2 < 4:
            get_up[n + 2].start()
        if n == 2:
            for copy in get_out:
                copy.start()
        if n == 3:
            get_qkv[0].start()

    def out_step():
        for n in range(4):
            get_out[n].wait()
        for n in range(4):
            block = flat(rows_up[0, :, :, :, :, pl.ds(n * width, width)])
            grad_attended[:, pl.ds(TILE * n, TILE)] = by_rows(branch[...], block).astype(low)
        get_qkv[1].start()

    def qkv_step(n):
        get_qkv[n].wait()
        block = flat(rows_up[(n + 1) % 2, :, :, :, :, pl.ds(0, 3 * width)])
        grad_normed[:, pl.ds(TILE * n, TILE)] = by_rows(first_big[:, pl.ds(0, 3 * width)], block)
        if n + 2 < 4:
            get_qkv[n + 2].start()

    def norm(gain, shift):
        def chunk(span, base):
            normed[span, :] = (normalised(stream[span, :])[0] * table[gain] + table[shift]).astype(low)

        over_rows(rows, chunk)

    def norm_back(span, gain, shift):
        level, scale = normalised(stream[span, :])
        grad = grad_normed[span, :]
        tally(gain, grad * level)
        tally(shift, grad)
        grad = grad * table[gain]
        mean = jnp.mean(grad, axis=-1, keepdims=True)
        along = jnp.mean(grad * level, axis=-1, keepdims=True)
        return scale * (grad - mean - level * along)

    def second_norm_back():
        def chunk(span, base):
            value = cotangent[span, :].astype(full) + norm_back(span, Table.GAIN_TWO, Table.SHIFT_TWO)
            grad_middle[span, :] = value
            branch[span, :] = value.astype(low)
            tally(Table.OUT, value.astype(low).astype(full))
            tally(Table.DOWN, cotangent[span, :].astype(full))

        over_rows(rows, chunk)

    def first_norm_back():
        def chunk(span, base):
            value = grad_middle[span, :] + norm_back(span, Table.GAIN_ONE, Table.SHIFT_ONE)
            tokens_out[span, :] = value.astype(low)

        over_rows(rows, chunk)
        store(tokens_out, o_tokens)

    def attention(first, last):
        attend_back(
            first, last, first_big, mask, grad_attended, sums, weights_low, grad_low
        )

    def pack():
        group = lax.broadcasted_iota(jnp.int32, (8, 128), 1) // 32
        line = lax.broadcasted_iota(jnp.int32, (8, 128), 0)
        shape = s_part.shape[:4]
        for device in range(math.prod(shape)):
            i, base = device % 4, 32 * (device - device % 4)
            mixed = jnp.zeros((8, 128), full)
            for q in range(4):
                tile = sums[q, :, pl.ds(base, 128)]
                turned = tile if i == q else pltpu.roll(tile, 32 * ((q - i) % 4), 1)
                mixed = jnp.where(group == q, turned, mixed)
            share = jnp.broadcast_to(wide_sums[:, pl.ds(128 * device, 128)], (8, 128))
            at, k = divmod(device, shape[3])
            at, m = divmod(at, shape[2])
            s_part[at // shape[1], at % shape[1], m, k] = jnp.where(line == 0, share, mixed)

    def unit_steps(unit):
        index, start, columns = units[unit]
        part, held = parts.at[unit % HELD], inbox.at[unit % INBOXES]
        wide, near, column = wide_in.at[unit], near_in.at[unit], column_in.at[unit]

        def first():
            if unit >= INBOXES:
                pl.semaphore_wait(free_sem.at[unit], 1)
            mail.send(unit, 7, part.at[:, :, :, 1 - c], held, place.other_core)

        def second():
            mail.arrived(unit, 7, held, place.other_core)
            for a, b in corners:
                held[a, b] = held[a, b] + part[a, b, :, c]
            mail.send(unit, 5, held.at[1 - y, :, :, 0], wide.at[0], place.along_y)
            mail.send(unit, 6, held.at[:, 1 - x, :, 1], wide.at[1], place.along_x)
            mail.settle(unit, 7)

        def third():
            mail.arrived(unit, 5, wide.at[0], place.along_y)
            mail.arrived(unit, 6, wide.at[1], place.along_x)
            for b in range(PLANE):
                held[y, b, :, 0] = held[y, b, :, 0] + wide[0, b]
                held[b, x, :, 1] = held[b, x, :, 1] + wide[1, b]
            mail.send(unit, 3, held.at[y, 1 - x, :, 0], near.at[0], place.along_x)
            mail.send(unit, 4, held.at[1 - y, x, :, 1], near.at[1], place.along_y)

        def fourth():
            mail.arrived(unit, 3, near.at[0], place.along_x)
            mail.arrived(unit, 4, near.at[1], place.along_y)
            for h in range(2):
                held[y, x, :, h] = held[y, x, :, h] + near[h]
            for k in range(nz):
                q = place.ahead[k]
                mail.send(unit, k, held.at[y, x, q], column.at[k], place.column(q))

        def last():
            total = held[y, x, z].astype(full)
            for k in range(nz):
                mail.arrived(unit, k, column.at[k], place.column(place.behind[k]))
                total = total + column[k].astype(full)
            if index == 3:
                final = r_tall.at[unit]
                final[...] = total
                store(final, outs[index].at[:, :, :, pl.ds(start, columns)])
            else:
                final = r_square.at[unit - 4]
                for k in range(total.shape[1]):
                    final[:, :, pl.ds(TILE * k, TILE)] = total[:, k]
                store(final, outs[index].at[:, :, pl.ds(start, columns)])
            for slot in (5, 6, 3, 4, *range(nz)):
                mail.settle(unit, slot)
            if unit + INBOXES < len(units):
                pl.semaphore_signal(
                    free_sem.at[unit + INBOXES], inc=1, device_id=place.other_core, device_id_type=MESH
                )

        return first, second, third, fourth, last

    def small_steps():
        unit = len(units)
        held = s_core

        def first():
            mail.send(unit, 7, s_part.at[:, :, :, 1 - c], held, place.other_core)

        def second():
            mail.arrived(unit, 7, held, place.other_core)
            for a, b in corners:
                held[a, b] = held[a, b] + s_part[a, b, :, c]
            mail.send(unit, 5, held.at[1 - y], s_wide, place.along_y)

        def third():
            mail.arrived(unit, 5, s_wide, place.along_y)
            held[y] = held[y] + s_wide[...]
            mail.send(unit, 3, held.at[y, 1 - x], s_near, place.along_x)

        def fourth():
            mail.arrived(unit, 3, s_near, place.along_x)
            held[y, x] = held[y, x] + s_near[...]
            for k in range(nz):
                q = place.ahead[k]
                mail.send(unit, k, held.at[y, x, q], s_column.at[k], place.column(q))

        def last():
            total = held[y, x, z]
            for k in range(nz):
                mail.arrived(unit, k, s_column.at[k], place.column(place.behind[k]))
                total = total + s_column[k]
            s_result[...] = total
            store(s_result, o_small)

        return first, second, third, fourth, last

    steps = [unit_steps(unit) for unit in range(len(units))] + [small_steps()]

    def part_of(unit):
        index, start, columns = units[unit]
        if index == 3:
            tall_part(unit, start // columns)
        elif index == 2:
            square_part(unit, normed, 0, hidden_grad, start)
        elif index == 1:
            square_part(unit, first_big, 3 * width, branch, 0)
        else:
            square_part(unit, normed, 0, first_big, start)

    def filler(turn):
        if turn == 0:
            for n in range(4):
                hidden_step(n)
        elif turn == 1:
            for n in range(4, 8):
                hidden_step(n)
        elif turn == 2:
            get_middle.wait()
            norm(Table.GAIN_TWO, Table.SHIFT_TWO)
            for n in range(4):
                up_step(n)
        elif turn == 3:
            get_projected.start()
            get_attended.start()
            second_norm_back()
            get_start.start()
            out_step()
            get_projected.wait()
            get_attended.wait()
        elif turn < 8:
            attention(2 * (turn - 4), 2 * (turn - 3))
        elif turn == 8:
            get_start.wait()
            norm(Table.GAIN_ONE, Table.SHIFT_ONE)
            qkv_step(0)
        elif turn == 9:
            qkv_step(1)
        elif turn == 10:
            qkv_step(2)
            qkv_step(3)
        elif turn == 11:
            first_norm_back()
            pack()

    for copy in (get_activated, get_down[0], get_slope[0], get_down[1], get_slope[1], get_middle, get_up[0], get_up[1]):
        copy.start()
    sums[...] = jnp.zeros_like(sums)
    fill_mask(lengths, codes, mask)
    get_activated.wait()
    total = len(steps)
    for turn in range(total + 3):
        if turn < total:
            if turn < len(units):
                part_of(turn)
            steps[turn][0]()
            filler(turn)
        for phase in range(1, 5):
            if 0 <= turn - phase + 1 < total:
                steps[turn - phase + 1][phase]()
    for copy in stores:
        copy.wait()
    mail.finish()


def run_backward(mesh, saved, cotangent, lengths, codes, shapes):
    depth = mesh.shape["fsdp"] // CORES
    grid = (PLANE, PLANE, depth, CORES)
    plane = (PLANE, PLANE, depth)
    rows, width = cotangent.shape
    hidden = shapes[2][1]
    devices = mesh.size
    low, full = jnp.bfloat16, jnp.float32
    listed = unit_list(shapes)
    units = [u for index in (3, 2, 1, 0) for u in listed if u[0] == index]
    count = len(units)
    share = width // devices // 2
    block = (2, width // TILE, share, TILE)
    inner = block[1:]
    anywhere = pl.BlockSpec(memory_space=pl.ANY)
    vmem = pl.BlockSpec(memory_space=pltpu.VMEM)
    smem = pl.BlockSpec(memory_space=pltpu.SMEM)
    talls = sum(u[0] == 3 for u in units)
    outs = pl.pallas_call(
        functools.partial(backward_kernel, depth, units),
        out_shape=[
            jax.ShapeDtypeStruct((2, share, shapes[0][1]), full),
            jax.ShapeDtypeStruct((2, share, shapes[1][1]), full),
            jax.ShapeDtypeStruct((2, share, shapes[2][1]), full),
            jax.ShapeDtypeStruct((2, hidden // width, share, width), full),
            jax.ShapeDtypeStruct((8, 128), full),
            jax.ShapeDtypeStruct((rows, width), low),
        ],
        in_specs=[anywhere] * 4 + [vmem] + [anywhere] * 6 + [vmem, smem, smem],
        out_specs=[anywhere] * 6,
        scratch_shapes=[
            pltpu.VMEM((INBOXES, *plane, *block), low),
            pltpu.VMEM((count, 2, PLANE, depth, *inner), low),
            pltpu.VMEM((count, 2, depth, *inner), low),
            pltpu.VMEM((count, depth - 1, *block), low),
            pltpu.VMEM((count - talls, 2, share, width), full),
            pltpu.VMEM((talls, *block), full),
            pltpu.VMEM((HELD, *grid, *block), low),
            pltpu.VMEM((*grid, 8, 128), full),
            pltpu.VMEM((*plane, 8, 128), full),
            pltpu.VMEM((PLANE, depth, 8, 128), full),
            pltpu.VMEM((depth, 8, 128), full),
            pltpu.VMEM((depth - 1, 8, 128), full),
            pltpu.VMEM((8, 128), full),
            pltpu.VMEM((rows, hidden), low),
            pltpu.VMEM((rows, hidden), low),
            pltpu.VMEM((2, rows, hidden // 8), low),
            pltpu.VMEM((2, depth, CORES, 2, share, hidden), low),
            pltpu.VMEM((2, depth // 2, CORES, 2, share * (hidden // width), width), low),
            pltpu.VMEM((rows, width), full),
            pltpu.VMEM((rows, width), full),
            pltpu.VMEM((rows, width), full),
            pltpu.VMEM((rows, width), low),
            pltpu.VMEM((rows, width), low),
            pltpu.VMEM((rows, width), low),
            pltpu.VMEM((2, rows, rows), low),
            pltpu.VMEM((2, rows, rows), low),
            pltpu.VMEM((rows, rows), full),
            pltpu.VMEM((4, 8, width), full),
            pltpu.VMEM((1, hidden), full),
            pltpu.VMEM((rows, width), low),
            pltpu.SemaphoreType.DMA((count + 1, SLOTS)),
            pltpu.SemaphoreType.DMA((count + 1, SLOTS)),
            pltpu.SemaphoreType.DMA((40,)),
            pltpu.SemaphoreType.DMA((24,)),
            pltpu.SemaphoreType.REGULAR((count,)),
        ],
        compiler_params=pltpu.CompilerParams(
            collective_id=1, has_side_effects=True, vmem_limit_bytes=62 << 20
        ),
    )(*saved, cotangent, lengths, codes)
    grads = [o.reshape(-1, o.shape[-1]) for o in outs[:4]]
    spread = outs[4].reshape(-1)
    wide, narrow = hidden // devices, width // devices
    return outs[5], grads, [spread[wide + narrow * k : wide + narrow * (k + 1)] for k in range(8)], spread[:wide]


def grid_body(mesh, tokens, cotangent, lengths, scale_codes, *params):
    matrices = params[:4]
    (gain_one, shift_one, bias_query, bias_value, bias_out, gain_two, shift_two, bias_up, bias_down) = params[4:]
    vectors = (gain_one, shift_one, bias_query, bias_value, bias_out, gain_two, shift_two, bias_down, bias_up)
    *saved, output = run_forward(mesh, tokens, lengths, scale_codes, matrices, vectors)
    shapes = [(m.shape[0] * mesh.size, m.shape[1]) for m in matrices]
    grad_tokens, grads, small, grad_up_bias = run_backward(mesh, saved, cotangent, lengths, scale_codes, shapes)
    return (output, grad_tokens, *grads, *small[:7], grad_up_bias, small[7])


def solution(mesh):
    placed = (
        P(("dp", "fsdp"), None),
        P(("dp", "fsdp"), None),
        P(("dp", "fsdp"), None),
        P(("dp", "fsdp"), None),
        P(("dp", "fsdp"), None),
        P(("dp", "fsdp"), None),
        P(("dp", "fsdp"), None),
        P(("dp", "fsdp"), None),
        P(("dp", "fsdp")),
        P(("dp", "fsdp")),
        P(("dp", "fsdp")),
        P(("dp", "fsdp")),
        P(("dp", "fsdp")),
        P(("dp", "fsdp")),
        P(("dp", "fsdp")),
        P(("dp", "fsdp")),
        P(("dp", "fsdp")),
    )
    per_device = body
    if mesh.shape["dp"] == PLANE * PLANE and mesh.shape["fsdp"] == 4 * CORES:
        per_device = functools.partial(grid_body, mesh)
    return jax.shard_map(
        per_device,
        mesh=mesh,
        in_specs=placed,
        out_specs=(
            P(("dp", "fsdp"), None),
            P(("dp", "fsdp"), None),
            P(("dp", "fsdp"), None),
            P(("dp", "fsdp"), None),
            P(("dp", "fsdp"), None),
            P(("dp", "fsdp"), None),
            P(("dp", "fsdp")),
            P(("dp", "fsdp")),
            P(("dp", "fsdp")),
            P(("dp", "fsdp")),
            P(("dp", "fsdp")),
            P(("dp", "fsdp")),
            P(("dp", "fsdp")),
            P(("dp", "fsdp")),
            P(("dp", "fsdp")),
        ),
        check_vma=False,
    )
```

```python
import functools
import math

import jax
import jax.numpy as jnp
from jax import lax
from jax.experimental import pallas as pl
from jax.experimental.pallas import tpu as pltpu
from jax.sharding import PartitionSpec as P

HEADS = 16
HEAD_DIM = 64


EPSILON = 1e-06


def contract(left, right, left_dim, right_dim):
    return lax.dot_general(
        left, right, (((left_dim,), (right_dim,)), ((), ())), preferred_element_type=jnp.float32
    )


def layer_norm(values, gain, shift):
    centred = values - jnp.mean(values, axis=-1, keepdims=True)
    variance = jnp.mean(centred * centred, axis=-1, keepdims=True)
    return centred * lax.rsqrt(variance + EPSILON) * gain + shift


def gelu_exact(values):
    return jax.nn.gelu(values, approximate=False)


def row_tables(length_row, code_row, row_count, feat_width):
    items = jnp.arange(length_row.shape[0], dtype=jnp.int32)
    item_starts = jnp.sum(
        jnp.where(items[None, :] < items[:, None], length_row[None, :], 0), axis=1
    )
    item_ends = item_starts + length_row
    row_index = jnp.arange(row_count, dtype=jnp.int32)
    member = (
        (row_index[:, None] >= item_starts[None, :]) & (row_index[:, None] < item_ends[None, :])
    ).astype(jnp.int32)
    item_ids = jnp.arange(length_row.shape[0], dtype=jnp.int32)
    segment = jnp.sum(member * item_ids[None, :], axis=1)
    place = row_index - jnp.sum(member * item_starts[None, :], axis=1)
    row_code = jnp.sum(member * code_row[None, :], axis=1)
    half_width = feat_width // 2
    frequency = jnp.exp(
        jnp.arange(half_width, dtype=jnp.float32) * (-math.log(10000.0) / half_width)
    )
    gsd_ratio = 0.5 * (row_code.astype(jnp.float32) + 1.0)
    phase_angle = (place.astype(jnp.float32) * gsd_ratio)[:, None] * frequency[None, :]
    return (segment, jnp.concatenate([jnp.sin(phase_angle), jnp.cos(phase_angle)], axis=1))


def body(
    tokens,
    cotangent,
    lengths,
    scale_codes,
    w_qkv,
    w_out,
    w_up,
    w_down,
    ln1_gain,
    ln1_shift,
    bias_query,
    bias_value,
    bias_out,
    ln2_gain,
    ln2_shift,
    bias_up,
    bias_down,
):
    gathered = (
        lax.all_gather(w_qkv, ("dp", "fsdp"), axis=0, tiled=True),
        lax.all_gather(w_out, ("dp", "fsdp"), axis=0, tiled=True),
        lax.all_gather(w_up, ("dp", "fsdp"), axis=0, tiled=True),
        lax.all_gather(w_down, ("dp", "fsdp"), axis=0, tiled=True),
        lax.all_gather(ln1_gain, ("dp", "fsdp"), axis=0, tiled=True),
        lax.all_gather(ln1_shift, ("dp", "fsdp"), axis=0, tiled=True),
        lax.all_gather(bias_query, ("dp", "fsdp"), axis=0, tiled=True),
        lax.all_gather(bias_value, ("dp", "fsdp"), axis=0, tiled=True),
        lax.all_gather(bias_out, ("dp", "fsdp"), axis=0, tiled=True),
        lax.all_gather(ln2_gain, ("dp", "fsdp"), axis=0, tiled=True),
        lax.all_gather(ln2_shift, ("dp", "fsdp"), axis=0, tiled=True),
        lax.all_gather(bias_up, ("dp", "fsdp"), axis=0, tiled=True),
        lax.all_gather(bias_down, ("dp", "fsdp"), axis=0, tiled=True),
    )
    (
        full_qkv,
        full_out,
        full_up,
        full_down,
        gain_first,
        shift_first,
        query_bias,
        value_bias,
        out_bias,
        gain_second,
        shift_second,
        up_bias,
        down_bias,
    ) = gathered
    gain_one = gain_first.astype(jnp.float32)
    shift_one = shift_first.astype(jnp.float32)
    gain_two = gain_second.astype(jnp.float32)
    shift_two = shift_second.astype(jnp.float32)
    row_count, model_width = tokens.shape
    head_width = model_width // HEADS
    score_scale = 1.0 / math.sqrt(HEAD_DIM)
    segment, encoding = row_tables(lengths[0], scale_codes[0], row_count, model_width)
    same_item = segment[:, None] == segment[None, :]
    start = tokens.astype(jnp.float32) + encoding
    normed_one = layer_norm(start, gain_one, shift_one).astype(jnp.bfloat16)
    qkv_bias = jnp.concatenate([query_bias, jnp.zeros_like(query_bias), value_bias]).astype(
        jnp.float32
    )
    projected = (
        jnp.dot(normed_one, full_qkv, preferred_element_type=jnp.float32) + qkv_bias
    ).astype(jnp.bfloat16)

    def split_heads(block):
        return block.reshape(row_count, HEADS, head_width).transpose(1, 0, 2)

    def join_heads(block):
        return block.transpose(1, 0, 2).reshape(row_count, model_width)

    query_heads = split_heads(projected[:, :model_width])
    key_heads = split_heads(projected[:, model_width : 2 * model_width])
    value_heads = split_heads(projected[:, 2 * model_width :])

    def forward_head(operands):
        query_head, key_head, value_head = operands
        scores = contract(query_head, key_head, 1, 1) * score_scale
        scores = jnp.where(same_item, scores, -1e30)
        top_score = jnp.max(scores, axis=1, keepdims=True)
        expon = jnp.exp(scores - top_score)
        total = jnp.sum(expon, axis=1, keepdims=True)
        weights_low = (expon / total).astype(jnp.bfloat16)
        result = jnp.dot(weights_low, value_head, preferred_element_type=jnp.float32)
        return (result, (top_score + jnp.log(total))[:, 0])

    attended_heads, log_totals = lax.map(forward_head, (query_heads, key_heads, value_heads))
    attended = join_heads(attended_heads).astype(jnp.bfloat16)
    middle = (
        start
        + jnp.dot(attended, full_out, preferred_element_type=jnp.float32)
        + out_bias.astype(jnp.float32)
    )
    normed_two = layer_norm(middle, gain_two, shift_two).astype(jnp.bfloat16)
    hidden_pre = jnp.dot(normed_two, full_up, preferred_element_type=jnp.float32) + up_bias.astype(
        jnp.float32
    )
    activated = gelu_exact(hidden_pre).astype(jnp.bfloat16)
    feed_out = jnp.dot(activated, full_down, preferred_element_type=jnp.float32) + down_bias.astype(
        jnp.float32
    )
    output = (middle + feed_out).astype(jnp.bfloat16)
    back_qkv, back_out, back_up, back_down = (
        lax.all_gather(w_qkv, ("dp", "fsdp"), axis=0, tiled=True),
        lax.all_gather(w_out, ("dp", "fsdp"), axis=0, tiled=True),
        lax.all_gather(w_up, ("dp", "fsdp"), axis=0, tiled=True),
        lax.all_gather(w_down, ("dp", "fsdp"), axis=0, tiled=True),
    )
    grad_output = cotangent.astype(jnp.float32)
    grad_down_bias = jnp.sum(grad_output, axis=0)
    grad_down = contract(activated, cotangent, 0, 0)
    grad_act = contract(cotangent, back_down, 1, 1)
    gelu_value, gelu_pull = jax.vjp(gelu_exact, hidden_pre)
    grad_hidden = gelu_pull(grad_act)[0].astype(jnp.bfloat16)
    grad_up_bias = jnp.sum(grad_hidden.astype(jnp.float32), axis=0)
    grad_up = contract(normed_two, grad_hidden, 0, 0)
    grad_normed_two = contract(grad_hidden, back_up, 1, 1)
    norm_value, second_pull = jax.vjp(layer_norm, middle, gain_two, shift_two)
    grad_middle_part, grad_gain_two, grad_shift_two = second_pull(grad_normed_two)
    grad_middle = grad_output + grad_middle_part
    branch_grad = grad_middle.astype(jnp.bfloat16)
    grad_out_bias = jnp.sum(branch_grad.astype(jnp.float32), axis=0)
    grad_out_weight = contract(attended, branch_grad, 0, 0)
    grad_attended = contract(branch_grad, back_out, 1, 1).astype(jnp.bfloat16)
    grad_heads = split_heads(grad_attended)

    def backward_head(operands):
        query_head, key_head, value_head, grad_head, log_total = operands
        scores = contract(query_head, key_head, 1, 1) * score_scale
        weights = jnp.where(same_item, jnp.exp(scores - log_total[:, None]), 0.0)
        weights_low = weights.astype(jnp.bfloat16)
        grad_weights = contract(grad_head, value_head, 1, 1)
        grad_value = contract(weights_low, grad_head, 0, 0)
        grad_scores = weights * (
            grad_weights - jnp.sum(weights * grad_weights, axis=1, keepdims=True)
        )
        grad_scores_low = grad_scores.astype(jnp.bfloat16)
        grad_query = (
            jnp.dot(grad_scores_low, key_head, preferred_element_type=jnp.float32) * score_scale
        )
        grad_key = contract(grad_scores_low, query_head, 0, 0) * score_scale
        return (grad_query, grad_key, grad_value)

    grad_query_heads, grad_key_heads, grad_value_heads = lax.map(
        backward_head, (query_heads, key_heads, value_heads, grad_heads, log_totals)
    )
    grad_projected = jnp.concatenate(
        [join_heads(grad_query_heads), join_heads(grad_key_heads), join_heads(grad_value_heads)],
        axis=1,
    ).astype(jnp.bfloat16)
    grad_query_bias = jnp.sum(grad_projected[:, :model_width].astype(jnp.float32), axis=0)
    grad_value_bias = jnp.sum(grad_projected[:, 2 * model_width :].astype(jnp.float32), axis=0)
    grad_qkv = contract(normed_one, grad_projected, 0, 0)
    grad_normed_one = contract(grad_projected, back_qkv, 1, 1)
    first_value, first_pull = jax.vjp(layer_norm, start, gain_one, shift_one)
    grad_start_part, grad_gain_one, grad_shift_one = first_pull(grad_normed_one)
    grad_tokens = (grad_middle + grad_start_part).astype(jnp.bfloat16)
    every_grad = (
        lax.psum_scatter(grad_qkv, ("dp", "fsdp"), scatter_dimension=0, tiled=True),
        lax.psum_scatter(grad_out_weight, ("dp", "fsdp"), scatter_dimension=0, tiled=True),
        lax.psum_scatter(grad_up, ("dp", "fsdp"), scatter_dimension=0, tiled=True),
        lax.psum_scatter(grad_down, ("dp", "fsdp"), scatter_dimension=0, tiled=True),
        lax.psum_scatter(grad_gain_one, ("dp", "fsdp"), scatter_dimension=0, tiled=True),
        lax.psum_scatter(grad_shift_one, ("dp", "fsdp"), scatter_dimension=0, tiled=True),
        lax.psum_scatter(grad_query_bias, ("dp", "fsdp"), scatter_dimension=0, tiled=True),
        lax.psum_scatter(grad_value_bias, ("dp", "fsdp"), scatter_dimension=0, tiled=True),
        lax.psum_scatter(grad_out_bias, ("dp", "fsdp"), scatter_dimension=0, tiled=True),
        lax.psum_scatter(grad_gain_two, ("dp", "fsdp"), scatter_dimension=0, tiled=True),
        lax.psum_scatter(grad_shift_two, ("dp", "fsdp"), scatter_dimension=0, tiled=True),
        lax.psum_scatter(grad_up_bias, ("dp", "fsdp"), scatter_dimension=0, tiled=True),
        lax.psum_scatter(grad_down_bias, ("dp", "fsdp"), scatter_dimension=0, tiled=True),
    )
    (
        shard_qkv,
        shard_out,
        shard_up,
        shard_down,
        shard_gain_one,
        shard_shift_one,
        shard_query_bias,
        shard_value_bias,
        shard_out_bias,
        shard_gain_two,
        shard_shift_two,
        shard_up_bias,
        shard_down_bias,
    ) = every_grad
    return (
        output,
        grad_tokens,
        shard_qkv,
        shard_out,
        shard_up,
        shard_down,
        shard_gain_one,
        shard_shift_one,
        shard_query_bias,
        shard_value_bias,
        shard_out_bias,
        shard_gain_two,
        shard_shift_two,
        shard_up_bias,
        shard_down_bias,
    )


PLANE = 2
CORES = 2
UNIT = 1024 * 1024
MESH = pl.DeviceIdType.MESH
ALL = slice(None)


class Place:
    def __init__(self, depth):
        dp, fsdp = lax.axis_index("dp"), lax.axis_index("fsdp")
        self.y, self.x = dp // PLANE, lax.rem(dp, PLANE)
        self.z, self.c = fsdp // CORES, lax.rem(fsdp, CORES)
        self.depth = depth
        y, x, z, c = self.y, self.x, self.z, self.c
        self.along_x = self.device(y, 1 - x, z, c)
        self.along_y = self.device(1 - y, x, z, c)
        self.other_core = self.device(y, x, z, 1 - c)
        self.ahead = [lax.rem(z + k, depth) for k in range(1, depth)]
        self.behind = [lax.rem(z + depth - k, depth) for k in range(1, depth)]

    def device(self, y, x, z, c):
        return (y * PLANE + x, z * CORES + c)

    def column(self, z):
        return self.device(self.y, self.x, z, self.c)

    def greet(self):
        partners = [self.column(q) for q in self.ahead]
        partners += [self.along_x, self.along_y, self.other_core]
        barrier = pltpu.get_barrier_semaphore()
        for partner in partners:
            pl.semaphore_signal(barrier, inc=1, device_id=partner, device_id_type=MESH)
        pl.semaphore_wait(barrier, len(partners))


class Mail:
    def __init__(self, send_sem, recv_sem):
        self.send_sem, self.recv_sem, self.sent = send_sem, recv_sem, {}

    def copy(self, unit, slot, source, target, device):
        return pltpu.make_async_remote_copy(
            src_ref=source,
            dst_ref=target,
            send_sem=self.send_sem.at[unit, slot],
            recv_sem=self.recv_sem.at[unit, slot],
            device_id=device,
            device_id_type=MESH,
        )

    def send(self, unit, slot, source, target, device):
        copy = self.copy(unit, slot, source, target, device)
        copy.start()
        self.sent[unit, slot] = copy

    def arrived(self, unit, slot, target, device):
        self.copy(unit, slot, target, target, device).wait_recv()

    def settle(self, unit, slot):
        self.sent.pop((unit, slot)).wait_send()

    def finish(self):
        for at in list(self.sent):
            self.settle(*at)


SLOTS = 14


def unit_list(shapes):
    units = []
    for index, (rows, columns) in enumerate(shapes):
        width = UNIT // rows
        units += [(index, first, width) for first in range(0, columns, width)]
    return units


def small_gather_phases(place, mail, unit, source, full, local_sem):
    y, x, z, c = place.y, place.x, place.z, place.c
    nz = place.depth - 1

    def first():
        pltpu.make_async_copy(source, full.at[y, x, z, c], local_sem).start()
        for k in range(nz):
            mail.send(unit, k, source, full.at[y, x, z, c], place.column(place.ahead[k]))

    def second():
        pltpu.make_async_copy(source, full.at[y, x, z, c], local_sem).wait()
        for k in range(nz):
            q = place.behind[k]
            mail.arrived(unit, k, full.at[y, x, q, c], place.column(q))
        mail.send(unit, 3, full.at[y, x, :, c], full.at[y, x, :, c], place.along_x)

    def third():
        mail.arrived(unit, 3, full.at[y, 1 - x, :, c], place.along_x)
        mail.send(unit, 5, full.at[y, :, :, c], full.at[y, :, :, c], place.along_y)

    def fourth():
        mail.arrived(unit, 5, full.at[1 - y, :, :, c], place.along_y)
        mail.send(unit, 7, full.at[:, :, :, c], full.at[:, :, :, c], place.other_core)

    def last():
        mail.arrived(unit, 7, full.at[:, :, :, 1 - c], place.other_core)

    return first, second, third, fourth, last


def by_rows(left, right):
    return contract(left, right, 1, 1)


def by_columns(left, right):
    return contract(left, right, 0, 0)


def plain(left, right):
    return jnp.dot(left, right, preferred_element_type=jnp.float32)


class Table:
    GAIN_ONE, SHIFT_ONE, QUERY, VALUE, OUT, GAIN_TWO, SHIFT_TWO, DOWN = range(8)

    def __init__(self, packed, narrow, wide):
        self.packed, self.narrow, self.wide = packed, narrow, wide

    def expand(self, devices):
        y_count, x_count, z_count, c_count = self.packed.shape[:4]

        def tile(d):
            d, c = divmod(d, c_count)
            d, z = divmod(d, z_count)
            y, x = divmod(d, x_count)
            return self.packed[y, x, z, c]

        group = lax.broadcasted_iota(jnp.int32, (8, 128), 1) // 32
        for base in range(0, devices, 4):
            tiles = [tile(base + i) for i in range(4)]
            for i in range(4):
                self.wide[:, pl.ds(128 * (base + i), 128)] = tiles[i][0:1, :]
            for q in range(4):
                mixed = jnp.zeros((8, 128), jnp.float32)
                for i in range(4):
                    turned = tiles[i] if i == q else pltpu.roll(tiles[i], 32 * ((i - q) % 4), 1)
                    mixed = jnp.where(group == i, turned, mixed)
                self.narrow[q, :, pl.ds(32 * base, 128)] = mixed

    def __getitem__(self, index):
        return self.narrow[index % 4, 1 + index // 4 : 2 + index // 4, :]


def row_facts(lengths, codes, row):
    begin = jnp.int32(0)
    segment = jnp.zeros(row.shape, jnp.int32)
    first = jnp.zeros(row.shape, jnp.int32)
    code = jnp.full(row.shape, codes[0, 0], jnp.int32)
    for item in range(1, lengths.shape[1]):
        begin = begin + lengths[0, item - 1]
        inside = row >= begin
        segment = jnp.where(inside, item, segment)
        first = jnp.where(inside, begin, first)
        code = jnp.where(inside, codes[0, item], code)
    return segment, (row - first).astype(jnp.float32) * (0.5 * (code.astype(jnp.float32) + 1.0))


def fill_mask(lengths, codes, mask):
    rows = mask.shape[0]
    across, _ = row_facts(lengths, codes, lax.broadcasted_iota(jnp.int32, (1, rows), 1))
    for base in range(0, rows, 128):
        down, _ = row_facts(lengths, codes, lax.broadcasted_iota(jnp.int32, (128, 1), 0) + base)
        mask[base : base + 128, :] = jnp.where(down == across, 0.0, -1e30)


def head_half(rows, which):
    lane = lax.broadcasted_iota(jnp.int32, (rows, 2 * HEAD_DIM), 1)
    return (lane >= HEAD_DIM) if which else (lane < HEAD_DIM)


def pair_span(pair, offset):
    return pl.ds(pl.multiple_of(offset + pair * 2 * HEAD_DIM, 2 * HEAD_DIM), 2 * HEAD_DIM)


def attend(first_pair, last_pair, projected, mask, attended):
    rows, width = attended.shape
    zero = jnp.zeros((), jnp.bfloat16)
    scale = jnp.asarray(1.0 / math.sqrt(HEAD_DIM), jnp.bfloat16)

    def one_pair(pair, carry):
        query = projected[:, pair_span(pair, 0)] * scale
        key = projected[:, pair_span(pair, width)]
        value = projected[:, pair_span(pair, 2 * width)]
        results = []
        for which in range(2):
            scores = by_rows(jnp.where(head_half(rows, which), query, zero), key) + mask[...]
            top = jnp.max(scores, axis=1, keepdims=True)
            expon = jnp.exp(scores - top)
            total = jnp.sum(expon, axis=1, keepdims=True)
            weights = (expon * (1.0 / total)).astype(jnp.bfloat16)
            results.append(plain(weights, value))
        mixed = jnp.where(head_half(rows, 0), results[0], results[1])
        attended[:, pair_span(pair, 0)] = mixed.astype(jnp.bfloat16)
        return carry

    lax.fori_loop(first_pair, last_pair, one_pair, 0)


CHUNK = 64


def over_rows(rows, step):
    def one(index, carry):
        step(pl.ds(pl.multiple_of(index * CHUNK, CHUNK), CHUNK), index * CHUNK)
        return carry

    lax.fori_loop(0, rows // CHUNK, one, 0)


def normalised(values):
    centred = values - jnp.mean(values, axis=-1, keepdims=True)
    variance = jnp.mean(centred * centred, axis=-1, keepdims=True)
    scale = lax.rsqrt(variance + EPSILON)
    return centred * scale, scale


def attend_back(first_pair, last_pair, projected, mask, grad_attended, sums, weights_low, grad_low):
    rows, width = grad_attended.shape
    zero = jnp.zeros((), jnp.bfloat16)
    scale = 1.0 / math.sqrt(HEAD_DIM)

    def one_pair(pair, carry):
        query, key, value = (projected[:, pair_span(pair, k * width)] for k in range(3))
        grad = grad_attended[:, pair_span(pair, 0)]
        scaled = query * jnp.asarray(scale, jnp.bfloat16)
        g_query, g_key, g_value = [], [], []
        for which in range(2):
            keep = head_half(rows, which)
            scores = by_rows(jnp.where(keep, key, zero), scaled) + mask[...]
            expon = jnp.exp(scores - jnp.max(scores, axis=0, keepdims=True))
            weights = expon * (1.0 / jnp.sum(expon, axis=0, keepdims=True))
            weights_low[which] = weights.astype(jnp.bfloat16)
            slopes = by_rows(jnp.where(keep, value, zero), grad)
            level = jnp.sum(weights * slopes, axis=0, keepdims=True)
            grad_low[which] = (weights * (slopes - level)).astype(jnp.bfloat16)
            g_value.append(plain(weights_low[which], grad))
            g_key.append(plain(grad_low[which], query))
            g_query.append(by_columns(grad_low[which], key))
        keep = head_half(rows, 0)
        for k, (parts, factor) in enumerate(((g_query, scale), (g_key, scale), (g_value, 1.0))):
            mixed = (jnp.where(keep, parts[0], parts[1]) * factor).astype(jnp.bfloat16)
            projected[:, pair_span(pair, k * width)] = mixed
            if k != 1:
                slot = Table.QUERY if k == 0 else Table.VALUE
                total = jnp.sum(mixed.astype(jnp.float32), axis=0, keepdims=True)
                sums[slot % 4, 1 + slot // 4 : 2 + slot // 4, pair_span(pair, 0)] = total
        return carry

    lax.fori_loop(first_pair, last_pair, one_pair, 0)


def gather_phases(place, mail, unit, kind, source, full, local_sem):
    y, x, z, c = place.y, place.x, place.z, place.c
    nz = place.depth - 1

    def begin():
        pltpu.make_async_copy(source, full(y, x, z, c, ALL), local_sem).start()
        for k in range(nz):
            mail.send(unit, k, source, full(y, x, z, c, ALL), place.column(place.ahead[k]))
        if kind:
            mail.send(unit, 3, source.at[0], full(y, x, z, c, 0), place.along_x)
            mail.send(unit, 4, source.at[1], full(y, x, z, c, 1), place.along_y)

    def second():
        pltpu.make_async_copy(source, full(y, x, z, c, ALL), local_sem).wait()
        if kind:
            for slot, partner, block in (
                (3, place.along_x, full(y, 1 - x, z, c, 0)),
                (4, place.along_y, full(1 - y, x, z, c, 1)),
            ):
                mail.arrived(unit, slot, block, partner)
                for k in range(nz):
                    mail.send(unit, 8 + 3 * (slot - 3) + k, block, block, place.column(place.ahead[k]))
            return
        for k in range(nz):
            q = place.behind[k]
            mail.arrived(unit, k, full(y, x, q, c, ALL), place.column(q))
        mail.send(unit, 3, full(y, x, ALL, c, 0), full(y, x, ALL, c, 0), place.along_x)
        mail.send(unit, 4, full(y, x, ALL, c, 1), full(y, x, ALL, c, 1), place.along_y)

    def third():
        if kind:
            for k in range(nz):
                q = place.behind[k]
                mail.arrived(unit, k, full(y, x, q, c, ALL), place.column(q))
            for k in range(nz):
                q = place.behind[k]
                mail.arrived(unit, 8 + k, full(y, 1 - x, q, c, 0), place.column(q))
        else:
            mail.arrived(unit, 3, full(y, 1 - x, ALL, c, 0), place.along_x)
        mail.send(unit, 5, full(y, ALL, ALL, c, 0), full(y, ALL, ALL, c, 0), place.along_y)
        if kind:
            for k in range(nz):
                q = place.behind[k]
                mail.arrived(unit, 11 + k, full(1 - y, x, q, c, 1), place.column(q))
        else:
            mail.arrived(unit, 4, full(1 - y, x, ALL, c, 1), place.along_y)
        mail.send(unit, 6, full(ALL, x, ALL, c, 1), full(ALL, x, ALL, c, 1), place.along_x)

    def fourth():
        mail.arrived(unit, 5, full(1 - y, ALL, ALL, c, 0), place.along_y)
        mail.arrived(unit, 6, full(ALL, 1 - x, ALL, c, 1), place.along_x)
        mail.send(unit, 7, full(ALL, ALL, ALL, c, ALL), full(ALL, ALL, ALL, c, ALL), place.other_core)

    def last():
        mail.arrived(unit, 7, full(ALL, ALL, ALL, 1 - c, ALL), place.other_core)

    return begin, second, third, fourth, last


class Sum:
    def __init__(self, place, mail, unit, kind, part, held, wide, late):
        self.place, self.mail, self.unit, self.kind = place, mail, unit, kind
        self.part, self.held, self.wide, self.late = part, held, wide, late
        self.nz = place.depth - 1

    def first(self):
        p = self.place
        self.mail.send(self.unit, 7, self.part.at[:, :, :, 1 - p.c], self.held, p.other_core)

    def second(self):
        p, mail, unit, held = self.place, self.mail, self.unit, self.held
        mail.arrived(unit, 7, held, p.other_core)
        for a in range(PLANE):
            for b in range(PLANE):
                held[a, b] = held[a, b] + self.part[a, b, :, p.c]
        mail.send(unit, 5, held.at[1 - p.y, :, :, 0], self.wide.at[0], p.along_y)
        mail.send(unit, 6, held.at[:, 1 - p.x, :, 1], self.wide.at[1], p.along_x)
        mail.settle(unit, 7)

    def pair(self, half, k):
        return self.late.at[pl.ds(2 * (self.nz * half + k), 2)]

    def near(self, half):
        depth = self.nz + 1
        return self.late.at[pl.ds(depth * half, depth)]

    def column(self, k):
        return self.late.at[pl.ds(2 * (self.nz + 1) + 2 * k, 2)]

    def final(self, half):
        return self.late.at[4 * self.nz + half]

    def third(self):
        p, mail, unit, held, wide = self.place, self.mail, self.unit, self.held, self.wide
        y, x = p.y, p.x
        mail.arrived(unit, 5, wide.at[0], p.along_y)
        for b in range(PLANE):
            held[y, b, :, 0] = held[y, b, :, 0] + wide[0, b]
        if self.kind:
            for k in range(self.nz):
                q = p.ahead[k]
                mail.send(unit, 8 + k, held.at[y, :, q, 0], self.pair(0, k), p.column(q))
        else:
            mail.send(unit, 3, held.at[y, 1 - x, :, 0], self.near(0), p.along_x)
        mail.arrived(unit, 6, wide.at[1], p.along_x)
        for b in range(PLANE):
            held[b, x, :, 1] = held[b, x, :, 1] + wide[1, b]
        if self.kind:
            for k in range(self.nz):
                q = p.ahead[k]
                mail.send(unit, 11 + k, held.at[:, x, q, 1], self.pair(1, k), p.column(q))
        else:
            mail.send(unit, 4, held.at[1 - y, x, :, 1], self.near(1), p.along_y)

    def fourth(self):
        p, mail, unit, held = self.place, self.mail, self.unit, self.held
        y, x, z = p.y, p.x, p.z
        full = jnp.float32
        if self.kind:
            for half in range(2):
                at = (y, ALL, z, 0) if half == 0 else (ALL, x, z, 1)
                total = held[at].astype(full)
                for k in range(self.nz):
                    mail.arrived(unit, 8 + 3 * half + k, self.pair(half, k), p.column(p.behind[k]))
                    total = total + self.pair(half, k)[...].astype(full)
                held[at] = total.astype(held.dtype)
            mail.send(unit, 3, held.at[y, 1 - x, z, 0], self.final(0), p.along_x)
            mail.send(unit, 4, held.at[1 - y, x, z, 1], self.final(1), p.along_y)
            return
        mail.arrived(unit, 3, self.near(0), p.along_x)
        mail.arrived(unit, 4, self.near(1), p.along_y)
        for half in range(2):
            held[y, x, :, half] = held[y, x, :, half] + self.near(half)[...]
        for k in range(self.nz):
            q = p.ahead[k]
            mail.send(unit, k, held.at[y, x, q], self.column(k), p.column(q))

    def last(self):
        p, mail, unit, held = self.place, self.mail, self.unit, self.held
        full = jnp.float32
        halves = [held[p.y, p.x, p.z, half].astype(full) for half in range(2)]
        if self.kind:
            mail.arrived(unit, 3, self.final(0), p.along_x)
            mail.arrived(unit, 4, self.final(1), p.along_y)
            halves = [v + self.final(half)[...].astype(full) for half, v in enumerate(halves)]
        else:
            for k in range(self.nz):
                mail.arrived(unit, k, self.column(k), p.column(p.behind[k]))
                halves = [v + self.column(k)[half].astype(full) for half, v in enumerate(halves)]
        for slot in [s for u, s in list(mail.sent) if u == unit]:
            mail.settle(unit, slot)
        return halves


INBOXES = 6
HELD = 4
TILE = 256
GATHER_KINDS = (0, 0, 0, 0, 0, 1, 0, 1, 0, 1, 0, 1)
SUM_KINDS = (0, 0, 0, 0, 0, 0, 0, 0, 0, 0, 0, 0)
AHEAD = 4
SUM_FROM = 14


def layer_kernel(depth, units, sums_units, *refs):
    refs = list(refs)

    def take(count):
        taken = refs[:count]
        del refs[:count]
        return taken

    sources = take(4)
    small, tokens, cotangent, lengths, codes = take(5)
    fulls = take(4)
    a_projected, a_attended, a_start = take(3)
    o_output, o_tokens = take(2)
    outs = take(4)
    (o_small,) = take(1)
    packed, narrow, wide = take(3)
    inbox, wide_in, late_in, r_square, r_tall, parts = take(6)
    s_part, s_core, s_wide, s_near, s_column, s_result = take(6)
    big, hidden_grad, square, tall, stream, grad_middle, grad_normed = take(7)
    normed, branch, grad_attended, finished, weights_low, grad_low, mask, sums, wide_sums = take(9)
    send_sem, recv_sem, local_sem, load_sem, store_sem, free_sem = take(6)

    place, mail = Place(depth), Mail(send_sem, recv_sem)
    y, x, z, c = place.y, place.x, place.z, place.c
    nz = depth - 1
    rows, width = stream.shape
    hidden = hidden_grad.shape[1]
    pairs = width // (2 * HEAD_DIM)
    low, full = jnp.bfloat16, jnp.float32
    table = Table(packed, narrow, wide)
    projected, attended = big.at[:, pl.ds(0, 3 * width)], big.at[:, pl.ds(3 * width, width)]
    corners = [(a, b) for a in range(PLANE) for b in range(PLANE)]
    stores, numbers = {}, iter(range(64))

    def store(name, source, target):
        copy = pltpu.make_async_copy(source, target, store_sem.at[len(stores)])
        copy.start()
        stores[name] = [copy, True]

    def stored(name):
        if stores[name][1]:
            stores[name][0].wait()
            stores[name][1] = False

    def load(source, target):
        return pltpu.make_async_copy(source, target, load_sem.at[next(numbers)])

    def flat(block):
        return block.reshape(-1, block.shape[-1])

    def piece(unit):
        index, first, columns = units[unit]
        span = pl.ds(first, columns)

        def view(*at):
            return fulls[index].at[at + (ALL, span)]

        return sources[index].at[:, :, span], view

    gathers = [
        gather_phases(place, mail, unit + 1, GATHER_KINDS[unit], *piece(unit), local_sem.at[unit + 1])
        for unit in range(len(units))
    ]
    small_gather = small_gather_phases(place, mail, 0, small, packed, local_sem.at[0])
    places = []
    for unit, (index, first, columns) in enumerate(units):
        buffer = tall if index == 3 else square
        places.append((buffer, sum((u[0] == 3) == (index == 3) for u in units[:unit]) % 2))
    loads = [
        load(piece(unit)[1](ALL, ALL, ALL, ALL, ALL), buffer.at[at])
        for unit, (buffer, at) in enumerate(places)
    ]

    def weights(unit, columns):
        buffer, at = places[unit]
        return flat(buffer[at, :, :, :, :, :, :, columns])

    def corner_loads(index, corner, buffer, at):
        a, b = corners[corner]
        chosen = [u for u in units if u[0] == index]
        return [
            load(
                fulls[index].at[a, b, :, :, :, :, pl.ds(first, columns)],
                buffer.at[at, e // PLANE, e % PLANE],
            )
            for e, (_, first, columns) in enumerate(chosen)
        ]

    get_down = [corner_loads(3, n, tall, n % 2) for n in range(4)]
    get_up = [corner_loads(2, n, square, n % 2) for n in range(4)]
    get_out = [
        load(fulls[1].at[a, b], square.at[0, n // PLANE, n % PLANE]) for n, (a, b) in enumerate(corners)
    ]
    get_qkv = [corner_loads(0, n, square, (n + 1) % 2) for n in range(4)]
    get_projected = load(a_projected, projected)
    get_attended = load(a_attended, attended)
    get_start = load(a_start, stream)

    def start_all(copies):
        for copy in copies:
            copy.start()

    def wait_all(copies):
        for copy in copies:
            copy.wait()

    def prepare():
        def chunk(span, base):
            row = lax.broadcasted_iota(jnp.int32, (CHUNK, 1), 0) + base
            _, factor = row_facts(lengths, codes, row)
            lane = lax.broadcasted_iota(jnp.int32, (1, width // 2), 1).astype(full)
            phase = factor * jnp.exp(lane * (-math.log(10000.0) / (width // 2)))
            left, right = pl.ds(0, width // 2), pl.ds(width // 2, width // 2)
            stream[span, left] = tokens[span, left].astype(full) + jnp.sin(phase)
            stream[span, right] = tokens[span, right].astype(full) + jnp.cos(phase)

        over_rows(rows, chunk)
        store("start", stream, a_start)
        fill_mask(lengths, codes, mask)
        sums[...] = jnp.zeros_like(sums)

    def norm(gain, shift):
        def chunk(span, base):
            normed[span, :] = (normalised(stream[span, :])[0] * table[gain] + table[shift]).astype(low)

        over_rows(rows, chunk)

    def project(unit, bias):
        tile = 512
        for first in range(0, width, tile):
            value = plain(normed[...], weights(unit, pl.ds(first, tile)))
            if bias is not None:
                value = value + table[bias][:, first : first + tile]
            big[:, pl.ds(unit * width + first, tile)] = value.astype(low)

    def project_out(unit):
        tile = 512
        stored("start")
        for first in range(0, width, tile):
            span = pl.ds(first, tile)
            value = plain(attended[...], weights(unit, span)) + table[Table.OUT][:, first : first + tile]
            stream[:, span] = stream[:, span] + value

    def rise(unit, number):
        def one(index, carry):
            at = pl.multiple_of(index * TILE, TILE)
            there = pl.ds(pl.multiple_of(number * width + at, TILE), TILE)
            pre = plain(normed[...], weights(unit, pl.ds(at, TILE))) + wide[:, there]
            normal = 0.5 * (1.0 + lax.erf(pre * math.sqrt(0.5)))
            density = jnp.exp(pre * pre * -0.5) * (1.0 / math.sqrt(2.0 * math.pi))
            big[:, there] = (pre * normal).astype(low)
            hidden_grad[:, there] = (normal + pre * density).astype(low)
            return carry

        lax.fori_loop(0, width // TILE, one, 0)

    def fall(unit, number, columns):
        span = pl.ds(number * columns, columns)
        value = plain(big[...], weights(unit, ALL)) + table[Table.DOWN][:, number * columns : (number + 1) * columns]
        finished[:, span] = (stream[:, span] + value).astype(low)

    def tally(slot, values):
        at = (slot % 4, pl.ds(1 + slot // 4, 1), ALL)
        sums[at] = sums[at] + jnp.sum(values, axis=0, keepdims=True)

    def square_part(unit, left, right, first):
        for k in range(width // TILE):
            value = by_columns(left[...], right[:, pl.ds(first + TILE * k, TILE)]).astype(low)
            parts[unit % HELD, :, :, :, :, :, k] = value.reshape(parts.shape[1:6] + (parts.shape[7], TILE))

    def tall_part(unit, first):
        def one(corner, carry):
            left = big[:, pl.ds(pl.multiple_of(corner * width, width), width)]
            value = by_columns(left, cotangent[:, pl.ds(first, TILE)]).astype(low)
            parts[unit % HELD, corner // PLANE, lax.rem(corner, PLANE)] = value.reshape(parts.shape[3:])
            return carry

        lax.fori_loop(0, PLANE * PLANE, one, 0)

    def part_of(unit):
        index, first, columns = sums_units[unit]
        if index == 3:
            tall_part(unit, first)
        elif index == 2:
            square_part(unit, normed, hidden_grad, first)
        elif index == 1:
            square_part(unit, attended, branch, 0)
        else:
            square_part(unit, normed, big, first)

    def hidden_step(n):
        wait_all(get_down[n])

        def one(m, carry):
            block = jnp.concatenate(
                [flat(tall[n % 2, e // PLANE, e % PLANE, m]) for e in range(4)], axis=1
            )
            span = pl.ds(pl.multiple_of(n * width + m * TILE, TILE), TILE)
            value = (by_rows(cotangent[...], block) * hidden_grad[:, span].astype(full)).astype(low)
            hidden_grad[:, span] = value
            wide_sums[:, span] = jnp.sum(value.astype(full), axis=0, keepdims=True)
            return carry

        lax.fori_loop(0, width // TILE, one, 0)
        if n + 2 < 4:
            start_all(get_down[n + 2])

    def back_through(copies, left, at, n):
        wait_all(copies)
        total = None
        for e in range(len(copies)):
            value = by_rows(left[:, pl.ds(e * width, width)], flat(square[at, e // PLANE, e % PLANE]))
            total = value if total is None else total + value
        grad_normed[:, pl.ds(TILE * n, TILE)] = total

    def up_step(n):
        back_through(get_up[n], hidden_grad, n % 2, n)
        if n + 2 < 4:
            start_all(get_up[n + 2])
        if n == 2:
            start_all(get_out)
        if n == 3:
            start_all(get_qkv[0])

    def out_step():
        wait_all(get_out)
        for n in range(4):
            block = flat(square[0, n // PLANE, n % PLANE])
            grad_attended[:, pl.ds(TILE * n, TILE)] = by_rows(branch[...], block).astype(low)
        start_all(get_qkv[1])

    def qkv_step(n):
        back_through(get_qkv[n], big, (n + 1) % 2, n)
        if n + 2 < 4:
            start_all(get_qkv[n + 2])

    def norm_back(span, gain, shift):
        level, scale = normalised(stream[span, :])
        grad = grad_normed[span, :]
        tally(gain, grad * level)
        tally(shift, grad)
        grad = grad * table[gain]
        mean = jnp.mean(grad, axis=-1, keepdims=True)
        along = jnp.mean(grad * level, axis=-1, keepdims=True)
        return scale * (grad - mean - level * along)

    def second_norm_back():
        def chunk(span, base):
            value = cotangent[span, :].astype(full) + norm_back(span, Table.GAIN_TWO, Table.SHIFT_TWO)
            grad_middle[span, :] = value
            branch[span, :] = value.astype(low)
            tally(Table.OUT, value.astype(low).astype(full))
            tally(Table.DOWN, cotangent[span, :].astype(full))

        over_rows(rows, chunk)

    def first_norm_back():
        stored("output")

        def chunk(span, base):
            value = grad_middle[span, :] + norm_back(span, Table.GAIN_ONE, Table.SHIFT_ONE)
            finished[span, :] = value.astype(low)

        over_rows(rows, chunk)
        store("tokens", finished, o_tokens)

    def attention_back(first, last):
        attend_back(first, last, big, mask, grad_attended, sums, weights_low, grad_low)

    def pack():
        group = lax.broadcasted_iota(jnp.int32, (8, 128), 1) // 32
        line = lax.broadcasted_iota(jnp.int32, (8, 128), 0)
        shape = s_part.shape[:4]
        for device in range(math.prod(shape)):
            i, base = device % 4, 32 * (device - device % 4)
            mixed = jnp.zeros((8, 128), full)
            for q in range(4):
                tile = sums[q, :, pl.ds(base, 128)]
                turned = tile if i == q else pltpu.roll(tile, 32 * ((q - i) % 4), 1)
                mixed = jnp.where(group == q, turned, mixed)
            share = jnp.broadcast_to(wide_sums[:, pl.ds(128 * device, 128)], (8, 128))
            at, k = divmod(device, shape[3])
            at, m = divmod(at, shape[2])
            s_part[at // shape[1], at % shape[1], m, k] = jnp.where(line == 0, share, mixed)

    base = len(units) + 1

    def unit_steps(unit):
        index, start, columns = sums_units[unit]
        piece = Sum(
            place, mail, base + unit, SUM_KINDS[unit],
            parts.at[unit % HELD], inbox.at[unit % INBOXES], wide_in.at[unit], late_in.at[unit],
        )

        def first():
            if unit >= INBOXES:
                pl.semaphore_wait(free_sem.at[unit], 1)
            piece.first()

        def last():
            halves = piece.last()
            if index == 3:
                final = r_tall.at[unit]
                for half, value in enumerate(halves):
                    final[half] = value
                store(f"part {unit}", final, outs[index].at[:, :, :, pl.ds(start, columns)])
            else:
                final = r_square.at[unit - 4]
                for half, value in enumerate(halves):
                    for k in range(value.shape[0]):
                        final[half, :, pl.ds(TILE * k, TILE)] = value[k]
                store(f"part {unit}", final, outs[index].at[:, :, pl.ds(start, columns)])
            if unit + INBOXES < len(sums_units):
                pl.semaphore_signal(
                    free_sem.at[unit + INBOXES], inc=1, device_id=place.other_core, device_id_type=MESH
                )

        return first, piece.second, piece.third, piece.fourth, last

    def small_steps():
        unit = base + len(sums_units)
        held = s_core

        def first():
            mail.send(unit, 7, s_part.at[:, :, :, 1 - c], held, place.other_core)

        def second():
            mail.arrived(unit, 7, held, place.other_core)
            for a, b in corners:
                held[a, b] = held[a, b] + s_part[a, b, :, c]
            mail.send(unit, 5, held.at[1 - y], s_wide, place.along_y)

        def third():
            mail.arrived(unit, 5, s_wide, place.along_y)
            held[y] = held[y] + s_wide[...]
            mail.send(unit, 3, held.at[y, 1 - x], s_near, place.along_x)

        def fourth():
            mail.arrived(unit, 3, s_near, place.along_x)
            held[y, x] = held[y, x] + s_near[...]
            for k in range(nz):
                q = place.ahead[k]
                mail.send(unit, k, held.at[y, x, q], s_column.at[k], place.column(q))

        def last():
            total = held[y, x, z]
            for k in range(nz):
                mail.arrived(unit, k, s_column.at[k], place.column(place.behind[k]))
                total = total + s_column[k]
            s_result[...] = total
            store("small", s_result, o_small)

        return first, second, third, fourth, last

    scatters = [unit_steps(unit) for unit in range(len(sums_units))] + [small_steps()]

    def compute(turn):
        unit = turn - AHEAD
        if turn == 0:
            prepare()
        if unit == 0:
            table.expand(PLANE * PLANE * depth * CORES)
            norm(Table.GAIN_ONE, Table.SHIFT_ONE)
        if unit == 3:
            attend(pairs // 2, pairs, projected, mask, attended)
            store("attended", attended, a_attended)
        if 0 <= unit < len(units):
            loads[unit].wait()
            index, first, columns = units[unit]
            if index == 0:
                project(unit, (Table.QUERY, None, Table.VALUE)[unit])
                if unit == 2:
                    store("projected", projected, a_projected)
                    attend(0, pairs // 2, projected, mask, attended)
            elif index == 1:
                project_out(unit)
                norm(Table.GAIN_TWO, Table.SHIFT_TWO)
                stored("projected")
                stored("attended")
            elif index == 2:
                rise(unit, first // columns)
                if unit == 7:
                    start_all(get_up[0])
            else:
                if unit == 8:
                    start_all(get_up[1])
                if unit == 11:
                    start_all(get_down[0])
                fall(unit, first // columns, columns)
                if unit == 11:
                    store("output", finished, o_output)
                    start_all(get_down[1])
        if turn == 15:
            hidden_step(0)
            hidden_step(1)
        elif turn == 16:
            hidden_step(2)
            hidden_step(3)
            up_step(0)
        elif turn == 17:
            start_all((get_projected, get_attended))
            for n in range(1, 4):
                up_step(n)
            second_norm_back()
            get_start.start()
        elif turn == 18:
            out_step()
            get_projected.wait()
            attention_back(0, 2)
        elif turn == 19:
            attention_back(2, 4)
        elif turn == 20:
            attention_back(4, 6)
            get_attended.wait()
        elif turn == 21:
            attention_back(6, 8)
            get_start.wait()
            norm(Table.GAIN_ONE, Table.SHIFT_ONE)
        elif turn == 22:
            qkv_step(0)
        elif turn == 23:
            qkv_step(1)
            qkv_step(2)
        elif turn == 24:
            qkv_step(3)
            first_norm_back()
            pack()

    place.greet()
    total = len(scatters)
    for turn in range(SUM_FROM + total + 3):
        for phase in range(5):
            unit = turn - phase
            if unit == 0:
                small_gather[phase]()
            if 0 <= unit < len(units):
                gathers[unit][phase]()
                if phase == AHEAD:
                    loads[unit].start()
        unit = turn - SUM_FROM
        if 0 <= unit < total:
            if unit < len(sums_units):
                part_of(unit)
            scatters[unit][0]()
        compute(turn)
        for phase in range(1, 5):
            unit = turn - SUM_FROM - phase + 1
            if 0 <= unit < total:
                scatters[unit][phase]()
    for name in list(stores):
        stored(name)
    mail.finish()


def run_layer(mesh, tokens, cotangent, lengths, codes, matrices, vectors):
    depth = mesh.shape["fsdp"] // CORES
    grid = (PLANE, PLANE, depth, CORES)
    plane = (PLANE, PLANE, depth)
    rows, width = tokens.shape
    hidden = matrices[2].shape[1]
    devices = mesh.size
    low, full = jnp.bfloat16, jnp.float32
    halves = [m.reshape(2, m.shape[0] // 2, m.shape[1]) for m in matrices]
    units = unit_list([(m.shape[0] * devices, m.shape[1]) for m in matrices])
    sums_units = [u for index in (3, 2, 1, 0) for u in units if u[0] == index]
    flat = jnp.concatenate([vectors[-1], *vectors[:-1]]).astype(full)
    small = jnp.pad(flat, (0, 1024 - flat.size)).reshape(8, 128)
    count = len(units)
    talls = sum(u[0] == 3 for u in units)
    share = width // devices // 2
    block = (2, width // TILE, share, TILE)
    inner = block[1:]

    def shaped(*shape, dtype=low):
        return jax.ShapeDtypeStruct(shape, dtype)

    anywhere = pl.BlockSpec(memory_space=pl.ANY)
    vmem = pl.BlockSpec(memory_space=pltpu.VMEM)
    smem = pl.BlockSpec(memory_space=pltpu.SMEM)
    out_shape = [shaped(*grid, *h.shape) for h in halves]
    out_shape += [shaped(rows, 3 * width), shaped(rows, width), shaped(rows, width, dtype=full)]
    out_shape += [shaped(rows, width), shaped(rows, width)]
    out_shape += [shaped(2, share, m.shape[1], dtype=full) for m in matrices[:3]]
    out_shape += [shaped(2, hidden // width, share, width, dtype=full), shaped(8, 128, dtype=full)]
    scratch = [
        ((*grid, 8, 128), full),
        ((4, 8, width), full),
        ((1, hidden), full),
        ((INBOXES, *plane, *block), low),
        ((count, 2, PLANE, depth, *inner), low),
        ((count, 4 * depth - 2, *inner), low),
        ((count - talls, 2, share, width), full),
        ((talls, *block), full),
        ((HELD, *grid, *block), low),
        ((*grid, 8, 128), full),
        ((*plane, 8, 128), full),
        ((PLANE, depth, 8, 128), full),
        ((depth, 8, 128), full),
        ((depth - 1, 8, 128), full),
        ((8, 128), full),
        ((rows, hidden), low),
        ((rows, hidden), low),
        ((2, *grid, 2, share, width), low),
        ((2, *grid, 2, share * (hidden // width), TILE), low),
        ((rows, width), full),
        ((rows, width), full),
        ((rows, width), full),
        ((rows, width), low),
        ((rows, width), low),
        ((rows, width), low),
        ((rows, width), low),
        ((2, rows, rows), low),
        ((2, rows, rows), low),
        ((rows, rows), full),
        ((4, 8, width), full),
        ((1, hidden), full),
    ]
    outs = pl.pallas_call(
        functools.partial(layer_kernel, depth, units, sums_units),
        out_shape=out_shape,
        in_specs=[anywhere] * 5 + [vmem, vmem, smem, smem],
        out_specs=[anywhere] * len(out_shape),
        scratch_shapes=[pltpu.VMEM(shape, dtype) for shape, dtype in scratch]
        + [
            pltpu.SemaphoreType.DMA((2 * count + 2, SLOTS)),
            pltpu.SemaphoreType.DMA((2 * count + 2, SLOTS)),
            pltpu.SemaphoreType.DMA((count + 1,)),
            pltpu.SemaphoreType.DMA((64,)),
            pltpu.SemaphoreType.DMA((24,)),
            pltpu.SemaphoreType.REGULAR((count,)),
        ],
        compiler_params=pltpu.CompilerParams(
            collective_id=0, has_side_effects=True, vmem_limit_bytes=62 << 20
        ),
    )(*halves, small, tokens, cotangent, lengths, codes)
    output, grad_tokens = outs[7:9]
    grads = [o.reshape(-1, o.shape[-1]) for o in outs[9:13]]
    spread = outs[13].reshape(-1)
    wide, narrow = hidden // devices, width // devices
    return output, grad_tokens, grads, [spread[wide + narrow * k : wide + narrow * (k + 1)] for k in range(8)], spread[:wide]


def grid_body(mesh, tokens, cotangent, lengths, scale_codes, *params):
    matrices = params[:4]
    (gain_one, shift_one, bias_query, bias_value, bias_out, gain_two, shift_two, bias_up, bias_down) = params[4:]
    vectors = (gain_one, shift_one, bias_query, bias_value, bias_out, gain_two, shift_two, bias_down, bias_up)
    output, grad_tokens, grads, small, grad_up_bias = run_layer(
        mesh, tokens, cotangent, lengths, scale_codes, matrices, vectors
    )
    return (output, grad_tokens, *grads, *small[:7], grad_up_bias, small[7])


def solution(mesh):
    placed = (
        P(("dp", "fsdp"), None),
        P(("dp", "fsdp"), None),
        P(("dp", "fsdp"), None),
        P(("dp", "fsdp"), None),
        P(("dp", "fsdp"), None),
        P(("dp", "fsdp"), None),
        P(("dp", "fsdp"), None),
        P(("dp", "fsdp"), None),
        P(("dp", "fsdp")),
        P(("dp", "fsdp")),
        P(("dp", "fsdp")),
        P(("dp", "fsdp")),
        P(("dp", "fsdp")),
        P(("dp", "fsdp")),
        P(("dp", "fsdp")),
        P(("dp", "fsdp")),
        P(("dp", "fsdp")),
    )
    per_device = body
    if mesh.shape["dp"] == PLANE * PLANE and mesh.shape["fsdp"] == 4 * CORES:
        per_device = functools.partial(grid_body, mesh)
    return jax.shard_map(
        per_device,
        mesh=mesh,
        in_specs=placed,
        out_specs=(
            P(("dp", "fsdp"), None),
            P(("dp", "fsdp"), None),
            P(("dp", "fsdp"), None),
            P(("dp", "fsdp"), None),
            P(("dp", "fsdp"), None),
            P(("dp", "fsdp"), None),
            P(("dp", "fsdp")),
            P(("dp", "fsdp")),
            P(("dp", "fsdp")),
            P(("dp", "fsdp")),
            P(("dp", "fsdp")),
            P(("dp", "fsdp")),
            P(("dp", "fsdp")),
            P(("dp", "fsdp")),
            P(("dp", "fsdp")),
        ),
        check_vma=False,
    )
```

```python
import functools
import math

import jax
import jax.numpy as jnp
from jax import lax
from jax.experimental import pallas as pl
from jax.experimental.pallas import tpu as pltpu
from jax.sharding import PartitionSpec as P

HEADS = 16
HEAD_DIM = 64


EPSILON = 1e-06


def contract(left, right, left_dim, right_dim):
    return lax.dot_general(
        left, right, (((left_dim,), (right_dim,)), ((), ())), preferred_element_type=jnp.float32
    )


def layer_norm(values, gain, shift):
    centred = values - jnp.mean(values, axis=-1, keepdims=True)
    variance = jnp.mean(centred * centred, axis=-1, keepdims=True)
    return centred * lax.rsqrt(variance + EPSILON) * gain + shift


def gelu_exact(values):
    return jax.nn.gelu(values, approximate=False)


def row_tables(length_row, code_row, row_count, feat_width):
    items = jnp.arange(length_row.shape[0], dtype=jnp.int32)
    item_starts = jnp.sum(
        jnp.where(items[None, :] < items[:, None], length_row[None, :], 0), axis=1
    )
    item_ends = item_starts + length_row
    row_index = jnp.arange(row_count, dtype=jnp.int32)
    member = (
        (row_index[:, None] >= item_starts[None, :]) & (row_index[:, None] < item_ends[None, :])
    ).astype(jnp.int32)
    item_ids = jnp.arange(length_row.shape[0], dtype=jnp.int32)
    segment = jnp.sum(member * item_ids[None, :], axis=1)
    place = row_index - jnp.sum(member * item_starts[None, :], axis=1)
    row_code = jnp.sum(member * code_row[None, :], axis=1)
    half_width = feat_width // 2
    frequency = jnp.exp(
        jnp.arange(half_width, dtype=jnp.float32) * (-math.log(10000.0) / half_width)
    )
    gsd_ratio = 0.5 * (row_code.astype(jnp.float32) + 1.0)
    phase_angle = (place.astype(jnp.float32) * gsd_ratio)[:, None] * frequency[None, :]
    return (segment, jnp.concatenate([jnp.sin(phase_angle), jnp.cos(phase_angle)], axis=1))


def body(
    tokens,
    cotangent,
    lengths,
    scale_codes,
    w_qkv,
    w_out,
    w_up,
    w_down,
    ln1_gain,
    ln1_shift,
    bias_query,
    bias_value,
    bias_out,
    ln2_gain,
    ln2_shift,
    bias_up,
    bias_down,
):
    gathered = (
        lax.all_gather(w_qkv, ("dp", "fsdp"), axis=0, tiled=True),
        lax.all_gather(w_out, ("dp", "fsdp"), axis=0, tiled=True),
        lax.all_gather(w_up, ("dp", "fsdp"), axis=0, tiled=True),
        lax.all_gather(w_down, ("dp", "fsdp"), axis=0, tiled=True),
        lax.all_gather(ln1_gain, ("dp", "fsdp"), axis=0, tiled=True),
        lax.all_gather(ln1_shift, ("dp", "fsdp"), axis=0, tiled=True),
        lax.all_gather(bias_query, ("dp", "fsdp"), axis=0, tiled=True),
        lax.all_gather(bias_value, ("dp", "fsdp"), axis=0, tiled=True),
        lax.all_gather(bias_out, ("dp", "fsdp"), axis=0, tiled=True),
        lax.all_gather(ln2_gain, ("dp", "fsdp"), axis=0, tiled=True),
        lax.all_gather(ln2_shift, ("dp", "fsdp"), axis=0, tiled=True),
        lax.all_gather(bias_up, ("dp", "fsdp"), axis=0, tiled=True),
        lax.all_gather(bias_down, ("dp", "fsdp"), axis=0, tiled=True),
    )
    (
        full_qkv,
        full_out,
        full_up,
        full_down,
        gain_first,
        shift_first,
        query_bias,
        value_bias,
        out_bias,
        gain_second,
        shift_second,
        up_bias,
        down_bias,
    ) = gathered
    gain_one = gain_first.astype(jnp.float32)
    shift_one = shift_first.astype(jnp.float32)
    gain_two = gain_second.astype(jnp.float32)
    shift_two = shift_second.astype(jnp.float32)
    row_count, model_width = tokens.shape
    head_width = model_width // HEADS
    score_scale = 1.0 / math.sqrt(HEAD_DIM)
    segment, encoding = row_tables(lengths[0], scale_codes[0], row_count, model_width)
    same_item = segment[:, None] == segment[None, :]
    start = tokens.astype(jnp.float32) + encoding
    normed_one = layer_norm(start, gain_one, shift_one).astype(jnp.bfloat16)
    qkv_bias = jnp.concatenate([query_bias, jnp.zeros_like(query_bias), value_bias]).astype(
        jnp.float32
    )
    projected = (
        jnp.dot(normed_one, full_qkv, preferred_element_type=jnp.float32) + qkv_bias
    ).astype(jnp.bfloat16)

    def split_heads(block):
        return block.reshape(row_count, HEADS, head_width).transpose(1, 0, 2)

    def join_heads(block):
        return block.transpose(1, 0, 2).reshape(row_count, model_width)

    query_heads = split_heads(projected[:, :model_width])
    key_heads = split_heads(projected[:, model_width : 2 * model_width])
    value_heads = split_heads(projected[:, 2 * model_width :])

    def forward_head(operands):
        query_head, key_head, value_head = operands
        scores = contract(query_head, key_head, 1, 1) * score_scale
        scores = jnp.where(same_item, scores, -1e30)
        top_score = jnp.max(scores, axis=1, keepdims=True)
        expon = jnp.exp(scores - top_score)
        total = jnp.sum(expon, axis=1, keepdims=True)
        weights_low = (expon / total).astype(jnp.bfloat16)
        result = jnp.dot(weights_low, value_head, preferred_element_type=jnp.float32)
        return (result, (top_score + jnp.log(total))[:, 0])

    attended_heads, log_totals = lax.map(forward_head, (query_heads, key_heads, value_heads))
    attended = join_heads(attended_heads).astype(jnp.bfloat16)
    middle = (
        start
        + jnp.dot(attended, full_out, preferred_element_type=jnp.float32)
        + out_bias.astype(jnp.float32)
    )
    normed_two = layer_norm(middle, gain_two, shift_two).astype(jnp.bfloat16)
    hidden_pre = jnp.dot(normed_two, full_up, preferred_element_type=jnp.float32) + up_bias.astype(
        jnp.float32
    )
    activated = gelu_exact(hidden_pre).astype(jnp.bfloat16)
    feed_out = jnp.dot(activated, full_down, preferred_element_type=jnp.float32) + down_bias.astype(
        jnp.float32
    )
    output = (middle + feed_out).astype(jnp.bfloat16)
    back_qkv, back_out, back_up, back_down = (
        lax.all_gather(w_qkv, ("dp", "fsdp"), axis=0, tiled=True),
        lax.all_gather(w_out, ("dp", "fsdp"), axis=0, tiled=True),
        lax.all_gather(w_up, ("dp", "fsdp"), axis=0, tiled=True),
        lax.all_gather(w_down, ("dp", "fsdp"), axis=0, tiled=True),
    )
    grad_output = cotangent.astype(jnp.float32)
    grad_down_bias = jnp.sum(grad_output, axis=0)
    grad_down = contract(activated, cotangent, 0, 0)
    grad_act = contract(cotangent, back_down, 1, 1)
    gelu_value, gelu_pull = jax.vjp(gelu_exact, hidden_pre)
    grad_hidden = gelu_pull(grad_act)[0].astype(jnp.bfloat16)
    grad_up_bias = jnp.sum(grad_hidden.astype(jnp.float32), axis=0)
    grad_up = contract(normed_two, grad_hidden, 0, 0)
    grad_normed_two = contract(grad_hidden, back_up, 1, 1)
    norm_value, second_pull = jax.vjp(layer_norm, middle, gain_two, shift_two)
    grad_middle_part, grad_gain_two, grad_shift_two = second_pull(grad_normed_two)
    grad_middle = grad_output + grad_middle_part
    branch_grad = grad_middle.astype(jnp.bfloat16)
    grad_out_bias = jnp.sum(branch_grad.astype(jnp.float32), axis=0)
    grad_out_weight = contract(attended, branch_grad, 0, 0)
    grad_attended = contract(branch_grad, back_out, 1, 1).astype(jnp.bfloat16)
    grad_heads = split_heads(grad_attended)

    def backward_head(operands):
        query_head, key_head, value_head, grad_head, log_total = operands
        scores = contract(query_head, key_head, 1, 1) * score_scale
        weights = jnp.where(same_item, jnp.exp(scores - log_total[:, None]), 0.0)
        weights_low = weights.astype(jnp.bfloat16)
        grad_weights = contract(grad_head, value_head, 1, 1)
        grad_value = contract(weights_low, grad_head, 0, 0)
        grad_scores = weights * (
            grad_weights - jnp.sum(weights * grad_weights, axis=1, keepdims=True)
        )
        grad_scores_low = grad_scores.astype(jnp.bfloat16)
        grad_query = (
            jnp.dot(grad_scores_low, key_head, preferred_element_type=jnp.float32) * score_scale
        )
        grad_key = contract(grad_scores_low, query_head, 0, 0) * score_scale
        return (grad_query, grad_key, grad_value)

    grad_query_heads, grad_key_heads, grad_value_heads = lax.map(
        backward_head, (query_heads, key_heads, value_heads, grad_heads, log_totals)
    )
    grad_projected = jnp.concatenate(
        [join_heads(grad_query_heads), join_heads(grad_key_heads), join_heads(grad_value_heads)],
        axis=1,
    ).astype(jnp.bfloat16)
    grad_query_bias = jnp.sum(grad_projected[:, :model_width].astype(jnp.float32), axis=0)
    grad_value_bias = jnp.sum(grad_projected[:, 2 * model_width :].astype(jnp.float32), axis=0)
    grad_qkv = contract(normed_one, grad_projected, 0, 0)
    grad_normed_one = contract(grad_projected, back_qkv, 1, 1)
    first_value, first_pull = jax.vjp(layer_norm, start, gain_one, shift_one)
    grad_start_part, grad_gain_one, grad_shift_one = first_pull(grad_normed_one)
    grad_tokens = (grad_middle + grad_start_part).astype(jnp.bfloat16)
    every_grad = (
        lax.psum_scatter(grad_qkv, ("dp", "fsdp"), scatter_dimension=0, tiled=True),
        lax.psum_scatter(grad_out_weight, ("dp", "fsdp"), scatter_dimension=0, tiled=True),
        lax.psum_scatter(grad_up, ("dp", "fsdp"), scatter_dimension=0, tiled=True),
        lax.psum_scatter(grad_down, ("dp", "fsdp"), scatter_dimension=0, tiled=True),
        lax.psum_scatter(grad_gain_one, ("dp", "fsdp"), scatter_dimension=0, tiled=True),
        lax.psum_scatter(grad_shift_one, ("dp", "fsdp"), scatter_dimension=0, tiled=True),
        lax.psum_scatter(grad_query_bias, ("dp", "fsdp"), scatter_dimension=0, tiled=True),
        lax.psum_scatter(grad_value_bias, ("dp", "fsdp"), scatter_dimension=0, tiled=True),
        lax.psum_scatter(grad_out_bias, ("dp", "fsdp"), scatter_dimension=0, tiled=True),
        lax.psum_scatter(grad_gain_two, ("dp", "fsdp"), scatter_dimension=0, tiled=True),
        lax.psum_scatter(grad_shift_two, ("dp", "fsdp"), scatter_dimension=0, tiled=True),
        lax.psum_scatter(grad_up_bias, ("dp", "fsdp"), scatter_dimension=0, tiled=True),
        lax.psum_scatter(grad_down_bias, ("dp", "fsdp"), scatter_dimension=0, tiled=True),
    )
    (
        shard_qkv,
        shard_out,
        shard_up,
        shard_down,
        shard_gain_one,
        shard_shift_one,
        shard_query_bias,
        shard_value_bias,
        shard_out_bias,
        shard_gain_two,
        shard_shift_two,
        shard_up_bias,
        shard_down_bias,
    ) = every_grad
    return (
        output,
        grad_tokens,
        shard_qkv,
        shard_out,
        shard_up,
        shard_down,
        shard_gain_one,
        shard_shift_one,
        shard_query_bias,
        shard_value_bias,
        shard_out_bias,
        shard_gain_two,
        shard_shift_two,
        shard_up_bias,
        shard_down_bias,
    )


PLANE = 2
CORES = 2
UNIT = 1024 * 1024
MESH = pl.DeviceIdType.MESH
ALL = slice(None)


class Place:
    def __init__(self, depth):
        dp, fsdp = lax.axis_index("dp"), lax.axis_index("fsdp")
        self.y, self.x = dp // PLANE, lax.rem(dp, PLANE)
        self.z, self.c = fsdp // CORES, lax.rem(fsdp, CORES)
        self.depth = depth
        y, x, z, c = self.y, self.x, self.z, self.c
        self.along_x = self.device(y, 1 - x, z, c)
        self.along_y = self.device(1 - y, x, z, c)
        self.other_core = self.device(y, x, z, 1 - c)
        self.ahead = [lax.rem(z + k, depth) for k in range(1, depth)]
        self.behind = [lax.rem(z + depth - k, depth) for k in range(1, depth)]

    def device(self, y, x, z, c):
        return (y * PLANE + x, z * CORES + c)

    def column(self, z):
        return self.device(self.y, self.x, z, self.c)

    def greet(self):
        partners = [self.column(q) for q in self.ahead]
        partners += [self.along_x, self.along_y, self.other_core]
        barrier = pltpu.get_barrier_semaphore()
        for partner in partners:
            pl.semaphore_signal(barrier, inc=1, device_id=partner, device_id_type=MESH)
        pl.semaphore_wait(barrier, len(partners))


class Mail:
    def __init__(self, send_sem, recv_sem):
        self.send_sem, self.recv_sem, self.sent = send_sem, recv_sem, {}

    def copy(self, unit, slot, source, target, device):
        return pltpu.make_async_remote_copy(
            src_ref=source,
            dst_ref=target,
            send_sem=self.send_sem.at[unit, slot],
            recv_sem=self.recv_sem.at[unit, slot],
            device_id=device,
            device_id_type=MESH,
        )

    def send(self, unit, slot, source, target, device):
        copy = self.copy(unit, slot, source, target, device)
        copy.start()
        self.sent[unit, slot] = copy

    def arrived(self, unit, slot, target, device):
        self.copy(unit, slot, target, target, device).wait_recv()

    def settle(self, unit, slot):
        self.sent.pop((unit, slot)).wait_send()

    def finish(self):
        for at in list(self.sent):
            self.settle(*at)


SLOTS = 14


def unit_list(shapes):
    units = []
    for index, (rows, columns) in enumerate(shapes):
        width = UNIT // rows
        units += [(index, first, width) for first in range(0, columns, width)]
    return units


def small_gather_phases(place, mail, unit, source, full, local_sem):
    y, x, z, c = place.y, place.x, place.z, place.c
    nz = place.depth - 1

    def first():
        pltpu.make_async_copy(source, full.at[y, x, z, c], local_sem).start()
        for k in range(nz):
            mail.send(unit, k, source, full.at[y, x, z, c], place.column(place.ahead[k]))

    def second():
        pltpu.make_async_copy(source, full.at[y, x, z, c], local_sem).wait()
        for k in range(nz):
            q = place.behind[k]
            mail.arrived(unit, k, full.at[y, x, q, c], place.column(q))
        mail.send(unit, 3, full.at[y, x, :, c], full.at[y, x, :, c], place.along_x)

    def third():
        mail.arrived(unit, 3, full.at[y, 1 - x, :, c], place.along_x)
        mail.send(unit, 5, full.at[y, :, :, c], full.at[y, :, :, c], place.along_y)

    def fourth():
        mail.arrived(unit, 5, full.at[1 - y, :, :, c], place.along_y)
        mail.send(unit, 7, full.at[:, :, :, c], full.at[:, :, :, c], place.other_core)

    def last():
        mail.arrived(unit, 7, full.at[:, :, :, 1 - c], place.other_core)

    return first, second, third, fourth, last


def by_rows(left, right):
    return contract(left, right, 1, 1)


def by_columns(left, right):
    return contract(left, right, 0, 0)


def plain(left, right):
    return jnp.dot(left, right, preferred_element_type=jnp.float32)


class Table:
    GAIN_ONE, SHIFT_ONE, QUERY, VALUE, OUT, GAIN_TWO, SHIFT_TWO, DOWN = range(8)

    def __init__(self, packed, narrow, wide):
        self.packed, self.narrow, self.wide = packed, narrow, wide

    def expand(self, devices):
        y_count, x_count, z_count, c_count = self.packed.shape[:4]

        def tile(d):
            d, c = divmod(d, c_count)
            d, z = divmod(d, z_count)
            y, x = divmod(d, x_count)
            return self.packed[y, x, z, c]

        group = lax.broadcasted_iota(jnp.int32, (8, 128), 1) // 32
        for base in range(0, devices, 4):
            tiles = [tile(base + i) for i in range(4)]
            for i in range(4):
                self.wide[:, pl.ds(128 * (base + i), 128)] = tiles[i][0:1, :]
            for q in range(4):
                mixed = jnp.zeros((8, 128), jnp.float32)
                for i in range(4):
                    turned = tiles[i] if i == q else pltpu.roll(tiles[i], 32 * ((i - q) % 4), 1)
                    mixed = jnp.where(group == i, turned, mixed)
                self.narrow[q, :, pl.ds(32 * base, 128)] = mixed

    def __getitem__(self, index):
        return self.narrow[index % 4, 1 + index // 4 : 2 + index // 4, :]


def row_facts(lengths, codes, row):
    begin = jnp.int32(0)
    segment = jnp.zeros(row.shape, jnp.int32)
    first = jnp.zeros(row.shape, jnp.int32)
    code = jnp.full(row.shape, codes[0, 0], jnp.int32)
    for item in range(1, lengths.shape[1]):
        begin = begin + lengths[0, item - 1]
        inside = row >= begin
        segment = jnp.where(inside, item, segment)
        first = jnp.where(inside, begin, first)
        code = jnp.where(inside, codes[0, item], code)
    return segment, (row - first).astype(jnp.float32) * (0.5 * (code.astype(jnp.float32) + 1.0))


def fill_mask(lengths, codes, mask):
    rows = mask.shape[0]
    across, _ = row_facts(lengths, codes, lax.broadcasted_iota(jnp.int32, (1, rows), 1))
    for base in range(0, rows, 128):
        down, _ = row_facts(lengths, codes, lax.broadcasted_iota(jnp.int32, (128, 1), 0) + base)
        mask[base : base + 128, :] = jnp.where(down == across, 0.0, -1e30)


def head_half(rows, which):
    lane = lax.broadcasted_iota(jnp.int32, (rows, 2 * HEAD_DIM), 1)
    return (lane >= HEAD_DIM) if which else (lane < HEAD_DIM)


def pair_span(pair, offset):
    return pl.ds(pl.multiple_of(offset + pair * 2 * HEAD_DIM, 2 * HEAD_DIM), 2 * HEAD_DIM)


def attend(first_pair, last_pair, projected, mask, attended):
    rows, width = attended.shape
    zero = jnp.zeros((), jnp.bfloat16)
    scale = jnp.asarray(1.0 / math.sqrt(HEAD_DIM), jnp.bfloat16)

    def one_pair(pair, carry):
        query = projected[:, pair_span(pair, 0)] * scale
        key = projected[:, pair_span(pair, width)]
        value = projected[:, pair_span(pair, 2 * width)]
        results = []
        for which in range(2):
            scores = by_rows(jnp.where(head_half(rows, which), query, zero), key) + mask[...]
            top = jnp.max(scores, axis=1, keepdims=True)
            expon = jnp.exp(scores - top)
            total = jnp.sum(expon, axis=1, keepdims=True)
            weights = (expon * (1.0 / total)).astype(jnp.bfloat16)
            results.append(plain(weights, value))
        mixed = jnp.where(head_half(rows, 0), results[0], results[1])
        attended[:, pair_span(pair, 0)] = mixed.astype(jnp.bfloat16)
        return carry

    lax.fori_loop(first_pair, last_pair, one_pair, 0)


CHUNK = 64


def over_rows(rows, step):
    def one(index, carry):
        step(pl.ds(pl.multiple_of(index * CHUNK, CHUNK), CHUNK), index * CHUNK)
        return carry

    lax.fori_loop(0, rows // CHUNK, one, 0)


def normalised(values):
    centred = values - jnp.mean(values, axis=-1, keepdims=True)
    variance = jnp.mean(centred * centred, axis=-1, keepdims=True)
    scale = lax.rsqrt(variance + EPSILON)
    return centred * scale, scale


def attend_back(first_pair, last_pair, projected, mask, grad_attended, sums, weights_low, grad_low):
    rows, width = grad_attended.shape
    zero = jnp.zeros((), jnp.bfloat16)
    scale = 1.0 / math.sqrt(HEAD_DIM)

    def one_pair(pair, carry):
        query, key, value = (projected[:, pair_span(pair, k * width)] for k in range(3))
        grad = grad_attended[:, pair_span(pair, 0)]
        scaled = query * jnp.asarray(scale, jnp.bfloat16)
        g_query, g_key, g_value = [], [], []
        for which in range(2):
            keep = head_half(rows, which)
            scores = by_rows(jnp.where(keep, key, zero), scaled) + mask[...]
            expon = jnp.exp(scores - jnp.max(scores, axis=0, keepdims=True))
            weights = expon * (1.0 / jnp.sum(expon, axis=0, keepdims=True))
            weights_low[which] = weights.astype(jnp.bfloat16)
            slopes = by_rows(jnp.where(keep, value, zero), grad)
            level = jnp.sum(weights * slopes, axis=0, keepdims=True)
            grad_low[which] = (weights * (slopes - level)).astype(jnp.bfloat16)
            g_value.append(plain(weights_low[which], grad))
            g_key.append(plain(grad_low[which], query))
            g_query.append(by_columns(grad_low[which], key))
        keep = head_half(rows, 0)
        for k, (parts, factor) in enumerate(((g_query, scale), (g_key, scale), (g_value, 1.0))):
            mixed = (jnp.where(keep, parts[0], parts[1]) * factor).astype(jnp.bfloat16)
            projected[:, pair_span(pair, k * width)] = mixed
            if k != 1:
                slot = Table.QUERY if k == 0 else Table.VALUE
                total = jnp.sum(mixed.astype(jnp.float32), axis=0, keepdims=True)
                sums[slot % 4, 1 + slot // 4 : 2 + slot // 4, pair_span(pair, 0)] = total
        return carry

    lax.fori_loop(first_pair, last_pair, one_pair, 0)


def gather_phases(place, mail, unit, kind, source, full, local_sem):
    y, x, z, c = place.y, place.x, place.z, place.c
    nz = place.depth - 1

    def begin():
        pltpu.make_async_copy(source, full(y, x, z, c, ALL), local_sem).start()
        for k in range(nz):
            mail.send(unit, k, source, full(y, x, z, c, ALL), place.column(place.ahead[k]))
        if kind:
            mail.send(unit, 3, source.at[0], full(y, x, z, c, 0), place.along_x)
            mail.send(unit, 4, source.at[1], full(y, x, z, c, 1), place.along_y)

    def second():
        pltpu.make_async_copy(source, full(y, x, z, c, ALL), local_sem).wait()
        if kind:
            for slot, partner, block in (
                (3, place.along_x, full(y, 1 - x, z, c, 0)),
                (4, place.along_y, full(1 - y, x, z, c, 1)),
            ):
                mail.arrived(unit, slot, block, partner)
                for k in range(nz):
                    mail.send(unit, 8 + 3 * (slot - 3) + k, block, block, place.column(place.ahead[k]))
            return
        for k in range(nz):
            q = place.behind[k]
            mail.arrived(unit, k, full(y, x, q, c, ALL), place.column(q))
        mail.send(unit, 3, full(y, x, ALL, c, 0), full(y, x, ALL, c, 0), place.along_x)
        mail.send(unit, 4, full(y, x, ALL, c, 1), full(y, x, ALL, c, 1), place.along_y)

    def third():
        if kind:
            for k in range(nz):
                q = place.behind[k]
                mail.arrived(unit, k, full(y, x, q, c, ALL), place.column(q))
            for k in range(nz):
                q = place.behind[k]
                mail.arrived(unit, 8 + k, full(y, 1 - x, q, c, 0), place.column(q))
        else:
            mail.arrived(unit, 3, full(y, 1 - x, ALL, c, 0), place.along_x)
        mail.send(unit, 5, full(y, ALL, ALL, c, 0), full(y, ALL, ALL, c, 0), place.along_y)
        if kind:
            for k in range(nz):
                q = place.behind[k]
                mail.arrived(unit, 11 + k, full(1 - y, x, q, c, 1), place.column(q))
        else:
            mail.arrived(unit, 4, full(1 - y, x, ALL, c, 1), place.along_y)
        mail.send(unit, 6, full(ALL, x, ALL, c, 1), full(ALL, x, ALL, c, 1), place.along_x)

    def fourth():
        mail.arrived(unit, 5, full(1 - y, ALL, ALL, c, 0), place.along_y)
        mail.arrived(unit, 6, full(ALL, 1 - x, ALL, c, 1), place.along_x)
        mail.send(unit, 7, full(ALL, ALL, ALL, c, ALL), full(ALL, ALL, ALL, c, ALL), place.other_core)

    def last():
        mail.arrived(unit, 7, full(ALL, ALL, ALL, 1 - c, ALL), place.other_core)

    return begin, second, third, fourth, last


class Sum:
    def __init__(self, place, mail, unit, kind, part, held, wide, late):
        self.place, self.mail, self.unit, self.kind = place, mail, unit, kind
        self.part, self.held, self.wide, self.late = part, held, wide, late
        self.nz = place.depth - 1

    def first(self):
        p = self.place
        self.mail.send(self.unit, 7, self.part.at[:, :, :, 1 - p.c], self.held, p.other_core)

    def second(self):
        p, mail, unit, held = self.place, self.mail, self.unit, self.held
        mail.arrived(unit, 7, held, p.other_core)
        for a in range(PLANE):
            for b in range(PLANE):
                held[a, b] = held[a, b] + self.part[a, b, :, p.c]
        mail.send(unit, 5, held.at[1 - p.y, :, :, 0], self.wide.at[0], p.along_y)
        mail.send(unit, 6, held.at[:, 1 - p.x, :, 1], self.wide.at[1], p.along_x)
        mail.settle(unit, 7)

    def pair(self, half, k):
        return self.late.at[pl.ds(2 * (self.nz * half + k), 2)]

    def near(self, half):
        depth = self.nz + 1
        return self.late.at[pl.ds(depth * half, depth)]

    def column(self, k):
        return self.late.at[pl.ds(2 * (self.nz + 1) + 2 * k, 2)]

    def final(self, half):
        return self.late.at[4 * self.nz + half]

    def third(self):
        p, mail, unit, held, wide = self.place, self.mail, self.unit, self.held, self.wide
        y, x = p.y, p.x
        mail.arrived(unit, 5, wide.at[0], p.along_y)
        for b in range(PLANE):
            held[y, b, :, 0] = held[y, b, :, 0] + wide[0, b]
        if self.kind:
            for k in range(self.nz):
                q = p.ahead[k]
                mail.send(unit, 8 + k, held.at[y, :, q, 0], self.pair(0, k), p.column(q))
        else:
            mail.send(unit, 3, held.at[y, 1 - x, :, 0], self.near(0), p.along_x)
        mail.arrived(unit, 6, wide.at[1], p.along_x)
        for b in range(PLANE):
            held[b, x, :, 1] = held[b, x, :, 1] + wide[1, b]
        if self.kind:
            for k in range(self.nz):
                q = p.ahead[k]
                mail.send(unit, 11 + k, held.at[:, x, q, 1], self.pair(1, k), p.column(q))
        else:
            mail.send(unit, 4, held.at[1 - y, x, :, 1], self.near(1), p.along_y)

    def fourth(self):
        p, mail, unit, held = self.place, self.mail, self.unit, self.held
        y, x, z = p.y, p.x, p.z
        full = jnp.float32
        if self.kind:
            for half in range(2):
                at = (y, ALL, z, 0) if half == 0 else (ALL, x, z, 1)
                total = held[at].astype(full)
                for k in range(self.nz):
                    mail.arrived(unit, 8 + 3 * half + k, self.pair(half, k), p.column(p.behind[k]))
                    total = total + self.pair(half, k)[...].astype(full)
                held[at] = total.astype(held.dtype)
            mail.send(unit, 3, held.at[y, 1 - x, z, 0], self.final(0), p.along_x)
            mail.send(unit, 4, held.at[1 - y, x, z, 1], self.final(1), p.along_y)
            return
        mail.arrived(unit, 3, self.near(0), p.along_x)
        mail.arrived(unit, 4, self.near(1), p.along_y)
        for half in range(2):
            held[y, x, :, half] = held[y, x, :, half] + self.near(half)[...]
        for k in range(self.nz):
            q = p.ahead[k]
            mail.send(unit, k, held.at[y, x, q], self.column(k), p.column(q))

    def last(self):
        p, mail, unit, held = self.place, self.mail, self.unit, self.held
        full = jnp.float32
        halves = [held[p.y, p.x, p.z, half].astype(full) for half in range(2)]
        if self.kind:
            mail.arrived(unit, 3, self.final(0), p.along_x)
            mail.arrived(unit, 4, self.final(1), p.along_y)
            halves = [v + self.final(half)[...].astype(full) for half, v in enumerate(halves)]
        else:
            for k in range(self.nz):
                mail.arrived(unit, k, self.column(k), p.column(p.behind[k]))
                halves = [v + self.column(k)[half].astype(full) for half, v in enumerate(halves)]
        for slot in [s for u, s in list(mail.sent) if u == unit]:
            mail.settle(unit, slot)
        return halves


INBOXES = 6
HELD = 4
TILE = 256
GATHER_KINDS = (0, 0, 0, 0, 0, 1, 0, 1, 0, 1, 0, 1)
SUM_KINDS = (0, 0, 0, 0, 0, 0, 0, 0, 0, 0, 0, 0)
ORDER = (
    ("g", 0, 0), ("prepare",), ("g", 1, 0), ("g", 0, 1), ("g", 2, 0), ("g", 0, 2), ("g", 1, 1), ("g", 3, 0),
    ("g", 0, 3), ("g", 2, 1), ("g", 4, 0), ("g", 5, 0), ("g", 1, 2), ("g", 2, 2), ("g", 3, 1), ("g", 6, 0),
    ("g", 1, 3), ("g", 4, 1), ("g", 1, 4), ("g", 5, 1), ("g", 7, 0), ("g", 0, 4), ("g", 3, 2), ("g", 2, 3),
    ("norm1",), ("g", 6, 1), ("g", 8, 0), ("g", 4, 2), ("g", 6, 2), ("project", 0), ("g", 7, 1), ("g", 8, 1),
    ("project", 1), ("g", 9, 0), ("g", 4, 3), ("g", 2, 4), ("project", 2), ("g", 10, 0), ("g", 5, 2), ("attend", 0),
    ("g", 8, 2), ("g", 6, 3), ("g", 4, 4), ("g", 3, 3), ("attend", 1), ("g", 7, 2), ("g", 3, 4), ("g", 9, 1),
    ("g", 5, 3), ("norm2",), ("rise", 0), ("g", 11, 0), ("g", 8, 3), ("g", 5, 4), ("g", 10, 1), ("g", 8, 4),
    ("g", 7, 3), ("g", 9, 2), ("g", 6, 4), ("g", 11, 1), ("rise", 1), ("g", 10, 2), ("rise", 2), ("g", 7, 4),
    ("rise", 3), ("part", 0), ("s", 0, 0), ("g", 9, 3), ("g", 11, 2), ("part", 1), ("fall", 0), ("g", 10, 3),
    ("s", 1, 0), ("s", 0, 1), ("g", 9, 4), ("part", 2), ("fall", 1), ("g", 10, 4), ("s", 2, 0), ("part", 3),
    ("s", 3, 0), ("fall", 2), ("g", 11, 3), ("s", 1, 1), ("g", 11, 4), ("s", 2, 1), ("fall", 3), ("hidden", 0),
    ("part", 4), ("s", 4, 0), ("s", 0, 2), ("hidden", 1), ("part", 5), ("s", 3, 1), ("hidden", 2), ("part", 6),
    ("s", 1, 2), ("hidden", 3), ("up", 0), ("s", 0, 3), ("up", 1), ("s", 5, 0), ("s", 2, 2), ("up", 2), ("up", 3),
    ("s", 4, 1), ("branch",), ("out",), ("s", 5, 1), ("s", 0, 4), ("s", 1, 3), ("part", 7), ("heads", 0), ("s", 3, 2),
    ("s", 4, 2), ("s", 6, 0), ("s", 2, 3), ("part", 8), ("s", 5, 2), ("s", 1, 4), ("s", 6, 1), ("s", 7, 0),
    ("heads", 1), ("again",), ("s", 2, 4), ("s", 4, 3), ("s", 3, 3), ("s", 8, 0), ("s", 7, 1), ("heads", 2),
    ("s", 8, 1), ("s", 6, 2), ("heads", 3), ("part", 9), ("s", 7, 2), ("s", 3, 4), ("s", 5, 3), ("s", 4, 4),
    ("s", 9, 0), ("part", 10), ("s", 9, 1), ("qkv", 0), ("s", 10, 0), ("qkv", 1), ("s", 6, 3), ("s", 7, 3),
    ("qkv", 2), ("s", 5, 4), ("s", 8, 2), ("s", 10, 1), ("qkv", 3), ("s", 9, 2), ("part", 11), ("tokens",),
    ("s", 11, 0), ("pack",), ("s", 8, 3), ("s", 12, 0), ("s", 11, 1), ("s", 10, 2), ("s", 7, 4), ("s", 9, 3),
    ("s", 11, 2), ("s", 12, 1), ("s", 10, 3), ("s", 8, 4), ("s", 12, 2), ("s", 6, 4), ("s", 11, 3), ("s", 9, 4),
    ("s", 12, 3), ("s", 12, 4), ("s", 10, 4), ("s", 11, 4),
)


def layer_kernel(depth, units, sums_units, *refs):
    refs = list(refs)

    def take(count):
        taken = refs[:count]
        del refs[:count]
        return taken

    sources = take(4)
    vectors = take(9)
    tokens, cotangent, lengths, codes = take(4)
    fulls = take(4)
    a_projected, a_attended, a_start = take(3)
    o_output, o_tokens = take(2)
    outs = take(4)
    (o_small,) = take(1)
    small, packed, narrow, wide = take(4)
    inbox, wide_in, late_in, r_square, r_tall, parts = take(6)
    s_part, s_core, s_wide, s_near, s_column, s_result = take(6)
    big, hidden_grad, square, tall, stream, grad_middle, grad_normed = take(7)
    normed, branch, grad_attended, finished, weights_low, grad_low, mask, sums, wide_sums = take(9)
    send_sem, recv_sem, local_sem, load_sem, store_sem, free_sem = take(6)

    place, mail = Place(depth), Mail(send_sem, recv_sem)
    y, x, z, c = place.y, place.x, place.z, place.c
    nz = depth - 1
    rows, width = stream.shape
    hidden = hidden_grad.shape[1]
    pairs = width // (2 * HEAD_DIM)
    low, full = jnp.bfloat16, jnp.float32
    table = Table(packed, narrow, wide)
    projected, attended = big.at[:, pl.ds(0, 3 * width)], big.at[:, pl.ds(3 * width, width)]
    corners = [(a, b) for a in range(PLANE) for b in range(PLANE)]
    stores, numbers = {}, iter(range(64))

    def store(name, source, target):
        copy = pltpu.make_async_copy(source, target, store_sem.at[len(stores)])
        copy.start()
        stores[name] = [copy, True]

    def stored(name):
        if stores[name][1]:
            stores[name][0].wait()
            stores[name][1] = False

    def load(source, target):
        return pltpu.make_async_copy(source, target, load_sem.at[next(numbers)])

    def flat(block):
        return block.reshape(-1, block.shape[-1])

    def pack_vectors():
        narrow[...] = jnp.zeros_like(narrow)
        count = vectors[0].shape[0]
        for k, ref in enumerate(vectors[:-1]):
            narrow[k % 4, k // 4 : k // 4 + 1, 0:count] = ref[...].astype(full).reshape(1, count)
        small[...] = jnp.zeros_like(small)
        small[0:1, :] = vectors[-1][...].astype(full).reshape(1, 128)
        for line in range(2):
            total = narrow[0, line : line + 1, 0:128]
            for q in range(1, 4):
                total = total + pltpu.roll(narrow[q, line : line + 1, 0:128], count * q, 1)
            small[1 + line : 2 + line, :] = total

    def piece(unit):
        index, first, columns = units[unit]
        span = pl.ds(first, columns)

        def view(*at):
            return fulls[index].at[at + (ALL, span)]

        return sources[index].at[:, :, span], view

    gathers = [
        gather_phases(place, mail, unit + 1, GATHER_KINDS[unit], *piece(unit), local_sem.at[unit + 1])
        for unit in range(len(units))
    ]
    small_gather = small_gather_phases(place, mail, 0, small, packed, local_sem.at[0])
    places = []
    for unit, (index, first, columns) in enumerate(units):
        buffer = tall if index == 3 else square
        places.append((buffer, sum((u[0] == 3) == (index == 3) for u in units[:unit]) % 2))
    loads = [
        load(piece(unit)[1](ALL, ALL, ALL, ALL, ALL), buffer.at[at])
        for unit, (buffer, at) in enumerate(places)
    ]

    def weights(unit, columns):
        buffer, at = places[unit]
        return flat(buffer[at, :, :, :, :, :, :, columns])

    def corner_loads(index, corner, buffer, at):
        a, b = corners[corner]
        chosen = [u for u in units if u[0] == index]
        return [
            load(
                fulls[index].at[a, b, :, :, :, :, pl.ds(first, columns)],
                buffer.at[at, e // PLANE, e % PLANE],
            )
            for e, (_, first, columns) in enumerate(chosen)
        ]

    get_down = [corner_loads(3, n, tall, n % 2) for n in range(4)]
    get_up = [corner_loads(2, n, square, n % 2) for n in range(4)]
    get_out = [
        load(fulls[1].at[a, b], square.at[0, n // PLANE, n % PLANE]) for n, (a, b) in enumerate(corners)
    ]
    get_qkv = [corner_loads(0, n, square, (n + 1) % 2) for n in range(4)]
    get_projected = load(a_projected, projected)
    get_attended = load(a_attended, attended)
    get_start = load(a_start, stream)

    def start_all(copies):
        for copy in copies:
            copy.start()

    def wait_all(copies):
        for copy in copies:
            copy.wait()

    get_tokens = load(tokens, finished)

    def prepare():
        get_tokens.wait()
        def chunk(span, base):
            row = lax.broadcasted_iota(jnp.int32, (CHUNK, 1), 0) + base
            _, factor = row_facts(lengths, codes, row)
            lane = lax.broadcasted_iota(jnp.int32, (1, width // 2), 1).astype(full)
            phase = factor * jnp.exp(lane * (-math.log(10000.0) / (width // 2)))
            left, right = pl.ds(0, width // 2), pl.ds(width // 2, width // 2)
            stream[span, left] = finished[span, left].astype(full) + jnp.sin(phase)
            stream[span, right] = finished[span, right].astype(full) + jnp.cos(phase)

        over_rows(rows, chunk)
        store("start", stream, a_start)
        fill_mask(lengths, codes, mask)
        sums[...] = jnp.zeros_like(sums)

    def norm(gain, shift):
        def chunk(span, base):
            normed[span, :] = (normalised(stream[span, :])[0] * table[gain] + table[shift]).astype(low)

        over_rows(rows, chunk)

    def project(unit, bias):
        tile = 512
        for first in range(0, width, tile):
            value = plain(normed[...], weights(unit, pl.ds(first, tile)))
            if bias is not None:
                value = value + table[bias][:, first : first + tile]
            big[:, pl.ds(unit * width + first, tile)] = value.astype(low)

    def project_out(unit):
        tile = 512
        stored("start")
        for first in range(0, width, tile):
            span = pl.ds(first, tile)
            value = plain(attended[...], weights(unit, span)) + table[Table.OUT][:, first : first + tile]
            stream[:, span] = stream[:, span] + value

    def rise(unit, number):
        def one(index, carry):
            at = pl.multiple_of(index * TILE, TILE)
            there = pl.ds(pl.multiple_of(number * width + at, TILE), TILE)
            pre = plain(normed[...], weights(unit, pl.ds(at, TILE))) + wide[:, there]
            normal = 0.5 * (1.0 + lax.erf(pre * math.sqrt(0.5)))
            density = jnp.exp(pre * pre * -0.5) * (1.0 / math.sqrt(2.0 * math.pi))
            big[:, there] = (pre * normal).astype(low)
            hidden_grad[:, there] = (normal + pre * density).astype(low)
            return carry

        lax.fori_loop(0, width // TILE, one, 0)

    def fall(unit, number, columns):
        span = pl.ds(number * columns, columns)
        value = plain(big[...], weights(unit, ALL)) + table[Table.DOWN][:, number * columns : (number + 1) * columns]
        finished[:, span] = (stream[:, span] + value).astype(low)

    def tally(slot, values):
        at = (slot % 4, pl.ds(1 + slot // 4, 1), ALL)
        sums[at] = sums[at] + jnp.sum(values, axis=0, keepdims=True)

    def square_part(unit, left, right, first):
        for k in range(width // TILE):
            value = by_columns(left[...], right[:, pl.ds(first + TILE * k, TILE)]).astype(low)
            parts[unit % HELD, :, :, :, :, :, k] = value.reshape(parts.shape[1:6] + (parts.shape[7], TILE))

    def tall_part(unit, first):
        def one(corner, carry):
            left = big[:, pl.ds(pl.multiple_of(corner * width, width), width)]
            value = by_columns(left, cotangent[:, pl.ds(first, TILE)]).astype(low)
            parts[unit % HELD, corner // PLANE, lax.rem(corner, PLANE)] = value.reshape(parts.shape[3:])
            return carry

        lax.fori_loop(0, PLANE * PLANE, one, 0)

    def part_of(unit):
        index, first, columns = sums_units[unit]
        if index == 3:
            tall_part(unit, first)
        elif index == 2:
            square_part(unit, normed, hidden_grad, first)
        elif index == 1:
            square_part(unit, attended, branch, 0)
        else:
            square_part(unit, normed, big, first)

    def hidden_step(n):
        wait_all(get_down[n])

        def one(m, carry):
            block = jnp.concatenate(
                [flat(tall[n % 2, e // PLANE, e % PLANE, m]) for e in range(4)], axis=1
            )
            span = pl.ds(pl.multiple_of(n * width + m * TILE, TILE), TILE)
            value = (by_rows(cotangent[...], block) * hidden_grad[:, span].astype(full)).astype(low)
            hidden_grad[:, span] = value
            wide_sums[:, span] = jnp.sum(value.astype(full), axis=0, keepdims=True)
            return carry

        lax.fori_loop(0, width // TILE, one, 0)
        if n + 2 < 4:
            start_all(get_down[n + 2])

    def back_through(copies, left, at, n):
        wait_all(copies)
        total = None
        for e in range(len(copies)):
            value = by_rows(left[:, pl.ds(e * width, width)], flat(square[at, e // PLANE, e % PLANE]))
            total = value if total is None else total + value
        grad_normed[:, pl.ds(TILE * n, TILE)] = total

    def up_step(n):
        back_through(get_up[n], hidden_grad, n % 2, n)
        if n + 2 < 4:
            start_all(get_up[n + 2])
        if n == 2:
            start_all(get_out)
        if n == 3:
            start_all(get_qkv[0])

    def out_step():
        wait_all(get_out)
        for n in range(4):
            block = flat(square[0, n // PLANE, n % PLANE])
            grad_attended[:, pl.ds(TILE * n, TILE)] = by_rows(branch[...], block).astype(low)
        start_all(get_qkv[1])

    def qkv_step(n):
        back_through(get_qkv[n], big, (n + 1) % 2, n)
        if n + 2 < 4:
            start_all(get_qkv[n + 2])

    def norm_back(span, gain, shift):
        level, scale = normalised(stream[span, :])
        grad = grad_normed[span, :]
        tally(gain, grad * level)
        tally(shift, grad)
        grad = grad * table[gain]
        mean = jnp.mean(grad, axis=-1, keepdims=True)
        along = jnp.mean(grad * level, axis=-1, keepdims=True)
        return scale * (grad - mean - level * along)

    def second_norm_back():
        def chunk(span, base):
            value = cotangent[span, :].astype(full) + norm_back(span, Table.GAIN_TWO, Table.SHIFT_TWO)
            grad_middle[span, :] = value
            branch[span, :] = value.astype(low)
            tally(Table.OUT, value.astype(low).astype(full))
            tally(Table.DOWN, cotangent[span, :].astype(full))

        over_rows(rows, chunk)

    def first_norm_back():
        stored("output")

        def chunk(span, base):
            value = grad_middle[span, :] + norm_back(span, Table.GAIN_ONE, Table.SHIFT_ONE)
            finished[span, :] = value.astype(low)

        over_rows(rows, chunk)
        store("tokens", finished, o_tokens)

    def attention_back(first, last):
        attend_back(first, last, big, mask, grad_attended, sums, weights_low, grad_low)

    def pack():
        group = lax.broadcasted_iota(jnp.int32, (8, 128), 1) // 32
        line = lax.broadcasted_iota(jnp.int32, (8, 128), 0)
        shape = s_part.shape[:4]
        for device in range(math.prod(shape)):
            i, base = device % 4, 32 * (device - device % 4)
            mixed = jnp.zeros((8, 128), full)
            for q in range(4):
                tile = sums[q, :, pl.ds(base, 128)]
                turned = tile if i == q else pltpu.roll(tile, 32 * ((q - i) % 4), 1)
                mixed = jnp.where(group == q, turned, mixed)
            share = jnp.broadcast_to(wide_sums[:, pl.ds(128 * device, 128)], (8, 128))
            at, k = divmod(device, shape[3])
            at, m = divmod(at, shape[2])
            s_part[at // shape[1], at % shape[1], m, k] = jnp.where(line == 0, share, mixed)

    base = len(units) + 1

    def unit_steps(unit):
        index, start, columns = sums_units[unit]
        piece = Sum(
            place, mail, base + unit, SUM_KINDS[unit],
            parts.at[unit % HELD], inbox.at[unit % INBOXES], wide_in.at[unit], late_in.at[unit],
        )

        def first():
            if unit >= INBOXES:
                pl.semaphore_wait(free_sem.at[unit], 1)
            piece.first()

        def last():
            halves = piece.last()
            if index == 3:
                final = r_tall.at[unit]
                for half, value in enumerate(halves):
                    final[half] = value
                store(f"part {unit}", final, outs[index].at[:, :, :, pl.ds(start, columns)])
            else:
                final = r_square.at[unit - 4]
                for half, value in enumerate(halves):
                    for k in range(value.shape[0]):
                        final[half, :, pl.ds(TILE * k, TILE)] = value[k]
                store(f"part {unit}", final, outs[index].at[:, :, pl.ds(start, columns)])
            if unit + INBOXES < len(sums_units):
                pl.semaphore_signal(
                    free_sem.at[unit + INBOXES], inc=1, device_id=place.other_core, device_id_type=MESH
                )

        return first, piece.second, piece.third, piece.fourth, last

    def small_steps():
        unit = base + len(sums_units)
        held = s_core

        def first():
            mail.send(unit, 7, s_part.at[:, :, :, 1 - c], held, place.other_core)

        def second():
            mail.arrived(unit, 7, held, place.other_core)
            for a, b in corners:
                held[a, b] = held[a, b] + s_part[a, b, :, c]
            mail.send(unit, 5, held.at[1 - y], s_wide, place.along_y)

        def third():
            mail.arrived(unit, 5, s_wide, place.along_y)
            held[y] = held[y] + s_wide[...]
            mail.send(unit, 3, held.at[y, 1 - x], s_near, place.along_x)

        def fourth():
            mail.arrived(unit, 3, s_near, place.along_x)
            held[y, x] = held[y, x] + s_near[...]
            for k in range(nz):
                q = place.ahead[k]
                mail.send(unit, k, held.at[y, x, q], s_column.at[k], place.column(q))

        def last():
            total = held[y, x, z]
            for k in range(nz):
                mail.arrived(unit, k, s_column.at[k], place.column(place.behind[k]))
                total = total + s_column[k]
            s_result[...] = total
            store("small", s_result, o_small)

        return first, second, third, fourth, last

    scatters = [unit_steps(unit) for unit in range(len(sums_units))] + [small_steps()]

    begun, landed, used = set(), set(), set()

    def try_load(unit):
        same = [u for u in range(unit) if places[u][0] is places[unit][0] and places[u][1] == places[unit][1]]
        if unit in landed and unit not in begun and used.issuperset(same):
            begun.add(unit)
            loads[unit].start()

    def use(unit, step, *args):
        loads[unit].wait()
        step(unit, *args)
        used.add(unit)
        for later in range(unit + 1, len(units)):
            try_load(later)

    passed = set()

    def reload(name):
        passed.add(name)
        if len(passed) == 5:
            start_all((get_projected, get_attended))

    def projection(unit):
        use(unit, project, (Table.QUERY, None, Table.VALUE)[unit])
        if unit == 2:
            store("projected", projected, a_projected)

    def attention(half):
        attend(half * pairs // 2, (half + 1) * pairs // 2, projected, mask, attended)
        if half == 1:
            store("attended", attended, a_attended)

    def first_norm():
        table.expand(PLANE * PLANE * depth * CORES)
        norm(Table.GAIN_ONE, Table.SHIFT_ONE)

    def second_norm():
        use(3, project_out)
        norm(Table.GAIN_TWO, Table.SHIFT_TWO)
        stored("projected")
        stored("attended")

    def rises(number):
        use(4 + number, rise, number)
        if number == 3:
            start_all(get_up[0] + get_up[1])

    def falls(number):
        use(8 + number, fall, number, TILE)
        if number == 3:
            store("output", finished, o_output)
            start_all(get_down[0] + get_down[1])
            reload("fall")

    def branch_back():
        second_norm_back()
        get_start.start()

    def heads_back(quarter):
        if quarter == 0:
            get_projected.wait()
        attention_back(quarter * pairs // 4, (quarter + 1) * pairs // 4)

    def norm_again():
        get_start.wait()
        norm(Table.GAIN_ONE, Table.SHIFT_ONE)

    def gradient(unit):
        if unit == 8:
            get_attended.wait()
        part_of(unit)
        if unit < 4:
            reload(unit)

    def gather(unit, phase):
        if unit == 0:
            small_gather[phase]()
        gathers[unit][phase]()
        if phase == 4:
            landed.add(unit)
            try_load(unit)

    actions = {
        "g": gather,
        "s": lambda unit, phase: scatters[unit][phase](),
        "prepare": prepare,
        "norm1": first_norm,
        "project": projection,
        "attend": attention,
        "norm2": second_norm,
        "rise": rises,
        "fall": falls,
        "hidden": hidden_step,
        "up": up_step,
        "branch": branch_back,
        "out": out_step,
        "heads": heads_back,
        "again": norm_again,
        "qkv": qkv_step,
        "tokens": first_norm_back,
        "pack": pack,
        "part": gradient,
    }
    get_tokens.start()
    pack_vectors()
    place.greet()
    for name, *args in ORDER:
        actions[name](*args)
    for name in list(stores):
        stored(name)
    mail.finish()


def run_layer(mesh, tokens, cotangent, lengths, codes, matrices, vectors):
    depth = mesh.shape["fsdp"] // CORES
    grid = (PLANE, PLANE, depth, CORES)
    plane = (PLANE, PLANE, depth)
    rows, width = tokens.shape
    hidden = matrices[2].shape[1]
    devices = mesh.size
    low, full = jnp.bfloat16, jnp.float32
    halves = [m.reshape(2, m.shape[0] // 2, m.shape[1]) for m in matrices]
    units = unit_list([(m.shape[0] * devices, m.shape[1]) for m in matrices])
    sums_units = [u for index in (3, 2, 1, 0) for u in units if u[0] == index]
    count = len(units)
    talls = sum(u[0] == 3 for u in units)
    share = width // devices // 2
    block = (2, width // TILE, share, TILE)
    inner = block[1:]

    def shaped(*shape, dtype=low):
        return jax.ShapeDtypeStruct(shape, dtype)

    anywhere = pl.BlockSpec(memory_space=pl.ANY)
    vmem = pl.BlockSpec(memory_space=pltpu.VMEM)
    smem = pl.BlockSpec(memory_space=pltpu.SMEM)
    out_shape = [shaped(*grid, *h.shape) for h in halves]
    out_shape += [shaped(rows, 3 * width), shaped(rows, width), shaped(rows, width, dtype=full)]
    out_shape += [shaped(rows, width), shaped(rows, width)]
    out_shape += [shaped(2, share, m.shape[1], dtype=full) for m in matrices[:3]]
    out_shape += [shaped(2, hidden // width, share, width, dtype=full), shaped(8, 128, dtype=full)]
    scratch = [
        ((8, 128), full),
        ((*grid, 8, 128), full),
        ((4, 8, width), full),
        ((1, hidden), full),
        ((INBOXES, *plane, *block), low),
        ((count, 2, PLANE, depth, *inner), low),
        ((count, 4 * depth - 2, *inner), low),
        ((count - talls, 2, share, width), full),
        ((talls, *block), full),
        ((HELD, *grid, *block), low),
        ((*grid, 8, 128), full),
        ((*plane, 8, 128), full),
        ((PLANE, depth, 8, 128), full),
        ((depth, 8, 128), full),
        ((depth - 1, 8, 128), full),
        ((8, 128), full),
        ((rows, hidden), low),
        ((rows, hidden), low),
        ((2, *grid, 2, share, width), low),
        ((2, *grid, 2, share * (hidden // width), TILE), low),
        ((rows, width), full),
        ((rows, width), full),
        ((rows, width), full),
        ((rows, width), low),
        ((rows, width), low),
        ((rows, width), low),
        ((rows, width), low),
        ((2, rows, rows), low),
        ((2, rows, rows), low),
        ((rows, rows), full),
        ((4, 8, width), full),
        ((1, hidden), full),
    ]
    outs = pl.pallas_call(
        functools.partial(layer_kernel, depth, units, sums_units),
        out_shape=out_shape,
        in_specs=[anywhere] * 4 + [vmem] * 9 + [anywhere, vmem, smem, smem],
        out_specs=[anywhere] * len(out_shape),
        scratch_shapes=[pltpu.VMEM(shape, dtype) for shape, dtype in scratch]
        + [
            pltpu.SemaphoreType.DMA((2 * count + 2, SLOTS)),
            pltpu.SemaphoreType.DMA((2 * count + 2, SLOTS)),
            pltpu.SemaphoreType.DMA((count + 1,)),
            pltpu.SemaphoreType.DMA((64,)),
            pltpu.SemaphoreType.DMA((24,)),
            pltpu.SemaphoreType.REGULAR((count,)),
        ],
        compiler_params=pltpu.CompilerParams(
            collective_id=0, has_side_effects=True, vmem_limit_bytes=62 << 20
        ),
    )(*halves, *vectors, tokens, cotangent, lengths, codes)
    output, grad_tokens = outs[7:9]
    grads = [o.reshape(-1, o.shape[-1]) for o in outs[9:13]]
    spread = outs[13].reshape(-1)
    wide, narrow = hidden // devices, width // devices
    return output, grad_tokens, grads, [spread[wide + narrow * k : wide + narrow * (k + 1)] for k in range(8)], spread[:wide]


def deliver_kernel(*refs):
    count = (len(refs) - 2) // 3
    arrays, results, held, came, went = refs[:count], refs[count : 2 * count], refs[2 * count : 3 * count], *refs[3 * count :]
    copies = [pltpu.make_async_copy(arrays[k], held[k], came.at[k]) for k in range(count)]
    onward = [pltpu.make_async_copy(held[k], results[k], went.at[k]) for k in range(count)]
    for copy in copies:
        copy.start()
    for first, second in zip(copies, onward):
        first.wait()
        second.start()
    for copy in onward:
        copy.wait()


def deliver(arrays):
    anywhere = pl.BlockSpec(memory_space=pl.ANY)
    return pl.pallas_call(
        deliver_kernel,
        out_shape=[jax.ShapeDtypeStruct(a.shape, a.dtype) for a in arrays],
        in_specs=[anywhere] * len(arrays),
        out_specs=[anywhere] * len(arrays),
        scratch_shapes=[pltpu.VMEM(a.shape, a.dtype) for a in arrays]
        + [pltpu.SemaphoreType.DMA((len(arrays),))] * 2,
        compiler_params=pltpu.CompilerParams(vmem_limit_bytes=62 << 20),
    )(*arrays)


def grid_body(mesh, tokens, cotangent, lengths, scale_codes, *params):
    matrices = params[:4]
    (gain_one, shift_one, bias_query, bias_value, bias_out, gain_two, shift_two, bias_up, bias_down) = params[4:]
    vectors = (gain_one, shift_one, bias_query, bias_value, bias_out, gain_two, shift_two, bias_down, bias_up)
    output, grad_tokens, grads, small, grad_up_bias = run_layer(
        mesh, tokens, cotangent, lengths, scale_codes, matrices, vectors
    )
    output, grad_tokens, *grads = deliver([output, grad_tokens, *grads])
    return (output, grad_tokens, *grads, *small[:7], grad_up_bias, small[7])


def solution(mesh):
    placed = (
        P(("dp", "fsdp"), None),
        P(("dp", "fsdp"), None),
        P(("dp", "fsdp"), None),
        P(("dp", "fsdp"), None),
        P(("dp", "fsdp"), None),
        P(("dp", "fsdp"), None),
        P(("dp", "fsdp"), None),
        P(("dp", "fsdp"), None),
        P(("dp", "fsdp")),
        P(("dp", "fsdp")),
        P(("dp", "fsdp")),
        P(("dp", "fsdp")),
        P(("dp", "fsdp")),
        P(("dp", "fsdp")),
        P(("dp", "fsdp")),
        P(("dp", "fsdp")),
        P(("dp", "fsdp")),
    )
    per_device = body
    if mesh.shape["dp"] == PLANE * PLANE and mesh.shape["fsdp"] == 4 * CORES:
        per_device = functools.partial(grid_body, mesh)
    return jax.shard_map(
        per_device,
        mesh=mesh,
        in_specs=placed,
        out_specs=(
            P(("dp", "fsdp"), None),
            P(("dp", "fsdp"), None),
            P(("dp", "fsdp"), None),
            P(("dp", "fsdp"), None),
            P(("dp", "fsdp"), None),
            P(("dp", "fsdp"), None),
            P(("dp", "fsdp")),
            P(("dp", "fsdp")),
            P(("dp", "fsdp")),
            P(("dp", "fsdp")),
            P(("dp", "fsdp")),
            P(("dp", "fsdp")),
            P(("dp", "fsdp")),
            P(("dp", "fsdp")),
            P(("dp", "fsdp")),
        ),
        check_vma=False,
    )
```

```python
import functools
import math

import jax
import jax.numpy as jnp
from jax import lax
from jax.experimental import pallas as pl
from jax.experimental.pallas import tpu as pltpu
from jax.sharding import PartitionSpec as P

HEADS = 16
HEAD_DIM = 64


EPSILON = 1e-06


def contract(left, right, left_dim, right_dim):
    return lax.dot_general(
        left, right, (((left_dim,), (right_dim,)), ((), ())), preferred_element_type=jnp.float32
    )


def layer_norm(values, gain, shift):
    centred = values - jnp.mean(values, axis=-1, keepdims=True)
    variance = jnp.mean(centred * centred, axis=-1, keepdims=True)
    return centred * lax.rsqrt(variance + EPSILON) * gain + shift


def gelu_exact(values):
    return jax.nn.gelu(values, approximate=False)


def row_tables(length_row, code_row, row_count, feat_width):
    items = jnp.arange(length_row.shape[0], dtype=jnp.int32)
    item_starts = jnp.sum(
        jnp.where(items[None, :] < items[:, None], length_row[None, :], 0), axis=1
    )
    item_ends = item_starts + length_row
    row_index = jnp.arange(row_count, dtype=jnp.int32)
    member = (
        (row_index[:, None] >= item_starts[None, :]) & (row_index[:, None] < item_ends[None, :])
    ).astype(jnp.int32)
    item_ids = jnp.arange(length_row.shape[0], dtype=jnp.int32)
    segment = jnp.sum(member * item_ids[None, :], axis=1)
    place = row_index - jnp.sum(member * item_starts[None, :], axis=1)
    row_code = jnp.sum(member * code_row[None, :], axis=1)
    half_width = feat_width // 2
    frequency = jnp.exp(
        jnp.arange(half_width, dtype=jnp.float32) * (-math.log(10000.0) / half_width)
    )
    gsd_ratio = 0.5 * (row_code.astype(jnp.float32) + 1.0)
    phase_angle = (place.astype(jnp.float32) * gsd_ratio)[:, None] * frequency[None, :]
    return (segment, jnp.concatenate([jnp.sin(phase_angle), jnp.cos(phase_angle)], axis=1))


def body(
    tokens,
    cotangent,
    lengths,
    scale_codes,
    w_qkv,
    w_out,
    w_up,
    w_down,
    ln1_gain,
    ln1_shift,
    bias_query,
    bias_value,
    bias_out,
    ln2_gain,
    ln2_shift,
    bias_up,
    bias_down,
):
    gathered = (
        lax.all_gather(w_qkv, ("dp", "fsdp"), axis=0, tiled=True),
        lax.all_gather(w_out, ("dp", "fsdp"), axis=0, tiled=True),
        lax.all_gather(w_up, ("dp", "fsdp"), axis=0, tiled=True),
        lax.all_gather(w_down, ("dp", "fsdp"), axis=0, tiled=True),
        lax.all_gather(ln1_gain, ("dp", "fsdp"), axis=0, tiled=True),
        lax.all_gather(ln1_shift, ("dp", "fsdp"), axis=0, tiled=True),
        lax.all_gather(bias_query, ("dp", "fsdp"), axis=0, tiled=True),
        lax.all_gather(bias_value, ("dp", "fsdp"), axis=0, tiled=True),
        lax.all_gather(bias_out, ("dp", "fsdp"), axis=0, tiled=True),
        lax.all_gather(ln2_gain, ("dp", "fsdp"), axis=0, tiled=True),
        lax.all_gather(ln2_shift, ("dp", "fsdp"), axis=0, tiled=True),
        lax.all_gather(bias_up, ("dp", "fsdp"), axis=0, tiled=True),
        lax.all_gather(bias_down, ("dp", "fsdp"), axis=0, tiled=True),
    )
    (
        full_qkv,
        full_out,
        full_up,
        full_down,
        gain_first,
        shift_first,
        query_bias,
        value_bias,
        out_bias,
        gain_second,
        shift_second,
        up_bias,
        down_bias,
    ) = gathered
    gain_one = gain_first.astype(jnp.float32)
    shift_one = shift_first.astype(jnp.float32)
    gain_two = gain_second.astype(jnp.float32)
    shift_two = shift_second.astype(jnp.float32)
    row_count, model_width = tokens.shape
    head_width = model_width // HEADS
    score_scale = 1.0 / math.sqrt(HEAD_DIM)
    segment, encoding = row_tables(lengths[0], scale_codes[0], row_count, model_width)
    same_item = segment[:, None] == segment[None, :]
    start = tokens.astype(jnp.float32) + encoding
    normed_one = layer_norm(start, gain_one, shift_one).astype(jnp.bfloat16)
    qkv_bias = jnp.concatenate([query_bias, jnp.zeros_like(query_bias), value_bias]).astype(
        jnp.float32
    )
    projected = (
        jnp.dot(normed_one, full_qkv, preferred_element_type=jnp.float32) + qkv_bias
    ).astype(jnp.bfloat16)

    def split_heads(block):
        return block.reshape(row_count, HEADS, head_width).transpose(1, 0, 2)

    def join_heads(block):
        return block.transpose(1, 0, 2).reshape(row_count, model_width)

    query_heads = split_heads(projected[:, :model_width])
    key_heads = split_heads(projected[:, model_width : 2 * model_width])
    value_heads = split_heads(projected[:, 2 * model_width :])

    def forward_head(operands):
        query_head, key_head, value_head = operands
        scores = contract(query_head, key_head, 1, 1) * score_scale
        scores = jnp.where(same_item, scores, -1e30)
        top_score = jnp.max(scores, axis=1, keepdims=True)
        expon = jnp.exp(scores - top_score)
        total = jnp.sum(expon, axis=1, keepdims=True)
        weights_low = (expon / total).astype(jnp.bfloat16)
        result = jnp.dot(weights_low, value_head, preferred_element_type=jnp.float32)
        return (result, (top_score + jnp.log(total))[:, 0])

    attended_heads, log_totals = lax.map(forward_head, (query_heads, key_heads, value_heads))
    attended = join_heads(attended_heads).astype(jnp.bfloat16)
    middle = (
        start
        + jnp.dot(attended, full_out, preferred_element_type=jnp.float32)
        + out_bias.astype(jnp.float32)
    )
    normed_two = layer_norm(middle, gain_two, shift_two).astype(jnp.bfloat16)
    hidden_pre = jnp.dot(normed_two, full_up, preferred_element_type=jnp.float32) + up_bias.astype(
        jnp.float32
    )
    activated = gelu_exact(hidden_pre).astype(jnp.bfloat16)
    feed_out = jnp.dot(activated, full_down, preferred_element_type=jnp.float32) + down_bias.astype(
        jnp.float32
    )
    output = (middle + feed_out).astype(jnp.bfloat16)
    back_qkv, back_out, back_up, back_down = (
        lax.all_gather(w_qkv, ("dp", "fsdp"), axis=0, tiled=True),
        lax.all_gather(w_out, ("dp", "fsdp"), axis=0, tiled=True),
        lax.all_gather(w_up, ("dp", "fsdp"), axis=0, tiled=True),
        lax.all_gather(w_down, ("dp", "fsdp"), axis=0, tiled=True),
    )
    grad_output = cotangent.astype(jnp.float32)
    grad_down_bias = jnp.sum(grad_output, axis=0)
    grad_down = contract(activated, cotangent, 0, 0)
    grad_act = contract(cotangent, back_down, 1, 1)
    gelu_value, gelu_pull = jax.vjp(gelu_exact, hidden_pre)
    grad_hidden = gelu_pull(grad_act)[0].astype(jnp.bfloat16)
    grad_up_bias = jnp.sum(grad_hidden.astype(jnp.float32), axis=0)
    grad_up = contract(normed_two, grad_hidden, 0, 0)
    grad_normed_two = contract(grad_hidden, back_up, 1, 1)
    norm_value, second_pull = jax.vjp(layer_norm, middle, gain_two, shift_two)
    grad_middle_part, grad_gain_two, grad_shift_two = second_pull(grad_normed_two)
    grad_middle = grad_output + grad_middle_part
    branch_grad = grad_middle.astype(jnp.bfloat16)
    grad_out_bias = jnp.sum(branch_grad.astype(jnp.float32), axis=0)
    grad_out_weight = contract(attended, branch_grad, 0, 0)
    grad_attended = contract(branch_grad, back_out, 1, 1).astype(jnp.bfloat16)
    grad_heads = split_heads(grad_attended)

    def backward_head(operands):
        query_head, key_head, value_head, grad_head, log_total = operands
        scores = contract(query_head, key_head, 1, 1) * score_scale
        weights = jnp.where(same_item, jnp.exp(scores - log_total[:, None]), 0.0)
        weights_low = weights.astype(jnp.bfloat16)
        grad_weights = contract(grad_head, value_head, 1, 1)
        grad_value = contract(weights_low, grad_head, 0, 0)
        grad_scores = weights * (
            grad_weights - jnp.sum(weights * grad_weights, axis=1, keepdims=True)
        )
        grad_scores_low = grad_scores.astype(jnp.bfloat16)
        grad_query = (
            jnp.dot(grad_scores_low, key_head, preferred_element_type=jnp.float32) * score_scale
        )
        grad_key = contract(grad_scores_low, query_head, 0, 0) * score_scale
        return (grad_query, grad_key, grad_value)

    grad_query_heads, grad_key_heads, grad_value_heads = lax.map(
        backward_head, (query_heads, key_heads, value_heads, grad_heads, log_totals)
    )
    grad_projected = jnp.concatenate(
        [join_heads(grad_query_heads), join_heads(grad_key_heads), join_heads(grad_value_heads)],
        axis=1,
    ).astype(jnp.bfloat16)
    grad_query_bias = jnp.sum(grad_projected[:, :model_width].astype(jnp.float32), axis=0)
    grad_value_bias = jnp.sum(grad_projected[:, 2 * model_width :].astype(jnp.float32), axis=0)
    grad_qkv = contract(normed_one, grad_projected, 0, 0)
    grad_normed_one = contract(grad_projected, back_qkv, 1, 1)
    first_value, first_pull = jax.vjp(layer_norm, start, gain_one, shift_one)
    grad_start_part, grad_gain_one, grad_shift_one = first_pull(grad_normed_one)
    grad_tokens = (grad_middle + grad_start_part).astype(jnp.bfloat16)
    every_grad = (
        lax.psum_scatter(grad_qkv, ("dp", "fsdp"), scatter_dimension=0, tiled=True),
        lax.psum_scatter(grad_out_weight, ("dp", "fsdp"), scatter_dimension=0, tiled=True),
        lax.psum_scatter(grad_up, ("dp", "fsdp"), scatter_dimension=0, tiled=True),
        lax.psum_scatter(grad_down, ("dp", "fsdp"), scatter_dimension=0, tiled=True),
        lax.psum_scatter(grad_gain_one, ("dp", "fsdp"), scatter_dimension=0, tiled=True),
        lax.psum_scatter(grad_shift_one, ("dp", "fsdp"), scatter_dimension=0, tiled=True),
        lax.psum_scatter(grad_query_bias, ("dp", "fsdp"), scatter_dimension=0, tiled=True),
        lax.psum_scatter(grad_value_bias, ("dp", "fsdp"), scatter_dimension=0, tiled=True),
        lax.psum_scatter(grad_out_bias, ("dp", "fsdp"), scatter_dimension=0, tiled=True),
        lax.psum_scatter(grad_gain_two, ("dp", "fsdp"), scatter_dimension=0, tiled=True),
        lax.psum_scatter(grad_shift_two, ("dp", "fsdp"), scatter_dimension=0, tiled=True),
        lax.psum_scatter(grad_up_bias, ("dp", "fsdp"), scatter_dimension=0, tiled=True),
        lax.psum_scatter(grad_down_bias, ("dp", "fsdp"), scatter_dimension=0, tiled=True),
    )
    (
        shard_qkv,
        shard_out,
        shard_up,
        shard_down,
        shard_gain_one,
        shard_shift_one,
        shard_query_bias,
        shard_value_bias,
        shard_out_bias,
        shard_gain_two,
        shard_shift_two,
        shard_up_bias,
        shard_down_bias,
    ) = every_grad
    return (
        output,
        grad_tokens,
        shard_qkv,
        shard_out,
        shard_up,
        shard_down,
        shard_gain_one,
        shard_shift_one,
        shard_query_bias,
        shard_value_bias,
        shard_out_bias,
        shard_gain_two,
        shard_shift_two,
        shard_up_bias,
        shard_down_bias,
    )


PLANE = 2
CORES = 2
UNIT = 1024 * 1024
MESH = pl.DeviceIdType.MESH
ALL = slice(None)


class Place:
    def __init__(self, depth):
        dp, fsdp = lax.axis_index("dp"), lax.axis_index("fsdp")
        self.y, self.x = dp // PLANE, lax.rem(dp, PLANE)
        self.z, self.c = fsdp // CORES, lax.rem(fsdp, CORES)
        self.depth = depth
        y, x, z, c = self.y, self.x, self.z, self.c
        self.along_x = self.device(y, 1 - x, z, c)
        self.along_y = self.device(1 - y, x, z, c)
        self.other_core = self.device(y, x, z, 1 - c)
        self.ahead = [lax.rem(z + k, depth) for k in range(1, depth)]
        self.behind = [lax.rem(z + depth - k, depth) for k in range(1, depth)]

    def device(self, y, x, z, c):
        return (y * PLANE + x, z * CORES + c)

    def column(self, z):
        return self.device(self.y, self.x, z, self.c)

    def greet(self):
        partners = [self.column(q) for q in self.ahead]
        partners += [self.along_x, self.along_y, self.other_core]
        barrier = pltpu.get_barrier_semaphore()
        for partner in partners:
            pl.semaphore_signal(barrier, inc=1, device_id=partner, device_id_type=MESH)
        pl.semaphore_wait(barrier, len(partners))


class Mail:
    def __init__(self, send_sem, recv_sem):
        self.send_sem, self.recv_sem, self.sent = send_sem, recv_sem, {}

    def copy(self, unit, slot, source, target, device):
        return pltpu.make_async_remote_copy(
            src_ref=source,
            dst_ref=target,
            send_sem=self.send_sem.at[unit, slot],
            recv_sem=self.recv_sem.at[unit, slot],
            device_id=device,
            device_id_type=MESH,
        )

    def send(self, unit, slot, source, target, device):
        copy = self.copy(unit, slot, source, target, device)
        copy.start()
        self.sent[unit, slot] = copy

    def arrived(self, unit, slot, target, device):
        self.copy(unit, slot, target, target, device).wait_recv()

    def settle(self, unit, slot):
        self.sent.pop((unit, slot)).wait_send()

    def finish(self):
        for at in list(self.sent):
            self.settle(*at)


SLOTS = 14


def unit_list(shapes):
    units = []
    for index, (rows, columns) in enumerate(shapes):
        width = UNIT // rows
        units += [(index, first, width) for first in range(0, columns, width)]
    return units


def small_gather_phases(place, mail, unit, source, full, local_sem):
    y, x, z, c = place.y, place.x, place.z, place.c
    nz = place.depth - 1

    def first():
        pltpu.make_async_copy(source, full.at[y, x, z, c], local_sem).start()
        for k in range(nz):
            mail.send(unit, k, source, full.at[y, x, z, c], place.column(place.ahead[k]))

    def second():
        pltpu.make_async_copy(source, full.at[y, x, z, c], local_sem).wait()
        for k in range(nz):
            q = place.behind[k]
            mail.arrived(unit, k, full.at[y, x, q, c], place.column(q))
        mail.send(unit, 3, full.at[y, x, :, c], full.at[y, x, :, c], place.along_x)

    def third():
        mail.arrived(unit, 3, full.at[y, 1 - x, :, c], place.along_x)
        mail.send(unit, 5, full.at[y, :, :, c], full.at[y, :, :, c], place.along_y)

    def fourth():
        mail.arrived(unit, 5, full.at[1 - y, :, :, c], place.along_y)
        mail.send(unit, 7, full.at[:, :, :, c], full.at[:, :, :, c], place.other_core)

    def last():
        mail.arrived(unit, 7, full.at[:, :, :, 1 - c], place.other_core)

    return first, second, third, fourth, last


def by_rows(left, right):
    return contract(left, right, 1, 1)


def by_columns(left, right):
    return contract(left, right, 0, 0)


def plain(left, right):
    return jnp.dot(left, right, preferred_element_type=jnp.float32)


class Table:
    GAIN_ONE, SHIFT_ONE, QUERY, VALUE, OUT, GAIN_TWO, SHIFT_TWO, DOWN = range(8)

    def __init__(self, packed, narrow, wide):
        self.packed, self.narrow, self.wide = packed, narrow, wide

    def expand(self, devices):
        y_count, x_count, z_count, c_count = self.packed.shape[:4]

        def tile(d):
            d, c = divmod(d, c_count)
            d, z = divmod(d, z_count)
            y, x = divmod(d, x_count)
            return self.packed[y, x, z, c]

        group = lax.broadcasted_iota(jnp.int32, (8, 128), 1) // 32
        for base in range(0, devices, 4):
            tiles = [tile(base + i) for i in range(4)]
            for i in range(4):
                self.wide[:, pl.ds(128 * (base + i), 128)] = tiles[i][0:1, :]
            for q in range(4):
                mixed = jnp.zeros((8, 128), jnp.float32)
                for i in range(4):
                    turned = tiles[i] if i == q else pltpu.roll(tiles[i], 32 * ((i - q) % 4), 1)
                    mixed = jnp.where(group == i, turned, mixed)
                self.narrow[q, :, pl.ds(32 * base, 128)] = mixed

    def __getitem__(self, index):
        return self.narrow[index % 4, 1 + index // 4 : 2 + index // 4, :]


def row_facts(lengths, codes, row):
    begin = jnp.int32(0)
    segment = jnp.zeros(row.shape, jnp.int32)
    first = jnp.zeros(row.shape, jnp.int32)
    code = jnp.full(row.shape, codes[0, 0], jnp.int32)
    for item in range(1, lengths.shape[1]):
        begin = begin + lengths[0, item - 1]
        inside = row >= begin
        segment = jnp.where(inside, item, segment)
        first = jnp.where(inside, begin, first)
        code = jnp.where(inside, codes[0, item], code)
    return segment, (row - first).astype(jnp.float32) * (0.5 * (code.astype(jnp.float32) + 1.0))


def fill_mask(lengths, codes, mask):
    rows = mask.shape[0]
    across, _ = row_facts(lengths, codes, lax.broadcasted_iota(jnp.int32, (1, rows), 1))
    for base in range(0, rows, 128):
        down, _ = row_facts(lengths, codes, lax.broadcasted_iota(jnp.int32, (128, 1), 0) + base)
        mask[base : base + 128, :] = jnp.where(down == across, 0.0, -1e30)


def head_half(rows, which):
    lane = lax.broadcasted_iota(jnp.int32, (rows, 2 * HEAD_DIM), 1)
    return (lane >= HEAD_DIM) if which else (lane < HEAD_DIM)


def pair_span(pair, offset):
    return pl.ds(pl.multiple_of(offset + pair * 2 * HEAD_DIM, 2 * HEAD_DIM), 2 * HEAD_DIM)


def attend(first_pair, last_pair, projected, mask, attended):
    rows, width = attended.shape
    zero = jnp.zeros((), jnp.bfloat16)
    scale = jnp.asarray(1.0 / math.sqrt(HEAD_DIM), jnp.bfloat16)

    def one_pair(pair, carry):
        query = projected[:, pair_span(pair, 0)] * scale
        key = projected[:, pair_span(pair, width)]
        value = projected[:, pair_span(pair, 2 * width)]
        results = []
        for which in range(2):
            scores = by_rows(jnp.where(head_half(rows, which), query, zero), key) + mask[...]
            top = jnp.max(scores, axis=1, keepdims=True)
            expon = jnp.exp(scores - top)
            total = jnp.sum(expon, axis=1, keepdims=True)
            weights = (expon * (1.0 / total)).astype(jnp.bfloat16)
            results.append(plain(weights, value))
        mixed = jnp.where(head_half(rows, 0), results[0], results[1])
        attended[:, pair_span(pair, 0)] = mixed.astype(jnp.bfloat16)
        return carry

    lax.fori_loop(first_pair, last_pair, one_pair, 0)


CHUNK = 64


def over_rows(rows, step):
    def one(index, carry):
        step(pl.ds(pl.multiple_of(index * CHUNK, CHUNK), CHUNK), index * CHUNK)
        return carry

    lax.fori_loop(0, rows // CHUNK, one, 0)


def normalised(values):
    centred = values - jnp.mean(values, axis=-1, keepdims=True)
    variance = jnp.mean(centred * centred, axis=-1, keepdims=True)
    scale = lax.rsqrt(variance + EPSILON)
    return centred * scale, scale


def attend_back(first_pair, last_pair, projected, mask, grad_attended, sums, weights_low, grad_low):
    rows, width = grad_attended.shape
    zero = jnp.zeros((), jnp.bfloat16)
    scale = 1.0 / math.sqrt(HEAD_DIM)

    def one_pair(pair, carry):
        query, key, value = (projected[:, pair_span(pair, k * width)] for k in range(3))
        grad = grad_attended[:, pair_span(pair, 0)]
        scaled = query * jnp.asarray(scale, jnp.bfloat16)
        g_query, g_key, g_value = [], [], []
        for which in range(2):
            keep = head_half(rows, which)
            scores = by_rows(jnp.where(keep, key, zero), scaled) + mask[...]
            expon = jnp.exp(scores - jnp.max(scores, axis=0, keepdims=True))
            weights = expon * (1.0 / jnp.sum(expon, axis=0, keepdims=True))
            weights_low[which] = weights.astype(jnp.bfloat16)
            slopes = by_rows(jnp.where(keep, value, zero), grad)
            level = jnp.sum(weights * slopes, axis=0, keepdims=True)
            grad_low[which] = (weights * (slopes - level)).astype(jnp.bfloat16)
            g_value.append(plain(weights_low[which], grad))
            g_key.append(plain(grad_low[which], query))
            g_query.append(by_columns(grad_low[which], key))
        keep = head_half(rows, 0)
        for k, (parts, factor) in enumerate(((g_query, scale), (g_key, scale), (g_value, 1.0))):
            mixed = (jnp.where(keep, parts[0], parts[1]) * factor).astype(jnp.bfloat16)
            projected[:, pair_span(pair, k * width)] = mixed
            if k != 1:
                slot = Table.QUERY if k == 0 else Table.VALUE
                total = jnp.sum(mixed.astype(jnp.float32), axis=0, keepdims=True)
                sums[slot % 4, 1 + slot // 4 : 2 + slot // 4, pair_span(pair, 0)] = total
        return carry

    lax.fori_loop(first_pair, last_pair, one_pair, 0)


def gather_phases(place, mail, unit, kind, source, full, local_sem):
    y, x, z, c = place.y, place.x, place.z, place.c
    nz = place.depth - 1

    def begin():
        pltpu.make_async_copy(source, full(y, x, z, c, ALL), local_sem).start()
        for k in range(nz):
            mail.send(unit, k, source, full(y, x, z, c, ALL), place.column(place.ahead[k]))
        if kind:
            mail.send(unit, 3, source.at[0], full(y, x, z, c, 0), place.along_x)
            mail.send(unit, 4, source.at[1], full(y, x, z, c, 1), place.along_y)

    def second():
        pltpu.make_async_copy(source, full(y, x, z, c, ALL), local_sem).wait()
        if kind:
            for slot, partner, block in (
                (3, place.along_x, full(y, 1 - x, z, c, 0)),
                (4, place.along_y, full(1 - y, x, z, c, 1)),
            ):
                mail.arrived(unit, slot, block, partner)
                for k in range(nz):
                    mail.send(unit, 8 + 3 * (slot - 3) + k, block, block, place.column(place.ahead[k]))
            return
        for k in range(nz):
            q = place.behind[k]
            mail.arrived(unit, k, full(y, x, q, c, ALL), place.column(q))
        mail.send(unit, 3, full(y, x, ALL, c, 0), full(y, x, ALL, c, 0), place.along_x)
        mail.send(unit, 4, full(y, x, ALL, c, 1), full(y, x, ALL, c, 1), place.along_y)

    def third():
        if kind:
            for k in range(nz):
                q = place.behind[k]
                mail.arrived(unit, k, full(y, x, q, c, ALL), place.column(q))
            for k in range(nz):
                q = place.behind[k]
                mail.arrived(unit, 8 + k, full(y, 1 - x, q, c, 0), place.column(q))
        else:
            mail.arrived(unit, 3, full(y, 1 - x, ALL, c, 0), place.along_x)
        mail.send(unit, 5, full(y, ALL, ALL, c, 0), full(y, ALL, ALL, c, 0), place.along_y)
        if kind:
            for k in range(nz):
                q = place.behind[k]
                mail.arrived(unit, 11 + k, full(1 - y, x, q, c, 1), place.column(q))
        else:
            mail.arrived(unit, 4, full(1 - y, x, ALL, c, 1), place.along_y)
        mail.send(unit, 6, full(ALL, x, ALL, c, 1), full(ALL, x, ALL, c, 1), place.along_x)

    def fourth():
        mail.arrived(unit, 5, full(1 - y, ALL, ALL, c, 0), place.along_y)
        mail.arrived(unit, 6, full(ALL, 1 - x, ALL, c, 1), place.along_x)
        mail.send(unit, 7, full(ALL, ALL, ALL, c, ALL), full(ALL, ALL, ALL, c, ALL), place.other_core)

    def last():
        mail.arrived(unit, 7, full(ALL, ALL, ALL, 1 - c, ALL), place.other_core)

    return begin, second, third, fourth, last


class Sum:
    def __init__(self, place, mail, unit, kind, part, held, wide, late):
        self.place, self.mail, self.unit, self.kind = place, mail, unit, kind
        self.part, self.held, self.wide, self.late = part, held, wide, late
        self.nz = place.depth - 1

    def first(self):
        p = self.place
        self.mail.send(self.unit, 7, self.part.at[:, :, :, 1 - p.c], self.held, p.other_core)

    def second(self):
        p, mail, unit, held = self.place, self.mail, self.unit, self.held
        mail.arrived(unit, 7, held, p.other_core)
        for a in range(PLANE):
            for b in range(PLANE):
                held[a, b] = held[a, b] + self.part[a, b, :, p.c]
        mail.send(unit, 5, held.at[1 - p.y, :, :, 0], self.wide.at[0], p.along_y)
        mail.send(unit, 6, held.at[:, 1 - p.x, :, 1], self.wide.at[1], p.along_x)
        mail.settle(unit, 7)

    def pair(self, half, k):
        return self.late.at[pl.ds(2 * (self.nz * half + k), 2)]

    def near(self, half):
        depth = self.nz + 1
        return self.late.at[pl.ds(depth * half, depth)]

    def column(self, k):
        return self.late.at[pl.ds(2 * (self.nz + 1) + 2 * k, 2)]

    def final(self, half):
        return self.late.at[4 * self.nz + half]

    def third(self):
        p, mail, unit, held, wide = self.place, self.mail, self.unit, self.held, self.wide
        y, x = p.y, p.x
        mail.arrived(unit, 5, wide.at[0], p.along_y)
        for b in range(PLANE):
            held[y, b, :, 0] = held[y, b, :, 0] + wide[0, b]
        if self.kind:
            for k in range(self.nz):
                q = p.ahead[k]
                mail.send(unit, 8 + k, held.at[y, :, q, 0], self.pair(0, k), p.column(q))
        else:
            mail.send(unit, 3, held.at[y, 1 - x, :, 0], self.near(0), p.along_x)
        mail.arrived(unit, 6, wide.at[1], p.along_x)
        for b in range(PLANE):
            held[b, x, :, 1] = held[b, x, :, 1] + wide[1, b]
        if self.kind:
            for k in range(self.nz):
                q = p.ahead[k]
                mail.send(unit, 11 + k, held.at[:, x, q, 1], self.pair(1, k), p.column(q))
        else:
            mail.send(unit, 4, held.at[1 - y, x, :, 1], self.near(1), p.along_y)

    def fourth(self):
        p, mail, unit, held = self.place, self.mail, self.unit, self.held
        y, x, z = p.y, p.x, p.z
        full = jnp.float32
        if self.kind:
            for half in range(2):
                at = (y, ALL, z, 0) if half == 0 else (ALL, x, z, 1)
                total = held[at].astype(full)
                for k in range(self.nz):
                    mail.arrived(unit, 8 + 3 * half + k, self.pair(half, k), p.column(p.behind[k]))
                    total = total + self.pair(half, k)[...].astype(full)
                held[at] = total.astype(held.dtype)
            mail.send(unit, 3, held.at[y, 1 - x, z, 0], self.final(0), p.along_x)
            mail.send(unit, 4, held.at[1 - y, x, z, 1], self.final(1), p.along_y)
            return
        mail.arrived(unit, 3, self.near(0), p.along_x)
        mail.arrived(unit, 4, self.near(1), p.along_y)
        for half in range(2):
            held[y, x, :, half] = held[y, x, :, half] + self.near(half)[...]
        for k in range(self.nz):
            q = p.ahead[k]
            mail.send(unit, k, held.at[y, x, q], self.column(k), p.column(q))

    def last(self):
        p, mail, unit, held = self.place, self.mail, self.unit, self.held
        full = jnp.float32
        halves = [held[p.y, p.x, p.z, half].astype(full) for half in range(2)]
        if self.kind:
            mail.arrived(unit, 3, self.final(0), p.along_x)
            mail.arrived(unit, 4, self.final(1), p.along_y)
            halves = [v + self.final(half)[...].astype(full) for half, v in enumerate(halves)]
        else:
            for k in range(self.nz):
                mail.arrived(unit, k, self.column(k), p.column(p.behind[k]))
                halves = [v + self.column(k)[half].astype(full) for half, v in enumerate(halves)]
        for slot in [s for u, s in list(mail.sent) if u == unit]:
            mail.settle(unit, slot)
        return halves


INBOXES = 6
HELD = 4
TILE = 256
GATHER_KINDS = (0, 0, 0, 0, 0, 1, 0, 1, 0, 1, 0, 1)
SUM_KINDS = (0, 1, 0, 1, 0, 1, 0, 1, 0, 0, 0, 0)
ORDER = (
    ("g", 0, 0), ("g", 0, 1), ("g", 1, 0), ("g", 0, 2), ("g", 2, 0), ("g", 1, 1), ("g", 3, 0), ("g", 1, 2),
    ("g", 2, 1), ("g", 4, 0), ("g", 3, 1), ("g", 5, 0), ("g", 6, 0), ("g", 2, 2), ("g", 0, 3), ("g", 3, 2),
    ("g", 5, 1), ("prepare",), ("g", 6, 1), ("g", 7, 0), ("g", 4, 1), ("g", 0, 4), ("g", 2, 3), ("g", 7, 1),
    ("g", 5, 2), ("norm1",), ("g", 3, 3), ("g", 6, 2), ("g", 1, 3), ("project", 0), ("g", 4, 2), ("g", 8, 0),
    ("g", 1, 4), ("project", 1), ("g", 2, 4), ("project", 2), ("g", 3, 4), ("g", 9, 0), ("attend", 0), ("g", 8, 1),
    ("g", 7, 2), ("g", 10, 0), ("attend", 1), ("g", 6, 3), ("g", 11, 0), ("g", 4, 3), ("g", 10, 1), ("norm2",),
    ("g", 9, 1), ("g", 8, 2), ("g", 6, 4), ("g", 4, 4), ("g", 5, 3), ("rise", 0), ("g", 7, 3), ("g", 5, 4),
    ("g", 10, 2), ("rise", 1), ("g", 11, 1), ("rise", 2), ("g", 9, 2), ("g", 7, 4), ("g", 8, 3), ("rise", 3),
    ("part", 0), ("g", 10, 3), ("s", 0, 0), ("g", 11, 2), ("part", 1), ("s", 1, 0), ("g", 8, 4), ("part", 2),
    ("fall", 0), ("g", 9, 3), ("part", 3), ("s", 1, 1), ("g", 10, 4), ("g", 9, 4), ("s", 2, 0), ("fall", 1),
    ("g", 11, 3), ("s", 0, 1), ("s", 3, 0), ("fall", 2), ("g", 11, 4), ("fall", 3), ("hidden", 0), ("s", 2, 1),
    ("hidden", 1), ("s", 1, 2), ("part", 4), ("hidden", 2), ("s", 4, 0), ("hidden", 3), ("s", 0, 2), ("part", 5),
    ("s", 3, 1), ("s", 5, 0), ("s", 2, 2), ("part", 6), ("up", 0), ("up", 1), ("s", 0, 3), ("up", 2), ("up", 3),
    ("s", 4, 1), ("part", 7), ("s", 2, 3), ("s", 5, 1), ("branch",), ("s", 1, 3), ("out",), ("s", 0, 4), ("s", 6, 0),
    ("s", 3, 2), ("heads", 0), ("s", 6, 1), ("s", 1, 4), ("heads", 1), ("s", 2, 4), ("s", 7, 0), ("part", 8),
    ("s", 8, 0), ("s", 4, 2), ("s", 5, 2), ("s", 7, 1), ("s", 3, 3), ("s", 8, 1), ("heads", 2), ("s", 4, 3),
    ("again",), ("heads", 3), ("s", 6, 2), ("part", 9), ("s", 3, 4), ("s", 9, 0), ("s", 7, 2), ("s", 8, 2),
    ("s", 9, 1), ("s", 4, 4), ("part", 10), ("s", 10, 0), ("part", 11), ("s", 5, 3), ("s", 6, 3), ("s", 8, 3),
    ("s", 10, 1), ("s", 5, 4), ("s", 11, 0), ("qkv", 0), ("s", 9, 2), ("qkv", 1), ("qkv", 2), ("s", 11, 1),
    ("qkv", 3), ("s", 9, 3), ("s", 10, 2), ("s", 6, 4), ("tokens",), ("s", 11, 2), ("s", 10, 3), ("pack",),
    ("s", 7, 3), ("s", 12, 0), ("s", 11, 3), ("s", 12, 1), ("s", 12, 2), ("s", 12, 3), ("s", 8, 4), ("s", 10, 4),
    ("s", 12, 4), ("s", 7, 4), ("s", 9, 4), ("s", 11, 4),
)


def layer_kernel(depth, units, sums_units, *refs):
    refs = list(refs)

    def take(count):
        taken = refs[:count]
        del refs[:count]
        return taken

    sources = take(4)
    vectors = take(9)
    tokens, cotangent, lengths, codes = take(4)
    fulls = take(4)
    a_projected, a_attended, a_start = take(3)
    o_output, o_tokens = take(2)
    outs = take(4)
    (o_small,) = take(1)
    small, packed, narrow, wide = take(4)
    inbox, wide_in, late_in, r_square, r_tall, parts = take(6)
    s_part, s_core, s_wide, s_near, s_column, s_result = take(6)
    big, hidden_grad, square, tall, stream, grad_middle, grad_normed = take(7)
    normed, branch, grad_attended, finished, weights_low, grad_low, mask, sums, wide_sums = take(9)
    send_sem, recv_sem, local_sem, load_sem, store_sem, free_sem = take(6)

    place, mail = Place(depth), Mail(send_sem, recv_sem)
    y, x, z, c = place.y, place.x, place.z, place.c
    nz = depth - 1
    rows, width = stream.shape
    hidden = hidden_grad.shape[1]
    pairs = width // (2 * HEAD_DIM)
    low, full = jnp.bfloat16, jnp.float32
    table = Table(packed, narrow, wide)
    projected, attended = big.at[:, pl.ds(0, 3 * width)], big.at[:, pl.ds(3 * width, width)]
    corners = [(a, b) for a in range(PLANE) for b in range(PLANE)]
    stores, numbers = {}, iter(range(64))

    def store(name, source, target):
        copy = pltpu.make_async_copy(source, target, store_sem.at[len(stores)])
        copy.start()
        stores[name] = [copy, True]

    def stored(name):
        if stores[name][1]:
            stores[name][0].wait()
            stores[name][1] = False

    def load(source, target):
        return pltpu.make_async_copy(source, target, load_sem.at[next(numbers)])

    def flat(block):
        return block.reshape(-1, block.shape[-1])

    def pack_vectors():
        narrow[...] = jnp.zeros_like(narrow)
        count = vectors[0].shape[0]
        for k, ref in enumerate(vectors[:-1]):
            narrow[k % 4, k // 4 : k // 4 + 1, 0:count] = ref[...].astype(full).reshape(1, count)
        small[...] = jnp.zeros_like(small)
        small[0:1, :] = vectors[-1][...].astype(full).reshape(1, 128)
        for line in range(2):
            total = narrow[0, line : line + 1, 0:128]
            for q in range(1, 4):
                total = total + pltpu.roll(narrow[q, line : line + 1, 0:128], count * q, 1)
            small[1 + line : 2 + line, :] = total

    def piece(unit):
        index, first, columns = units[unit]
        span = pl.ds(first, columns)

        def view(*at):
            return fulls[index].at[at + (ALL, span)]

        return sources[index].at[:, :, span], view

    gathers = [
        gather_phases(place, mail, unit + 1, GATHER_KINDS[unit], *piece(unit), local_sem.at[unit + 1])
        for unit in range(len(units))
    ]
    small_gather = small_gather_phases(place, mail, 0, small, packed, local_sem.at[0])
    places = []
    for unit, (index, first, columns) in enumerate(units):
        buffer = tall if index == 3 else square
        places.append((buffer, sum((u[0] == 3) == (index == 3) for u in units[:unit]) % 2))
    loads = [
        load(piece(unit)[1](ALL, ALL, ALL, ALL, ALL), buffer.at[at])
        for unit, (buffer, at) in enumerate(places)
    ]

    def weights(unit, columns):
        buffer, at = places[unit]
        return flat(buffer[at, :, :, :, :, :, :, columns])

    def corner_loads(index, corner, buffer, at):
        a, b = corners[corner]
        chosen = [u for u in units if u[0] == index]
        return [
            load(
                fulls[index].at[a, b, :, :, :, :, pl.ds(first, columns)],
                buffer.at[at, e // PLANE, e % PLANE],
            )
            for e, (_, first, columns) in enumerate(chosen)
        ]

    get_down = [corner_loads(3, n, tall, n % 2) for n in range(4)]
    get_up = [corner_loads(2, n, square, n % 2) for n in range(4)]
    get_out = [
        load(fulls[1].at[a, b], square.at[0, n // PLANE, n % PLANE]) for n, (a, b) in enumerate(corners)
    ]
    get_qkv = [corner_loads(0, n, square, (n + 1) % 2) for n in range(4)]
    get_projected = load(a_projected, projected)
    get_attended = load(a_attended, attended)
    get_start = load(a_start, stream)

    def start_all(copies):
        for copy in copies:
            copy.start()

    def wait_all(copies):
        for copy in copies:
            copy.wait()

    get_tokens = load(tokens, finished)

    def prepare():
        get_tokens.wait()
        def chunk(span, base):
            row = lax.broadcasted_iota(jnp.int32, (CHUNK, 1), 0) + base
            _, factor = row_facts(lengths, codes, row)
            lane = lax.broadcasted_iota(jnp.int32, (1, width // 2), 1).astype(full)
            phase = factor * jnp.exp(lane * (-math.log(10000.0) / (width // 2)))
            left, right = pl.ds(0, width // 2), pl.ds(width // 2, width // 2)
            stream[span, left] = finished[span, left].astype(full) + jnp.sin(phase)
            stream[span, right] = finished[span, right].astype(full) + jnp.cos(phase)

        over_rows(rows, chunk)
        store("start", stream, a_start)
        fill_mask(lengths, codes, mask)
        sums[...] = jnp.zeros_like(sums)

    def norm(gain, shift):
        def chunk(span, base):
            normed[span, :] = (normalised(stream[span, :])[0] * table[gain] + table[shift]).astype(low)

        over_rows(rows, chunk)

    def project(unit, bias):
        tile = 512
        for first in range(0, width, tile):
            value = plain(normed[...], weights(unit, pl.ds(first, tile)))
            if bias is not None:
                value = value + table[bias][:, first : first + tile]
            big[:, pl.ds(unit * width + first, tile)] = value.astype(low)

    def project_out(unit):
        tile = 512
        stored("start")
        for first in range(0, width, tile):
            span = pl.ds(first, tile)
            value = plain(attended[...], weights(unit, span)) + table[Table.OUT][:, first : first + tile]
            stream[:, span] = stream[:, span] + value

    def rise(unit, number):
        def one(index, carry):
            at = pl.multiple_of(index * TILE, TILE)
            there = pl.ds(pl.multiple_of(number * width + at, TILE), TILE)
            pre = plain(normed[...], weights(unit, pl.ds(at, TILE))) + wide[:, there]
            normal = 0.5 * (1.0 + lax.erf(pre * math.sqrt(0.5)))
            density = jnp.exp(pre * pre * -0.5) * (1.0 / math.sqrt(2.0 * math.pi))
            big[:, there] = (pre * normal).astype(low)
            hidden_grad[:, there] = (normal + pre * density).astype(low)
            return carry

        lax.fori_loop(0, width // TILE, one, 0)

    def fall(unit, number, columns):
        span = pl.ds(number * columns, columns)
        value = plain(big[...], weights(unit, ALL)) + table[Table.DOWN][:, number * columns : (number + 1) * columns]
        finished[:, span] = (stream[:, span] + value).astype(low)

    def tally(slot, values):
        at = (slot % 4, pl.ds(1 + slot // 4, 1), ALL)
        sums[at] = sums[at] + jnp.sum(values, axis=0, keepdims=True)

    def square_part(unit, left, right, first):
        for k in range(width // TILE):
            value = by_columns(left[...], right[:, pl.ds(first + TILE * k, TILE)]).astype(low)
            parts[unit % HELD, :, :, :, :, :, k] = value.reshape(parts.shape[1:6] + (parts.shape[7], TILE))

    def tall_part(unit, first):
        def one(corner, carry):
            left = big[:, pl.ds(pl.multiple_of(corner * width, width), width)]
            value = by_columns(left, cotangent[:, pl.ds(first, TILE)]).astype(low)
            parts[unit % HELD, corner // PLANE, lax.rem(corner, PLANE)] = value.reshape(parts.shape[3:])
            return carry

        lax.fori_loop(0, PLANE * PLANE, one, 0)

    def part_of(unit):
        index, first, columns = sums_units[unit]
        if index == 3:
            tall_part(unit, first)
        elif index == 2:
            square_part(unit, normed, hidden_grad, first)
        elif index == 1:
            square_part(unit, attended, branch, 0)
        else:
            square_part(unit, normed, big, first)

    def hidden_step(n):
        wait_all(get_down[n])

        def one(m, carry):
            block = jnp.concatenate(
                [flat(tall[n % 2, e // PLANE, e % PLANE, m]) for e in range(4)], axis=1
            )
            span = pl.ds(pl.multiple_of(n * width + m * TILE, TILE), TILE)
            value = (by_rows(cotangent[...], block) * hidden_grad[:, span].astype(full)).astype(low)
            hidden_grad[:, span] = value
            wide_sums[:, span] = jnp.sum(value.astype(full), axis=0, keepdims=True)
            return carry

        lax.fori_loop(0, width // TILE, one, 0)
        if n + 2 < 4:
            start_all(get_down[n + 2])

    def back_through(copies, left, at, n):
        wait_all(copies)
        total = None
        for e in range(len(copies)):
            value = by_rows(left[:, pl.ds(e * width, width)], flat(square[at, e // PLANE, e % PLANE]))
            total = value if total is None else total + value
        grad_normed[:, pl.ds(TILE * n, TILE)] = total

    def up_step(n):
        back_through(get_up[n], hidden_grad, n % 2, n)
        if n + 2 < 4:
            start_all(get_up[n + 2])
        if n == 2:
            start_all(get_out)
        if n == 3:
            start_all(get_qkv[0])

    def out_step():
        wait_all(get_out)
        for n in range(4):
            block = flat(square[0, n // PLANE, n % PLANE])
            grad_attended[:, pl.ds(TILE * n, TILE)] = by_rows(branch[...], block).astype(low)
        start_all(get_qkv[1])

    def qkv_step(n):
        back_through(get_qkv[n], big, (n + 1) % 2, n)
        if n + 2 < 4:
            start_all(get_qkv[n + 2])

    def norm_back(span, gain, shift):
        level, scale = normalised(stream[span, :])
        grad = grad_normed[span, :]
        tally(gain, grad * level)
        tally(shift, grad)
        grad = grad * table[gain]
        mean = jnp.mean(grad, axis=-1, keepdims=True)
        along = jnp.mean(grad * level, axis=-1, keepdims=True)
        return scale * (grad - mean - level * along)

    def second_norm_back():
        def chunk(span, base):
            value = cotangent[span, :].astype(full) + norm_back(span, Table.GAIN_TWO, Table.SHIFT_TWO)
            grad_middle[span, :] = value
            branch[span, :] = value.astype(low)
            tally(Table.OUT, value.astype(low).astype(full))
            tally(Table.DOWN, cotangent[span, :].astype(full))

        over_rows(rows, chunk)

    def first_norm_back():
        stored("output")

        def chunk(span, base):
            value = grad_middle[span, :] + norm_back(span, Table.GAIN_ONE, Table.SHIFT_ONE)
            finished[span, :] = value.astype(low)

        over_rows(rows, chunk)
        store("tokens", finished, o_tokens)

    def attention_back(first, last):
        attend_back(first, last, big, mask, grad_attended, sums, weights_low, grad_low)

    def pack():
        group = lax.broadcasted_iota(jnp.int32, (8, 128), 1) // 32
        line = lax.broadcasted_iota(jnp.int32, (8, 128), 0)
        shape = s_part.shape[:4]
        for device in range(math.prod(shape)):
            i, base = device % 4, 32 * (device - device % 4)
            mixed = jnp.zeros((8, 128), full)
            for q in range(4):
                tile = sums[q, :, pl.ds(base, 128)]
                turned = tile if i == q else pltpu.roll(tile, 32 * ((q - i) % 4), 1)
                mixed = jnp.where(group == q, turned, mixed)
            share = jnp.broadcast_to(wide_sums[:, pl.ds(128 * device, 128)], (8, 128))
            at, k = divmod(device, shape[3])
            at, m = divmod(at, shape[2])
            s_part[at // shape[1], at % shape[1], m, k] = jnp.where(line == 0, share, mixed)

    base = len(units) + 1

    def unit_steps(unit):
        index, start, columns = sums_units[unit]
        piece = Sum(
            place, mail, base + unit, SUM_KINDS[unit],
            parts.at[unit % HELD], inbox.at[unit % INBOXES], wide_in.at[unit], late_in.at[unit],
        )

        def first():
            if unit >= INBOXES:
                pl.semaphore_wait(free_sem.at[unit], 1)
            piece.first()

        def last():
            halves = piece.last()
            if index == 3:
                final = r_tall.at[unit]
                for half, value in enumerate(halves):
                    final[half] = value
                store(f"part {unit}", final, outs[index].at[:, :, :, pl.ds(start, columns)])
            else:
                final = r_square.at[unit - 4]
                for half, value in enumerate(halves):
                    for k in range(value.shape[0]):
                        final[half, :, pl.ds(TILE * k, TILE)] = value[k]
                store(f"part {unit}", final, outs[index].at[:, :, pl.ds(start, columns)])
            if unit + INBOXES < len(sums_units):
                pl.semaphore_signal(
                    free_sem.at[unit + INBOXES], inc=1, device_id=place.other_core, device_id_type=MESH
                )

        return first, piece.second, piece.third, piece.fourth, last

    def small_steps():
        unit = base + len(sums_units)
        held = s_core

        def first():
            mail.send(unit, 7, s_part.at[:, :, :, 1 - c], held, place.other_core)

        def second():
            mail.arrived(unit, 7, held, place.other_core)
            for a, b in corners:
                held[a, b] = held[a, b] + s_part[a, b, :, c]
            mail.send(unit, 5, held.at[1 - y], s_wide, place.along_y)

        def third():
            mail.arrived(unit, 5, s_wide, place.along_y)
            held[y] = held[y] + s_wide[...]
            mail.send(unit, 3, held.at[y, 1 - x], s_near, place.along_x)

        def fourth():
            mail.arrived(unit, 3, s_near, place.along_x)
            held[y, x] = held[y, x] + s_near[...]
            for k in range(nz):
                q = place.ahead[k]
                mail.send(unit, k, held.at[y, x, q], s_column.at[k], place.column(q))

        def last():
            total = held[y, x, z]
            for k in range(nz):
                mail.arrived(unit, k, s_column.at[k], place.column(place.behind[k]))
                total = total + s_column[k]
            s_result[...] = total
            store("small", s_result, o_small)

        return first, second, third, fourth, last

    scatters = [unit_steps(unit) for unit in range(len(sums_units))] + [small_steps()]

    begun, landed, used = set(), set(), set()

    def try_load(unit):
        same = [u for u in range(unit) if places[u][0] is places[unit][0] and places[u][1] == places[unit][1]]
        if unit in landed and unit not in begun and used.issuperset(same):
            begun.add(unit)
            loads[unit].start()

    def use(unit, step, *args):
        loads[unit].wait()
        step(unit, *args)
        used.add(unit)
        for later in range(unit + 1, len(units)):
            try_load(later)

    passed = set()

    def reload(name):
        passed.add(name)
        if len(passed) == 5:
            start_all((get_projected, get_attended))

    def projection(unit):
        use(unit, project, (Table.QUERY, None, Table.VALUE)[unit])
        if unit == 2:
            store("projected", projected, a_projected)

    def attention(half):
        attend(half * pairs // 2, (half + 1) * pairs // 2, projected, mask, attended)
        if half == 1:
            store("attended", attended, a_attended)

    def first_norm():
        table.expand(PLANE * PLANE * depth * CORES)
        norm(Table.GAIN_ONE, Table.SHIFT_ONE)

    def second_norm():
        use(3, project_out)
        norm(Table.GAIN_TWO, Table.SHIFT_TWO)
        stored("projected")
        stored("attended")

    def rises(number):
        use(4 + number, rise, number)
        if number == 3:
            start_all(get_up[0] + get_up[1])

    def falls(number):
        use(8 + number, fall, number, TILE)
        if number == 3:
            store("output", finished, o_output)
            start_all(get_down[0] + get_down[1])
            reload("fall")

    def branch_back():
        second_norm_back()
        get_start.start()

    def heads_back(quarter):
        if quarter == 0:
            get_projected.wait()
        attention_back(quarter * pairs // 4, (quarter + 1) * pairs // 4)

    def norm_again():
        get_start.wait()
        norm(Table.GAIN_ONE, Table.SHIFT_ONE)

    def gradient(unit):
        if unit == 8:
            get_attended.wait()
        part_of(unit)
        if unit < 4:
            reload(unit)

    def gather(unit, phase):
        if unit == 0:
            small_gather[phase]()
        gathers[unit][phase]()
        if phase == 4:
            landed.add(unit)
            try_load(unit)

    actions = {
        "g": gather,
        "s": lambda unit, phase: scatters[unit][phase](),
        "prepare": prepare,
        "norm1": first_norm,
        "project": projection,
        "attend": attention,
        "norm2": second_norm,
        "rise": rises,
        "fall": falls,
        "hidden": hidden_step,
        "up": up_step,
        "branch": branch_back,
        "out": out_step,
        "heads": heads_back,
        "again": norm_again,
        "qkv": qkv_step,
        "tokens": first_norm_back,
        "pack": pack,
        "part": gradient,
    }
    get_tokens.start()
    pack_vectors()
    place.greet()
    for name, *args in ORDER:
        actions[name](*args)
    for name in list(stores):
        stored(name)
    mail.finish()


def run_layer(mesh, tokens, cotangent, lengths, codes, matrices, vectors):
    depth = mesh.shape["fsdp"] // CORES
    grid = (PLANE, PLANE, depth, CORES)
    plane = (PLANE, PLANE, depth)
    rows, width = tokens.shape
    hidden = matrices[2].shape[1]
    devices = mesh.size
    low, full = jnp.bfloat16, jnp.float32
    halves = [m.reshape(2, m.shape[0] // 2, m.shape[1]) for m in matrices]
    units = unit_list([(m.shape[0] * devices, m.shape[1]) for m in matrices])
    sums_units = [u for index in (3, 2, 1, 0) for u in units if u[0] == index]
    count = len(units)
    talls = sum(u[0] == 3 for u in units)
    share = width // devices // 2
    block = (2, width // TILE, share, TILE)
    inner = block[1:]

    def shaped(*shape, dtype=low):
        return jax.ShapeDtypeStruct(shape, dtype)

    anywhere = pl.BlockSpec(memory_space=pl.ANY)
    vmem = pl.BlockSpec(memory_space=pltpu.VMEM)
    smem = pl.BlockSpec(memory_space=pltpu.SMEM)
    out_shape = [shaped(*grid, *h.shape) for h in halves]
    out_shape += [shaped(rows, 3 * width), shaped(rows, width), shaped(rows, width, dtype=full)]
    out_shape += [shaped(rows, width), shaped(rows, width)]
    out_shape += [shaped(2, share, m.shape[1], dtype=full) for m in matrices[:3]]
    out_shape += [shaped(2, hidden // width, share, width, dtype=full), shaped(8, 128, dtype=full)]
    scratch = [
        ((8, 128), full),
        ((*grid, 8, 128), full),
        ((4, 8, width), full),
        ((1, hidden), full),
        ((INBOXES, *plane, *block), low),
        ((count, 2, PLANE, depth, *inner), low),
        ((count, 4 * depth - 2, *inner), low),
        ((count - talls, 2, share, width), full),
        ((talls, *block), full),
        ((HELD, *grid, *block), low),
        ((*grid, 8, 128), full),
        ((*plane, 8, 128), full),
        ((PLANE, depth, 8, 128), full),
        ((depth, 8, 128), full),
        ((depth - 1, 8, 128), full),
        ((8, 128), full),
        ((rows, hidden), low),
        ((rows, hidden), low),
        ((2, *grid, 2, share, width), low),
        ((2, *grid, 2, share * (hidden // width), TILE), low),
        ((rows, width), full),
        ((rows, width), full),
        ((rows, width), full),
        ((rows, width), low),
        ((rows, width), low),
        ((rows, width), low),
        ((rows, width), low),
        ((2, rows, rows), low),
        ((2, rows, rows), low),
        ((rows, rows), full),
        ((4, 8, width), full),
        ((1, hidden), full),
    ]
    outs = pl.pallas_call(
        functools.partial(layer_kernel, depth, units, sums_units),
        out_shape=out_shape,
        in_specs=[anywhere] * 4 + [vmem] * 9 + [anywhere, vmem, smem, smem],
        out_specs=[anywhere] * len(out_shape),
        scratch_shapes=[pltpu.VMEM(shape, dtype) for shape, dtype in scratch]
        + [
            pltpu.SemaphoreType.DMA((2 * count + 2, SLOTS)),
            pltpu.SemaphoreType.DMA((2 * count + 2, SLOTS)),
            pltpu.SemaphoreType.DMA((count + 1,)),
            pltpu.SemaphoreType.DMA((64,)),
            pltpu.SemaphoreType.DMA((24,)),
            pltpu.SemaphoreType.REGULAR((count,)),
        ],
        compiler_params=pltpu.CompilerParams(
            collective_id=0, has_side_effects=True, vmem_limit_bytes=62 << 20
        ),
    )(*halves, *vectors, tokens, cotangent, lengths, codes)
    output, grad_tokens = outs[7:9]
    grads = [o.reshape(-1, o.shape[-1]) for o in outs[9:13]]
    return output, grad_tokens, grads, outs[13]


def deliver_kernel(count, *refs):
    arrays, small = refs[:count], refs[count]
    results, vectors = refs[count + 1 : 2 * count + 1], refs[2 * count + 1 : -count - 2]
    held, came, went = refs[-count - 2 : -2], refs[-2], refs[-1]
    copies = [pltpu.make_async_copy(arrays[k], held[k], came.at[k]) for k in range(count)]
    onward = [pltpu.make_async_copy(held[k], results[k], went.at[k]) for k in range(count)]
    for copy in copies:
        copy.start()
    narrow = vectors[0].shape[0]
    vectors[-1][...] = small[0:1, :].reshape(128)
    for k, vector in enumerate(vectors[:-1]):
        line = small[1 + k // 4 : 2 + k // 4, :]
        if k % 4:
            line = pltpu.roll(line, 128 - narrow * (k % 4), 1)
        vector[...] = line[:, 0:narrow].reshape(narrow)
    for first, second in zip(copies, onward):
        first.wait()
        second.start()
    for copy in onward:
        copy.wait()


def deliver(arrays, small, narrow, wide):
    anywhere = pl.BlockSpec(memory_space=pl.ANY)
    vmem = pl.BlockSpec(memory_space=pltpu.VMEM)
    sizes = [narrow] * 8 + [wide]
    return pl.pallas_call(
        functools.partial(deliver_kernel, len(arrays)),
        out_shape=[jax.ShapeDtypeStruct(a.shape, a.dtype) for a in arrays]
        + [jax.ShapeDtypeStruct((size,), jnp.float32) for size in sizes],
        in_specs=[anywhere] * len(arrays) + [vmem],
        out_specs=[anywhere] * len(arrays) + [vmem] * len(sizes),
        scratch_shapes=[pltpu.VMEM(a.shape, a.dtype) for a in arrays]
        + [pltpu.SemaphoreType.DMA((len(arrays),))] * 2,
        compiler_params=pltpu.CompilerParams(vmem_limit_bytes=62 << 20),
    )(*arrays, small)


def grid_body(mesh, tokens, cotangent, lengths, scale_codes, *params):
    matrices = params[:4]
    (gain_one, shift_one, bias_query, bias_value, bias_out, gain_two, shift_two, bias_up, bias_down) = params[4:]
    vectors = (gain_one, shift_one, bias_query, bias_value, bias_out, gain_two, shift_two, bias_down, bias_up)
    output, grad_tokens, grads, small = run_layer(
        mesh, tokens, cotangent, lengths, scale_codes, matrices, vectors
    )
    wide, narrow = params[11].shape[0], params[4].shape[0]
    results = deliver([output, grad_tokens, *grads], small, narrow, wide)
    output, grad_tokens, *grads = results[:6]
    *small, grad_up_bias = results[6:]
    return (output, grad_tokens, *grads, *small[:7], grad_up_bias, small[7])


def solution(mesh):
    placed = (
        P(("dp", "fsdp"), None),
        P(("dp", "fsdp"), None),
        P(("dp", "fsdp"), None),
        P(("dp", "fsdp"), None),
        P(("dp", "fsdp"), None),
        P(("dp", "fsdp"), None),
        P(("dp", "fsdp"), None),
        P(("dp", "fsdp"), None),
        P(("dp", "fsdp")),
        P(("dp", "fsdp")),
        P(("dp", "fsdp")),
        P(("dp", "fsdp")),
        P(("dp", "fsdp")),
        P(("dp", "fsdp")),
        P(("dp", "fsdp")),
        P(("dp", "fsdp")),
        P(("dp", "fsdp")),
    )
    per_device = body
    if mesh.shape["dp"] == PLANE * PLANE and mesh.shape["fsdp"] == 4 * CORES:
        per_device = functools.partial(grid_body, mesh)
    return jax.shard_map(
        per_device,
        mesh=mesh,
        in_specs=placed,
        out_specs=(
            P(("dp", "fsdp"), None),
            P(("dp", "fsdp"), None),
            P(("dp", "fsdp"), None),
            P(("dp", "fsdp"), None),
            P(("dp", "fsdp"), None),
            P(("dp", "fsdp"), None),
            P(("dp", "fsdp")),
            P(("dp", "fsdp")),
            P(("dp", "fsdp")),
            P(("dp", "fsdp")),
            P(("dp", "fsdp")),
            P(("dp", "fsdp")),
            P(("dp", "fsdp")),
            P(("dp", "fsdp")),
            P(("dp", "fsdp")),
        ),
        check_vma=False,
    )
```

```python
import functools
import math

import jax
import jax.numpy as jnp
from jax import lax
from jax.experimental import pallas as pl
from jax.experimental.pallas import tpu as pltpu
from jax.sharding import PartitionSpec as P

HEADS = 16
HEAD_DIM = 64


EPSILON = 1e-06


def contract(left, right, left_dim, right_dim):
    return lax.dot_general(
        left, right, (((left_dim,), (right_dim,)), ((), ())), preferred_element_type=jnp.float32
    )


def layer_norm(values, gain, shift):
    centred = values - jnp.mean(values, axis=-1, keepdims=True)
    variance = jnp.mean(centred * centred, axis=-1, keepdims=True)
    return centred * lax.rsqrt(variance + EPSILON) * gain + shift


def gelu_exact(values):
    return jax.nn.gelu(values, approximate=False)


def row_tables(length_row, code_row, row_count, feat_width):
    items = jnp.arange(length_row.shape[0], dtype=jnp.int32)
    item_starts = jnp.sum(
        jnp.where(items[None, :] < items[:, None], length_row[None, :], 0), axis=1
    )
    item_ends = item_starts + length_row
    row_index = jnp.arange(row_count, dtype=jnp.int32)
    member = (
        (row_index[:, None] >= item_starts[None, :]) & (row_index[:, None] < item_ends[None, :])
    ).astype(jnp.int32)
    item_ids = jnp.arange(length_row.shape[0], dtype=jnp.int32)
    segment = jnp.sum(member * item_ids[None, :], axis=1)
    place = row_index - jnp.sum(member * item_starts[None, :], axis=1)
    row_code = jnp.sum(member * code_row[None, :], axis=1)
    half_width = feat_width // 2
    frequency = jnp.exp(
        jnp.arange(half_width, dtype=jnp.float32) * (-math.log(10000.0) / half_width)
    )
    gsd_ratio = 0.5 * (row_code.astype(jnp.float32) + 1.0)
    phase_angle = (place.astype(jnp.float32) * gsd_ratio)[:, None] * frequency[None, :]
    return (segment, jnp.concatenate([jnp.sin(phase_angle), jnp.cos(phase_angle)], axis=1))


def body(
    tokens,
    cotangent,
    lengths,
    scale_codes,
    w_qkv,
    w_out,
    w_up,
    w_down,
    ln1_gain,
    ln1_shift,
    bias_query,
    bias_value,
    bias_out,
    ln2_gain,
    ln2_shift,
    bias_up,
    bias_down,
):
    gathered = (
        lax.all_gather(w_qkv, ("dp", "fsdp"), axis=0, tiled=True),
        lax.all_gather(w_out, ("dp", "fsdp"), axis=0, tiled=True),
        lax.all_gather(w_up, ("dp", "fsdp"), axis=0, tiled=True),
        lax.all_gather(w_down, ("dp", "fsdp"), axis=0, tiled=True),
        lax.all_gather(ln1_gain, ("dp", "fsdp"), axis=0, tiled=True),
        lax.all_gather(ln1_shift, ("dp", "fsdp"), axis=0, tiled=True),
        lax.all_gather(bias_query, ("dp", "fsdp"), axis=0, tiled=True),
        lax.all_gather(bias_value, ("dp", "fsdp"), axis=0, tiled=True),
        lax.all_gather(bias_out, ("dp", "fsdp"), axis=0, tiled=True),
        lax.all_gather(ln2_gain, ("dp", "fsdp"), axis=0, tiled=True),
        lax.all_gather(ln2_shift, ("dp", "fsdp"), axis=0, tiled=True),
        lax.all_gather(bias_up, ("dp", "fsdp"), axis=0, tiled=True),
        lax.all_gather(bias_down, ("dp", "fsdp"), axis=0, tiled=True),
    )
    (
        full_qkv,
        full_out,
        full_up,
        full_down,
        gain_first,
        shift_first,
        query_bias,
        value_bias,
        out_bias,
        gain_second,
        shift_second,
        up_bias,
        down_bias,
    ) = gathered
    gain_one = gain_first.astype(jnp.float32)
    shift_one = shift_first.astype(jnp.float32)
    gain_two = gain_second.astype(jnp.float32)
    shift_two = shift_second.astype(jnp.float32)
    row_count, model_width = tokens.shape
    head_width = model_width // HEADS
    score_scale = 1.0 / math.sqrt(HEAD_DIM)
    segment, encoding = row_tables(lengths[0], scale_codes[0], row_count, model_width)
    same_item = segment[:, None] == segment[None, :]
    start = tokens.astype(jnp.float32) + encoding
    normed_one = layer_norm(start, gain_one, shift_one).astype(jnp.bfloat16)
    qkv_bias = jnp.concatenate([query_bias, jnp.zeros_like(query_bias), value_bias]).astype(
        jnp.float32
    )
    projected = (
        jnp.dot(normed_one, full_qkv, preferred_element_type=jnp.float32) + qkv_bias
    ).astype(jnp.bfloat16)

    def split_heads(block):
        return block.reshape(row_count, HEADS, head_width).transpose(1, 0, 2)

    def join_heads(block):
        return block.transpose(1, 0, 2).reshape(row_count, model_width)

    query_heads = split_heads(projected[:, :model_width])
    key_heads = split_heads(projected[:, model_width : 2 * model_width])
    value_heads = split_heads(projected[:, 2 * model_width :])

    def forward_head(operands):
        query_head, key_head, value_head = operands
        scores = contract(query_head, key_head, 1, 1) * score_scale
        scores = jnp.where(same_item, scores, -1e30)
        top_score = jnp.max(scores, axis=1, keepdims=True)
        expon = jnp.exp(scores - top_score)
        total = jnp.sum(expon, axis=1, keepdims=True)
        weights_low = (expon / total).astype(jnp.bfloat16)
        result = jnp.dot(weights_low, value_head, preferred_element_type=jnp.float32)
        return (result, (top_score + jnp.log(total))[:, 0])

    attended_heads, log_totals = lax.map(forward_head, (query_heads, key_heads, value_heads))
    attended = join_heads(attended_heads).astype(jnp.bfloat16)
    middle = (
        start
        + jnp.dot(attended, full_out, preferred_element_type=jnp.float32)
        + out_bias.astype(jnp.float32)
    )
    normed_two = layer_norm(middle, gain_two, shift_two).astype(jnp.bfloat16)
    hidden_pre = jnp.dot(normed_two, full_up, preferred_element_type=jnp.float32) + up_bias.astype(
        jnp.float32
    )
    activated = gelu_exact(hidden_pre).astype(jnp.bfloat16)
    feed_out = jnp.dot(activated, full_down, preferred_element_type=jnp.float32) + down_bias.astype(
        jnp.float32
    )
    output = (middle + feed_out).astype(jnp.bfloat16)
    back_qkv, back_out, back_up, back_down = (
        lax.all_gather(w_qkv, ("dp", "fsdp"), axis=0, tiled=True),
        lax.all_gather(w_out, ("dp", "fsdp"), axis=0, tiled=True),
        lax.all_gather(w_up, ("dp", "fsdp"), axis=0, tiled=True),
        lax.all_gather(w_down, ("dp", "fsdp"), axis=0, tiled=True),
    )
    grad_output = cotangent.astype(jnp.float32)
    grad_down_bias = jnp.sum(grad_output, axis=0)
    grad_down = contract(activated, cotangent, 0, 0)
    grad_act = contract(cotangent, back_down, 1, 1)
    gelu_value, gelu_pull = jax.vjp(gelu_exact, hidden_pre)
    grad_hidden = gelu_pull(grad_act)[0].astype(jnp.bfloat16)
    grad_up_bias = jnp.sum(grad_hidden.astype(jnp.float32), axis=0)
    grad_up = contract(normed_two, grad_hidden, 0, 0)
    grad_normed_two = contract(grad_hidden, back_up, 1, 1)
    norm_value, second_pull = jax.vjp(layer_norm, middle, gain_two, shift_two)
    grad_middle_part, grad_gain_two, grad_shift_two = second_pull(grad_normed_two)
    grad_middle = grad_output + grad_middle_part
    branch_grad = grad_middle.astype(jnp.bfloat16)
    grad_out_bias = jnp.sum(branch_grad.astype(jnp.float32), axis=0)
    grad_out_weight = contract(attended, branch_grad, 0, 0)
    grad_attended = contract(branch_grad, back_out, 1, 1).astype(jnp.bfloat16)
    grad_heads = split_heads(grad_attended)

    def backward_head(operands):
        query_head, key_head, value_head, grad_head, log_total = operands
        scores = contract(query_head, key_head, 1, 1) * score_scale
        weights = jnp.where(same_item, jnp.exp(scores - log_total[:, None]), 0.0)
        weights_low = weights.astype(jnp.bfloat16)
        grad_weights = contract(grad_head, value_head, 1, 1)
        grad_value = contract(weights_low, grad_head, 0, 0)
        grad_scores = weights * (
            grad_weights - jnp.sum(weights * grad_weights, axis=1, keepdims=True)
        )
        grad_scores_low = grad_scores.astype(jnp.bfloat16)
        grad_query = (
            jnp.dot(grad_scores_low, key_head, preferred_element_type=jnp.float32) * score_scale
        )
        grad_key = contract(grad_scores_low, query_head, 0, 0) * score_scale
        return (grad_query, grad_key, grad_value)

    grad_query_heads, grad_key_heads, grad_value_heads = lax.map(
        backward_head, (query_heads, key_heads, value_heads, grad_heads, log_totals)
    )
    grad_projected = jnp.concatenate(
        [join_heads(grad_query_heads), join_heads(grad_key_heads), join_heads(grad_value_heads)],
        axis=1,
    ).astype(jnp.bfloat16)
    grad_query_bias = jnp.sum(grad_projected[:, :model_width].astype(jnp.float32), axis=0)
    grad_value_bias = jnp.sum(grad_projected[:, 2 * model_width :].astype(jnp.float32), axis=0)
    grad_qkv = contract(normed_one, grad_projected, 0, 0)
    grad_normed_one = contract(grad_projected, back_qkv, 1, 1)
    first_value, first_pull = jax.vjp(layer_norm, start, gain_one, shift_one)
    grad_start_part, grad_gain_one, grad_shift_one = first_pull(grad_normed_one)
    grad_tokens = (grad_middle + grad_start_part).astype(jnp.bfloat16)
    every_grad = (
        lax.psum_scatter(grad_qkv, ("dp", "fsdp"), scatter_dimension=0, tiled=True),
        lax.psum_scatter(grad_out_weight, ("dp", "fsdp"), scatter_dimension=0, tiled=True),
        lax.psum_scatter(grad_up, ("dp", "fsdp"), scatter_dimension=0, tiled=True),
        lax.psum_scatter(grad_down, ("dp", "fsdp"), scatter_dimension=0, tiled=True),
        lax.psum_scatter(grad_gain_one, ("dp", "fsdp"), scatter_dimension=0, tiled=True),
        lax.psum_scatter(grad_shift_one, ("dp", "fsdp"), scatter_dimension=0, tiled=True),
        lax.psum_scatter(grad_query_bias, ("dp", "fsdp"), scatter_dimension=0, tiled=True),
        lax.psum_scatter(grad_value_bias, ("dp", "fsdp"), scatter_dimension=0, tiled=True),
        lax.psum_scatter(grad_out_bias, ("dp", "fsdp"), scatter_dimension=0, tiled=True),
        lax.psum_scatter(grad_gain_two, ("dp", "fsdp"), scatter_dimension=0, tiled=True),
        lax.psum_scatter(grad_shift_two, ("dp", "fsdp"), scatter_dimension=0, tiled=True),
        lax.psum_scatter(grad_up_bias, ("dp", "fsdp"), scatter_dimension=0, tiled=True),
        lax.psum_scatter(grad_down_bias, ("dp", "fsdp"), scatter_dimension=0, tiled=True),
    )
    (
        shard_qkv,
        shard_out,
        shard_up,
        shard_down,
        shard_gain_one,
        shard_shift_one,
        shard_query_bias,
        shard_value_bias,
        shard_out_bias,
        shard_gain_two,
        shard_shift_two,
        shard_up_bias,
        shard_down_bias,
    ) = every_grad
    return (
        output,
        grad_tokens,
        shard_qkv,
        shard_out,
        shard_up,
        shard_down,
        shard_gain_one,
        shard_shift_one,
        shard_query_bias,
        shard_value_bias,
        shard_out_bias,
        shard_gain_two,
        shard_shift_two,
        shard_up_bias,
        shard_down_bias,
    )


PLANE = 2
CORES = 2
UNIT = 1024 * 1024
MESH = pl.DeviceIdType.MESH
ALL = slice(None)


class Place:
    def __init__(self, depth):
        dp, fsdp = lax.axis_index("dp"), lax.axis_index("fsdp")
        self.y, self.x = dp // PLANE, lax.rem(dp, PLANE)
        self.z, self.c = fsdp // CORES, lax.rem(fsdp, CORES)
        self.depth = depth
        y, x, z, c = self.y, self.x, self.z, self.c
        self.along_x = self.device(y, 1 - x, z, c)
        self.along_y = self.device(1 - y, x, z, c)
        self.other_core = self.device(y, x, z, 1 - c)
        self.ahead = [lax.rem(z + k, depth) for k in range(1, depth)]
        self.behind = [lax.rem(z + depth - k, depth) for k in range(1, depth)]

    def device(self, y, x, z, c):
        return (y * PLANE + x, z * CORES + c)

    def column(self, z):
        return self.device(self.y, self.x, z, self.c)

    def greet(self):
        partners = [self.column(q) for q in self.ahead]
        partners += [self.along_x, self.along_y, self.other_core]
        barrier = pltpu.get_barrier_semaphore()
        for partner in partners:
            pl.semaphore_signal(barrier, inc=1, device_id=partner, device_id_type=MESH)
        pl.semaphore_wait(barrier, len(partners))


class Mail:
    def __init__(self, send_sem, recv_sem):
        self.send_sem, self.recv_sem, self.sent = send_sem, recv_sem, {}

    def copy(self, unit, slot, source, target, device):
        return pltpu.make_async_remote_copy(
            src_ref=source,
            dst_ref=target,
            send_sem=self.send_sem.at[unit, slot],
            recv_sem=self.recv_sem.at[unit, slot],
            device_id=device,
            device_id_type=MESH,
        )

    def send(self, unit, slot, source, target, device):
        copy = self.copy(unit, slot, source, target, device)
        copy.start()
        self.sent[unit, slot] = copy

    def arrived(self, unit, slot, target, device):
        self.copy(unit, slot, target, target, device).wait_recv()

    def settle(self, unit, slot):
        self.sent.pop((unit, slot)).wait_send()

    def finish(self):
        for at in list(self.sent):
            self.settle(*at)


SLOTS = 14


def unit_list(shapes):
    units = []
    for index, (rows, columns) in enumerate(shapes):
        width = UNIT // rows
        units += [(index, first, width) for first in range(0, columns, width)]
    return units


def small_gather_phases(place, mail, unit, source, full, local_sem):
    y, x, z, c = place.y, place.x, place.z, place.c
    nz = place.depth - 1

    def first():
        pltpu.make_async_copy(source, full.at[y, x, z, c], local_sem).start()
        for k in range(nz):
            mail.send(unit, k, source, full.at[y, x, z, c], place.column(place.ahead[k]))

    def second():
        pltpu.make_async_copy(source, full.at[y, x, z, c], local_sem).wait()
        for k in range(nz):
            q = place.behind[k]
            mail.arrived(unit, k, full.at[y, x, q, c], place.column(q))
        mail.send(unit, 3, full.at[y, x, :, c], full.at[y, x, :, c], place.along_x)

    def third():
        mail.arrived(unit, 3, full.at[y, 1 - x, :, c], place.along_x)
        mail.send(unit, 5, full.at[y, :, :, c], full.at[y, :, :, c], place.along_y)

    def fourth():
        mail.arrived(unit, 5, full.at[1 - y, :, :, c], place.along_y)
        mail.send(unit, 7, full.at[:, :, :, c], full.at[:, :, :, c], place.other_core)

    def last():
        mail.arrived(unit, 7, full.at[:, :, :, 1 - c], place.other_core)

    return first, second, third, fourth, last


def by_rows(left, right):
    return contract(left, right, 1, 1)


def by_columns(left, right):
    return contract(left, right, 0, 0)


def plain(left, right):
    return jnp.dot(left, right, preferred_element_type=jnp.float32)


class Table:
    GAIN_ONE, SHIFT_ONE, QUERY, VALUE, OUT, GAIN_TWO, SHIFT_TWO, DOWN = range(8)

    def __init__(self, packed, narrow, wide):
        self.packed, self.narrow, self.wide = packed, narrow, wide

    def expand(self, devices):
        y_count, x_count, z_count, c_count = self.packed.shape[:4]

        def tile(d):
            d, c = divmod(d, c_count)
            d, z = divmod(d, z_count)
            y, x = divmod(d, x_count)
            return self.packed[y, x, z, c]

        group = lax.broadcasted_iota(jnp.int32, (8, 128), 1) // 32
        for base in range(0, devices, 4):
            tiles = [tile(base + i) for i in range(4)]
            for i in range(4):
                self.wide[:, pl.ds(128 * (base + i), 128)] = tiles[i][0:1, :]
            for q in range(4):
                mixed = jnp.zeros((8, 128), jnp.float32)
                for i in range(4):
                    turned = tiles[i] if i == q else pltpu.roll(tiles[i], 32 * ((i - q) % 4), 1)
                    mixed = jnp.where(group == i, turned, mixed)
                self.narrow[q, :, pl.ds(32 * base, 128)] = mixed

    def __getitem__(self, index):
        return self.narrow[index % 4, 1 + index // 4 : 2 + index // 4, :]


def row_facts(lengths, codes, row):
    begin = jnp.int32(0)
    segment = jnp.zeros(row.shape, jnp.int32)
    first = jnp.zeros(row.shape, jnp.int32)
    code = jnp.full(row.shape, codes[0, 0], jnp.int32)
    for item in range(1, lengths.shape[1]):
        begin = begin + lengths[0, item - 1]
        inside = row >= begin
        segment = jnp.where(inside, item, segment)
        first = jnp.where(inside, begin, first)
        code = jnp.where(inside, codes[0, item], code)
    return segment, (row - first).astype(jnp.float32) * (0.5 * (code.astype(jnp.float32) + 1.0))


def fill_mask(lengths, codes, mask):
    rows = mask.shape[0]
    across, _ = row_facts(lengths, codes, lax.broadcasted_iota(jnp.int32, (1, rows), 1))
    for base in range(0, rows, 128):
        down, _ = row_facts(lengths, codes, lax.broadcasted_iota(jnp.int32, (128, 1), 0) + base)
        mask[base : base + 128, :] = jnp.where(down == across, 0.0, -1e30)


def head_half(rows, which):
    lane = lax.broadcasted_iota(jnp.int32, (rows, 2 * HEAD_DIM), 1)
    return (lane >= HEAD_DIM) if which else (lane < HEAD_DIM)


def pair_span(pair, offset):
    return pl.ds(pl.multiple_of(offset + pair * 2 * HEAD_DIM, 2 * HEAD_DIM), 2 * HEAD_DIM)


def attend(first_pair, last_pair, projected, mask, attended):
    rows, width = attended.shape
    zero = jnp.zeros((), jnp.bfloat16)
    scale = jnp.asarray(1.0 / math.sqrt(HEAD_DIM), jnp.bfloat16)

    def one_pair(pair, carry):
        query = projected[:, pair_span(pair, 0)] * scale
        key = projected[:, pair_span(pair, width)]
        value = projected[:, pair_span(pair, 2 * width)]
        results = []
        for which in range(2):
            scores = by_rows(jnp.where(head_half(rows, which), query, zero), key) + mask[...]
            top = jnp.max(scores, axis=1, keepdims=True)
            expon = jnp.exp(scores - top)
            total = jnp.sum(expon, axis=1, keepdims=True)
            weights = (expon * (1.0 / total)).astype(jnp.bfloat16)
            results.append(plain(weights, value))
        mixed = jnp.where(head_half(rows, 0), results[0], results[1])
        attended[:, pair_span(pair, 0)] = mixed.astype(jnp.bfloat16)
        return carry

    lax.fori_loop(first_pair, last_pair, one_pair, 0)


CHUNK = 64


def over_rows(rows, step):
    def one(index, carry):
        step(pl.ds(pl.multiple_of(index * CHUNK, CHUNK), CHUNK), index * CHUNK)
        return carry

    lax.fori_loop(0, rows // CHUNK, one, 0)


def normalised(values):
    centred = values - jnp.mean(values, axis=-1, keepdims=True)
    variance = jnp.mean(centred * centred, axis=-1, keepdims=True)
    scale = lax.rsqrt(variance + EPSILON)
    return centred * scale, scale


def attend_back(first_pair, last_pair, projected, mask, grad_attended, sums, weights_low, grad_low):
    rows, width = grad_attended.shape
    zero = jnp.zeros((), jnp.bfloat16)
    scale = 1.0 / math.sqrt(HEAD_DIM)

    def one_pair(pair, carry):
        query, key, value = (projected[:, pair_span(pair, k * width)] for k in range(3))
        grad = grad_attended[:, pair_span(pair, 0)]
        scaled = query * jnp.asarray(scale, jnp.bfloat16)
        g_query, g_key, g_value = [], [], []
        for which in range(2):
            keep = head_half(rows, which)
            scores = by_rows(jnp.where(keep, key, zero), scaled) + mask[...]
            expon = jnp.exp(scores - jnp.max(scores, axis=0, keepdims=True))
            weights = expon * (1.0 / jnp.sum(expon, axis=0, keepdims=True))
            weights_low[which] = weights.astype(jnp.bfloat16)
            slopes = by_rows(jnp.where(keep, value, zero), grad)
            level = jnp.sum(weights * slopes, axis=0, keepdims=True)
            grad_low[which] = (weights * (slopes - level)).astype(jnp.bfloat16)
            g_value.append(plain(weights_low[which], grad))
            g_key.append(plain(grad_low[which], query))
            g_query.append(by_columns(grad_low[which], key))
        keep = head_half(rows, 0)
        for k, (parts, factor) in enumerate(((g_query, scale), (g_key, scale), (g_value, 1.0))):
            mixed = (jnp.where(keep, parts[0], parts[1]) * factor).astype(jnp.bfloat16)
            projected[:, pair_span(pair, k * width)] = mixed
            if k != 1:
                slot = Table.QUERY if k == 0 else Table.VALUE
                total = jnp.sum(mixed.astype(jnp.float32), axis=0, keepdims=True)
                sums[slot % 4, 1 + slot // 4 : 2 + slot // 4, pair_span(pair, 0)] = total
        return carry

    lax.fori_loop(first_pair, last_pair, one_pair, 0)


def gather_phases(place, mail, unit, kind, source, full, local_sem):
    y, x, z, c = place.y, place.x, place.z, place.c
    nz = place.depth - 1

    def begin():
        pltpu.make_async_copy(source, full(y, x, z, c, ALL), local_sem).start()
        for k in range(nz):
            mail.send(unit, k, source, full(y, x, z, c, ALL), place.column(place.ahead[k]))
        if kind:
            mail.send(unit, 3, source.at[0], full(y, x, z, c, 0), place.along_x)
            mail.send(unit, 4, source.at[1], full(y, x, z, c, 1), place.along_y)

    def second():
        pltpu.make_async_copy(source, full(y, x, z, c, ALL), local_sem).wait()
        if kind:
            for slot, partner, block in (
                (3, place.along_x, full(y, 1 - x, z, c, 0)),
                (4, place.along_y, full(1 - y, x, z, c, 1)),
            ):
                mail.arrived(unit, slot, block, partner)
                for k in range(nz):
                    mail.send(unit, 8 + 3 * (slot - 3) + k, block, block, place.column(place.ahead[k]))
            return
        for k in range(nz):
            q = place.behind[k]
            mail.arrived(unit, k, full(y, x, q, c, ALL), place.column(q))
        mail.send(unit, 3, full(y, x, ALL, c, 0), full(y, x, ALL, c, 0), place.along_x)
        mail.send(unit, 4, full(y, x, ALL, c, 1), full(y, x, ALL, c, 1), place.along_y)

    def third():
        if kind:
            for k in range(nz):
                q = place.behind[k]
                mail.arrived(unit, k, full(y, x, q, c, ALL), place.column(q))
            for k in range(nz):
                q = place.behind[k]
                mail.arrived(unit, 8 + k, full(y, 1 - x, q, c, 0), place.column(q))
        else:
            mail.arrived(unit, 3, full(y, 1 - x, ALL, c, 0), place.along_x)
        mail.send(unit, 5, full(y, ALL, ALL, c, 0), full(y, ALL, ALL, c, 0), place.along_y)
        if kind:
            for k in range(nz):
                q = place.behind[k]
                mail.arrived(unit, 11 + k, full(1 - y, x, q, c, 1), place.column(q))
        else:
            mail.arrived(unit, 4, full(1 - y, x, ALL, c, 1), place.along_y)
        mail.send(unit, 6, full(ALL, x, ALL, c, 1), full(ALL, x, ALL, c, 1), place.along_x)

    def fourth():
        mail.arrived(unit, 5, full(1 - y, ALL, ALL, c, 0), place.along_y)
        mail.arrived(unit, 6, full(ALL, 1 - x, ALL, c, 1), place.along_x)
        mail.send(unit, 7, full(ALL, ALL, ALL, c, ALL), full(ALL, ALL, ALL, c, ALL), place.other_core)

    def last():
        mail.arrived(unit, 7, full(ALL, ALL, ALL, 1 - c, ALL), place.other_core)

    return begin, second, third, fourth, last


class Sum:
    def __init__(self, place, mail, unit, kind, part, held, wide, late):
        self.place, self.mail, self.unit, self.kind = place, mail, unit, kind
        self.part, self.held, self.wide, self.late = part, held, wide, late
        self.nz = place.depth - 1

    def first(self):
        p = self.place
        self.mail.send(self.unit, 7, self.part.at[:, :, :, 1 - p.c], self.held, p.other_core)

    def second(self):
        p, mail, unit, held = self.place, self.mail, self.unit, self.held
        mail.arrived(unit, 7, held, p.other_core)
        for a in range(PLANE):
            for b in range(PLANE):
                held[a, b] = held[a, b] + self.part[a, b, :, p.c]
        mail.send(unit, 5, held.at[1 - p.y, :, :, 0], self.wide.at[0], p.along_y)
        mail.send(unit, 6, held.at[:, 1 - p.x, :, 1], self.wide.at[1], p.along_x)
        mail.settle(unit, 7)

    def pair(self, half, k):
        return self.late.at[pl.ds(2 * (self.nz * half + k), 2)]

    def near(self, half):
        depth = self.nz + 1
        return self.late.at[pl.ds(depth * half, depth)]

    def column(self, k):
        return self.late.at[pl.ds(2 * (self.nz + 1) + 2 * k, 2)]

    def final(self, half):
        return self.late.at[4 * self.nz + half]

    def third(self):
        p, mail, unit, held, wide = self.place, self.mail, self.unit, self.held, self.wide
        y, x = p.y, p.x
        mail.arrived(unit, 5, wide.at[0], p.along_y)
        for b in range(PLANE):
            held[y, b, :, 0] = held[y, b, :, 0] + wide[0, b]
        if self.kind:
            for k in range(self.nz):
                q = p.ahead[k]
                mail.send(unit, 8 + k, held.at[y, :, q, 0], self.pair(0, k), p.column(q))
        else:
            mail.send(unit, 3, held.at[y, 1 - x, :, 0], self.near(0), p.along_x)
        mail.arrived(unit, 6, wide.at[1], p.along_x)
        for b in range(PLANE):
            held[b, x, :, 1] = held[b, x, :, 1] + wide[1, b]
        if self.kind:
            for k in range(self.nz):
                q = p.ahead[k]
                mail.send(unit, 11 + k, held.at[:, x, q, 1], self.pair(1, k), p.column(q))
        else:
            mail.send(unit, 4, held.at[1 - y, x, :, 1], self.near(1), p.along_y)

    def fourth(self):
        p, mail, unit, held = self.place, self.mail, self.unit, self.held
        y, x, z = p.y, p.x, p.z
        full = jnp.float32
        if self.kind:
            for half in range(2):
                at = (y, ALL, z, 0) if half == 0 else (ALL, x, z, 1)
                total = held[at].astype(full)
                for k in range(self.nz):
                    mail.arrived(unit, 8 + 3 * half + k, self.pair(half, k), p.column(p.behind[k]))
                    total = total + self.pair(half, k)[...].astype(full)
                held[at] = total.astype(held.dtype)
            mail.send(unit, 3, held.at[y, 1 - x, z, 0], self.final(0), p.along_x)
            mail.send(unit, 4, held.at[1 - y, x, z, 1], self.final(1), p.along_y)
            return
        mail.arrived(unit, 3, self.near(0), p.along_x)
        mail.arrived(unit, 4, self.near(1), p.along_y)
        for half in range(2):
            held[y, x, :, half] = held[y, x, :, half] + self.near(half)[...]
        for k in range(self.nz):
            q = p.ahead[k]
            mail.send(unit, k, held.at[y, x, q], self.column(k), p.column(q))

    def last(self):
        p, mail, unit, held = self.place, self.mail, self.unit, self.held
        full = jnp.float32
        halves = [held[p.y, p.x, p.z, half].astype(full) for half in range(2)]
        if self.kind:
            mail.arrived(unit, 3, self.final(0), p.along_x)
            mail.arrived(unit, 4, self.final(1), p.along_y)
            halves = [v + self.final(half)[...].astype(full) for half, v in enumerate(halves)]
        else:
            for k in range(self.nz):
                mail.arrived(unit, k, self.column(k), p.column(p.behind[k]))
                halves = [v + self.column(k)[half].astype(full) for half, v in enumerate(halves)]
        for slot in [s for u, s in list(mail.sent) if u == unit]:
            mail.settle(unit, slot)
        return halves


INBOXES = 6
HELD = 4
TILE = 256
GATHER_KINDS = (0, 0, 0, 0, 0, 1, 0, 1, 0, 1, 0, 1)
SUM_KINDS = (0, 1, 0, 1, 0, 1, 0, 1, 0, 0, 0, 0)
ORDER = (
    ("g", 0, 0), ("prepare",), ("g", 1, 0), ("g", 0, 1), ("g", 2, 0), ("g", 0, 2), ("g", 3, 0), ("g", 1, 1),
    ("g", 2, 1), ("g", 4, 0), ("g", 3, 1), ("g", 1, 2), ("g", 0, 3), ("g", 5, 0), ("g", 5, 1), ("g", 2, 2),
    ("g", 4, 1), ("g", 6, 0), ("g", 0, 4), ("g", 1, 3), ("g", 3, 2), ("g", 7, 0), ("g", 7, 1), ("g", 5, 2),
    ("g", 1, 4), ("g", 6, 1), ("g", 8, 0), ("g", 9, 0), ("g", 2, 3), ("norm1",), ("project", 0), ("g", 2, 4),
    ("project", 1), ("g", 4, 2), ("g", 6, 2), ("g", 3, 3), ("project", 2), ("g", 10, 0), ("attend", 0), ("g", 7, 2),
    ("attend", 1), ("g", 6, 3), ("g", 3, 4), ("g", 5, 3), ("g", 10, 1), ("g", 4, 3), ("norm2",), ("g", 8, 1),
    ("g", 9, 1), ("g", 4, 4), ("g", 11, 0), ("g", 5, 4), ("g", 7, 3), ("g", 6, 4), ("g", 10, 2), ("rise", 0),
    ("g", 7, 4), ("rise", 1), ("g", 8, 2), ("rise", 2), ("g", 11, 1), ("g", 10, 3), ("g", 9, 2), ("rise", 3),
    ("part", 0), ("part", 1), ("g", 11, 2), ("g", 8, 3), ("s", 0, 0), ("part", 2), ("s", 1, 0), ("part", 3),
    ("g", 10, 4), ("s", 2, 0), ("g", 8, 4), ("g", 9, 3), ("s", 1, 1), ("fall", 0), ("s", 0, 1), ("g", 9, 4),
    ("g", 11, 3), ("fall", 1), ("s", 3, 0), ("fall", 2), ("g", 11, 4), ("fall", 3), ("hidden", 0), ("part", 4),
    ("s", 2, 1), ("hidden", 1), ("s", 1, 2), ("hidden", 2), ("s", 0, 2), ("part", 5), ("hidden", 3), ("s", 4, 0),
    ("s", 3, 1), ("up", 0), ("s", 5, 0), ("s", 2, 2), ("up", 1), ("part", 6), ("s", 0, 3), ("up", 2), ("s", 5, 1),
    ("part", 7), ("s", 1, 3), ("up", 3), ("s", 2, 3), ("branch",), ("s", 4, 1), ("s", 3, 2), ("s", 0, 4), ("out",),
    ("s", 6, 0), ("heads", 0), ("s", 6, 1), ("s", 1, 4), ("part", 8), ("s", 2, 4), ("s", 7, 0), ("s", 8, 0),
    ("s", 4, 2), ("heads", 1), ("s", 5, 2), ("s", 8, 1), ("s", 3, 3), ("again",), ("s", 7, 1), ("heads", 2),
    ("s", 4, 3), ("heads", 3), ("s", 6, 2), ("s", 3, 4), ("part", 9), ("s", 8, 2), ("s", 9, 0), ("s", 7, 2),
    ("s", 5, 3), ("s", 9, 1), ("part", 10), ("s", 4, 4), ("s", 10, 0), ("s", 5, 4), ("part", 11), ("s", 10, 1),
    ("qkv", 0), ("qkv", 1), ("s", 8, 3), ("s", 11, 0), ("s", 6, 3), ("s", 9, 2), ("qkv", 2), ("qkv", 3), ("s", 11, 1),
    ("tokens",), ("pack",), ("s", 9, 3), ("s", 10, 2), ("s", 6, 4), ("s", 11, 2), ("s", 12, 0), ("s", 10, 3),
    ("s", 12, 1), ("s", 12, 2), ("s", 11, 3), ("s", 12, 3), ("s", 7, 3), ("s", 9, 4), ("s", 12, 4), ("s", 8, 4),
    ("s", 10, 4), ("s", 7, 4), ("s", 11, 4),
)


def layer_kernel(depth, units, sums_units, *refs):
    refs = list(refs)

    def take(count):
        taken = refs[:count]
        del refs[:count]
        return taken

    sources = take(4)
    vectors = take(9)
    tokens, cotangent, lengths, codes = take(4)
    fulls = take(4)
    a_projected, a_attended, a_start = take(3)
    o_output, o_tokens = take(2)
    outs = take(4)
    (o_small,) = take(1)
    small, packed, narrow, wide = take(4)
    inbox, wide_in, late_in, r_square, r_tall, parts = take(6)
    s_part, s_core, s_wide, s_near, s_column, s_result = take(6)
    big, hidden_grad, square, tall, stream, grad_middle, grad_normed = take(7)
    normed, branch, grad_attended, finished, weights_low, grad_low, mask, sums, wide_sums = take(9)
    send_sem, recv_sem, local_sem, load_sem, store_sem, free_sem = take(6)

    place, mail = Place(depth), Mail(send_sem, recv_sem)
    y, x, z, c = place.y, place.x, place.z, place.c
    nz = depth - 1
    rows, width = stream.shape
    hidden = hidden_grad.shape[1]
    pairs = width // (2 * HEAD_DIM)
    low, full = jnp.bfloat16, jnp.float32
    table = Table(packed, narrow, wide)
    projected, attended = big.at[:, pl.ds(0, 3 * width)], big.at[:, pl.ds(3 * width, width)]
    corners = [(a, b) for a in range(PLANE) for b in range(PLANE)]
    stores, numbers = {}, iter(range(64))

    def store(name, source, target):
        copy = pltpu.make_async_copy(source, target, store_sem.at[len(stores)])
        copy.start()
        stores[name] = [copy, True]

    def stored(name):
        if stores[name][1]:
            stores[name][0].wait()
            stores[name][1] = False

    def load(source, target):
        return pltpu.make_async_copy(source, target, load_sem.at[next(numbers)])

    def flat(block):
        return block.reshape(-1, block.shape[-1])

    def pack_vectors():
        narrow[...] = jnp.zeros_like(narrow)
        count = vectors[0].shape[0]
        for k, ref in enumerate(vectors[:-1]):
            narrow[k % 4, k // 4 : k // 4 + 1, 0:count] = ref[...].astype(full).reshape(1, count)
        small[...] = jnp.zeros_like(small)
        small[0:1, :] = vectors[-1][...].astype(full).reshape(1, 128)
        for line in range(2):
            total = narrow[0, line : line + 1, 0:128]
            for q in range(1, 4):
                total = total + pltpu.roll(narrow[q, line : line + 1, 0:128], count * q, 1)
            small[1 + line : 2 + line, :] = total

    def piece(unit):
        index, first, columns = units[unit]
        span = pl.ds(first, columns)

        def view(*at):
            return fulls[index].at[at + (ALL, span)]

        return sources[index].at[:, :, span], view

    gathers = [
        gather_phases(place, mail, unit + 1, GATHER_KINDS[unit], *piece(unit), local_sem.at[unit + 1])
        for unit in range(len(units))
    ]
    small_gather = small_gather_phases(place, mail, 0, small, packed, local_sem.at[0])
    places = []
    for unit, (index, first, columns) in enumerate(units):
        buffer = tall if index == 3 else square
        places.append((buffer, sum((u[0] == 3) == (index == 3) for u in units[:unit]) % 2))
    loads = [
        load(piece(unit)[1](ALL, ALL, ALL, ALL, ALL), buffer.at[at])
        for unit, (buffer, at) in enumerate(places)
    ]

    def weights(unit, columns):
        buffer, at = places[unit]
        return flat(buffer[at, :, :, :, :, :, :, columns])

    def corner_loads(index, corner, buffer, at):
        a, b = corners[corner]
        chosen = [u for u in units if u[0] == index]
        return [
            load(
                fulls[index].at[a, b, :, :, :, :, pl.ds(first, columns)],
                buffer.at[at, e // PLANE, e % PLANE],
            )
            for e, (_, first, columns) in enumerate(chosen)
        ]

    get_down = [corner_loads(3, n, tall, n % 2) for n in range(4)]
    get_up = [corner_loads(2, n, square, n % 2) for n in range(4)]
    get_out = [
        load(fulls[1].at[a, b], square.at[0, n // PLANE, n % PLANE]) for n, (a, b) in enumerate(corners)
    ]
    get_qkv = [corner_loads(0, n, square, (n + 1) % 2) for n in range(4)]
    get_projected = load(a_projected, projected)
    get_attended = load(a_attended, attended)
    get_start = load(a_start, stream)

    def start_all(copies):
        for copy in copies:
            copy.start()

    def wait_all(copies):
        for copy in copies:
            copy.wait()

    get_tokens = load(tokens, finished)

    def prepare():
        get_tokens.wait()
        def chunk(span, base):
            row = lax.broadcasted_iota(jnp.int32, (CHUNK, 1), 0) + base
            _, factor = row_facts(lengths, codes, row)
            lane = lax.broadcasted_iota(jnp.int32, (1, width // 2), 1).astype(full)
            phase = factor * jnp.exp(lane * (-math.log(10000.0) / (width // 2)))
            left, right = pl.ds(0, width // 2), pl.ds(width // 2, width // 2)
            stream[span, left] = finished[span, left].astype(full) + jnp.sin(phase)
            stream[span, right] = finished[span, right].astype(full) + jnp.cos(phase)

        over_rows(rows, chunk)
        store("start", stream, a_start)
        fill_mask(lengths, codes, mask)
        sums[...] = jnp.zeros_like(sums)

    def norm(gain, shift):
        def chunk(span, base):
            normed[span, :] = (normalised(stream[span, :])[0] * table[gain] + table[shift]).astype(low)

        over_rows(rows, chunk)

    def project(unit, bias):
        tile = 512
        for first in range(0, width, tile):
            value = plain(normed[...], weights(unit, pl.ds(first, tile)))
            if bias is not None:
                value = value + table[bias][:, first : first + tile]
            big[:, pl.ds(unit * width + first, tile)] = value.astype(low)

    def project_out(unit):
        tile = 512
        stored("start")
        for first in range(0, width, tile):
            span = pl.ds(first, tile)
            value = plain(attended[...], weights(unit, span)) + table[Table.OUT][:, first : first + tile]
            stream[:, span] = stream[:, span] + value

    def rise(unit, number):
        def one(index, carry):
            at = pl.multiple_of(index * TILE, TILE)
            there = pl.ds(pl.multiple_of(number * width + at, TILE), TILE)
            pre = plain(normed[...], weights(unit, pl.ds(at, TILE))) + wide[:, there]
            normal = 0.5 * (1.0 + lax.erf(pre * math.sqrt(0.5)))
            density = jnp.exp(pre * pre * -0.5) * (1.0 / math.sqrt(2.0 * math.pi))
            big[:, there] = (pre * normal).astype(low)
            hidden_grad[:, there] = (normal + pre * density).astype(low)
            return carry

        lax.fori_loop(0, width // TILE, one, 0)

    def fall(unit, number, columns):
        span = pl.ds(number * columns, columns)
        value = plain(big[...], weights(unit, ALL)) + table[Table.DOWN][:, number * columns : (number + 1) * columns]
        finished[:, span] = (stream[:, span] + value).astype(low)

    def tally(slot, values):
        at = (slot % 4, pl.ds(1 + slot // 4, 1), ALL)
        sums[at] = sums[at] + jnp.sum(values, axis=0, keepdims=True)

    def square_part(unit, left, right, first):
        for k in range(width // TILE):
            value = by_columns(left[...], right[:, pl.ds(first + TILE * k, TILE)]).astype(low)
            parts[unit % HELD, :, :, :, :, :, k] = value.reshape(parts.shape[1:6] + (parts.shape[7], TILE))

    def tall_part(unit, first):
        def one(corner, carry):
            left = big[:, pl.ds(pl.multiple_of(corner * width, width), width)]
            value = by_columns(left, cotangent[:, pl.ds(first, TILE)]).astype(low)
            parts[unit % HELD, corner // PLANE, lax.rem(corner, PLANE)] = value.reshape(parts.shape[3:])
            return carry

        lax.fori_loop(0, PLANE * PLANE, one, 0)

    def part_of(unit):
        index, first, columns = sums_units[unit]
        if index == 3:
            tall_part(unit, first)
        elif index == 2:
            square_part(unit, normed, hidden_grad, first)
        elif index == 1:
            square_part(unit, attended, branch, 0)
        else:
            square_part(unit, normed, big, first)

    def hidden_step(n):
        wait_all(get_down[n])

        def one(m, carry):
            block = jnp.concatenate(
                [flat(tall[n % 2, e // PLANE, e % PLANE, m]) for e in range(4)], axis=1
            )
            span = pl.ds(pl.multiple_of(n * width + m * TILE, TILE), TILE)
            value = (by_rows(cotangent[...], block) * hidden_grad[:, span].astype(full)).astype(low)
            hidden_grad[:, span] = value
            wide_sums[:, span] = jnp.sum(value.astype(full), axis=0, keepdims=True)
            return carry

        lax.fori_loop(0, width // TILE, one, 0)
        if n + 2 < 4:
            start_all(get_down[n + 2])

    def back_through(copies, left, at, n):
        wait_all(copies)
        total = None
        for e in range(len(copies)):
            value = by_rows(left[:, pl.ds(e * width, width)], flat(square[at, e // PLANE, e % PLANE]))
            total = value if total is None else total + value
        grad_normed[:, pl.ds(TILE * n, TILE)] = total

    def up_step(n):
        back_through(get_up[n], hidden_grad, n % 2, n)
        if n + 2 < 4:
            start_all(get_up[n + 2])
        if n == 2:
            start_all(get_out)
        if n == 3:
            start_all(get_qkv[0])

    def out_step():
        wait_all(get_out)
        for n in range(4):
            block = flat(square[0, n // PLANE, n % PLANE])
            grad_attended[:, pl.ds(TILE * n, TILE)] = by_rows(branch[...], block).astype(low)
        start_all(get_qkv[1])

    def qkv_step(n):
        back_through(get_qkv[n], big, (n + 1) % 2, n)
        if n + 2 < 4:
            start_all(get_qkv[n + 2])

    def norm_back(span, gain, shift):
        level, scale = normalised(stream[span, :])
        grad = grad_normed[span, :]
        tally(gain, grad * level)
        tally(shift, grad)
        grad = grad * table[gain]
        mean = jnp.mean(grad, axis=-1, keepdims=True)
        along = jnp.mean(grad * level, axis=-1, keepdims=True)
        return scale * (grad - mean - level * along)

    def second_norm_back():
        def chunk(span, base):
            value = cotangent[span, :].astype(full) + norm_back(span, Table.GAIN_TWO, Table.SHIFT_TWO)
            grad_middle[span, :] = value
            branch[span, :] = value.astype(low)
            tally(Table.OUT, value.astype(low).astype(full))
            tally(Table.DOWN, cotangent[span, :].astype(full))

        over_rows(rows, chunk)

    def first_norm_back():
        stored("output")

        def chunk(span, base):
            value = grad_middle[span, :] + norm_back(span, Table.GAIN_ONE, Table.SHIFT_ONE)
            finished[span, :] = value.astype(low)

        over_rows(rows, chunk)
        store("tokens", finished, o_tokens)

    def attention_back(first, last):
        attend_back(first, last, big, mask, grad_attended, sums, weights_low, grad_low)

    def pack():
        group = lax.broadcasted_iota(jnp.int32, (8, 128), 1) // 32
        line = lax.broadcasted_iota(jnp.int32, (8, 128), 0)
        shape = s_part.shape[:4]
        for device in range(math.prod(shape)):
            i, base = device % 4, 32 * (device - device % 4)
            mixed = jnp.zeros((8, 128), full)
            for q in range(4):
                tile = sums[q, :, pl.ds(base, 128)]
                turned = tile if i == q else pltpu.roll(tile, 32 * ((q - i) % 4), 1)
                mixed = jnp.where(group == q, turned, mixed)
            share = jnp.broadcast_to(wide_sums[:, pl.ds(128 * device, 128)], (8, 128))
            at, k = divmod(device, shape[3])
            at, m = divmod(at, shape[2])
            s_part[at // shape[1], at % shape[1], m, k] = jnp.where(line == 0, share, mixed)

    base = len(units) + 1

    def unit_steps(unit):
        index, start, columns = sums_units[unit]
        piece = Sum(
            place, mail, base + unit, SUM_KINDS[unit],
            parts.at[unit % HELD], inbox.at[unit % INBOXES], wide_in.at[unit], late_in.at[unit],
        )

        def first():
            if unit >= INBOXES:
                pl.semaphore_wait(free_sem.at[unit], 1)
            piece.first()

        def last():
            halves = piece.last()
            if index == 3:
                final = r_tall.at[unit]
                for half, value in enumerate(halves):
                    final[half] = value
                store(f"part {unit}", final, outs[index].at[:, :, :, pl.ds(start, columns)])
            else:
                final = r_square.at[unit - 4]
                for half, value in enumerate(halves):
                    for k in range(value.shape[0]):
                        final[half, :, pl.ds(TILE * k, TILE)] = value[k]
                store(f"part {unit}", final, outs[index].at[:, :, pl.ds(start, columns)])
            if unit + INBOXES < len(sums_units):
                pl.semaphore_signal(
                    free_sem.at[unit + INBOXES], inc=1, device_id=place.other_core, device_id_type=MESH
                )

        return first, piece.second, piece.third, piece.fourth, last

    def small_steps():
        unit = base + len(sums_units)
        held = s_core

        def first():
            mail.send(unit, 7, s_part.at[:, :, :, 1 - c], held, place.other_core)

        def second():
            mail.arrived(unit, 7, held, place.other_core)
            for a, b in corners:
                held[a, b] = held[a, b] + s_part[a, b, :, c]
            mail.send(unit, 5, held.at[1 - y], s_wide, place.along_y)

        def third():
            mail.arrived(unit, 5, s_wide, place.along_y)
            held[y] = held[y] + s_wide[...]
            mail.send(unit, 3, held.at[y, 1 - x], s_near, place.along_x)

        def fourth():
            mail.arrived(unit, 3, s_near, place.along_x)
            held[y, x] = held[y, x] + s_near[...]
            for k in range(nz):
                q = place.ahead[k]
                mail.send(unit, k, held.at[y, x, q], s_column.at[k], place.column(q))

        def last():
            total = held[y, x, z]
            for k in range(nz):
                mail.arrived(unit, k, s_column.at[k], place.column(place.behind[k]))
                total = total + s_column[k]
            s_result[...] = total
            store("small", s_result, o_small)

        return first, second, third, fourth, last

    scatters = [unit_steps(unit) for unit in range(len(sums_units))] + [small_steps()]

    begun, landed, used = set(), set(), set()

    def try_load(unit):
        same = [u for u in range(unit) if places[u][0] is places[unit][0] and places[u][1] == places[unit][1]]
        if unit in landed and unit not in begun and used.issuperset(same):
            begun.add(unit)
            loads[unit].start()

    def use(unit, step, *args):
        loads[unit].wait()
        step(unit, *args)
        used.add(unit)
        for later in range(unit + 1, len(units)):
            try_load(later)

    passed = set()

    def reload(name):
        passed.add(name)
        if len(passed) == 5:
            start_all((get_projected, get_attended))

    def projection(unit):
        use(unit, project, (Table.QUERY, None, Table.VALUE)[unit])
        if unit == 2:
            store("projected", projected, a_projected)

    def attention(half):
        attend(half * pairs // 2, (half + 1) * pairs // 2, projected, mask, attended)
        if half == 1:
            store("attended", attended, a_attended)

    def first_norm():
        table.expand(PLANE * PLANE * depth * CORES)
        norm(Table.GAIN_ONE, Table.SHIFT_ONE)

    def second_norm():
        use(3, project_out)
        norm(Table.GAIN_TWO, Table.SHIFT_TWO)
        stored("projected")
        stored("attended")

    def rises(number):
        use(4 + number, rise, number)
        if number == 3:
            start_all(get_up[0] + get_up[1])

    def falls(number):
        use(8 + number, fall, number, TILE)
        if number == 3:
            store("output", finished, o_output)
            start_all(get_down[0] + get_down[1])
            reload("fall")

    def branch_back():
        second_norm_back()
        get_start.start()

    def heads_back(quarter):
        if quarter == 0:
            get_projected.wait()
        attention_back(quarter * pairs // 4, (quarter + 1) * pairs // 4)

    def norm_again():
        get_start.wait()
        norm(Table.GAIN_ONE, Table.SHIFT_ONE)

    def gradient(unit):
        if unit == 8:
            get_attended.wait()
        part_of(unit)
        if unit < 4:
            reload(unit)

    def gather(unit, phase):
        if unit == 0:
            small_gather[phase]()
        gathers[unit][phase]()
        if phase == 4:
            landed.add(unit)
            try_load(unit)

    actions = {
        "g": gather,
        "s": lambda unit, phase: scatters[unit][phase](),
        "prepare": prepare,
        "norm1": first_norm,
        "project": projection,
        "attend": attention,
        "norm2": second_norm,
        "rise": rises,
        "fall": falls,
        "hidden": hidden_step,
        "up": up_step,
        "branch": branch_back,
        "out": out_step,
        "heads": heads_back,
        "again": norm_again,
        "qkv": qkv_step,
        "tokens": first_norm_back,
        "pack": pack,
        "part": gradient,
    }
    get_tokens.start()
    pack_vectors()
    place.greet()
    for name, *args in ORDER:
        actions[name](*args)
    for name in list(stores):
        stored(name)
    mail.finish()


def run_layer(mesh, tokens, cotangent, lengths, codes, matrices, vectors):
    depth = mesh.shape["fsdp"] // CORES
    grid = (PLANE, PLANE, depth, CORES)
    plane = (PLANE, PLANE, depth)
    rows, width = tokens.shape
    hidden = matrices[2].shape[1]
    devices = mesh.size
    low, full = jnp.bfloat16, jnp.float32
    halves = [m.reshape(2, m.shape[0] // 2, m.shape[1]) for m in matrices]
    units = unit_list([(m.shape[0] * devices, m.shape[1]) for m in matrices])
    sums_units = [u for index in (3, 2, 1, 0) for u in units if u[0] == index]
    count = len(units)
    talls = sum(u[0] == 3 for u in units)
    share = width // devices // 2
    block = (2, width // TILE, share, TILE)
    inner = block[1:]

    def shaped(*shape, dtype=low):
        return jax.ShapeDtypeStruct(shape, dtype)

    anywhere = pl.BlockSpec(memory_space=pl.ANY)
    vmem = pl.BlockSpec(memory_space=pltpu.VMEM)
    smem = pl.BlockSpec(memory_space=pltpu.SMEM)
    out_shape = [shaped(*grid, *h.shape) for h in halves]
    out_shape += [shaped(rows, 3 * width), shaped(rows, width), shaped(rows, width, dtype=full)]
    out_shape += [shaped(rows, width), shaped(rows, width)]
    out_shape += [shaped(2, share, m.shape[1], dtype=full) for m in matrices[:3]]
    out_shape += [shaped(2, hidden // width, share, width, dtype=full), shaped(8, 128, dtype=full)]
    scratch = [
        ((8, 128), full),
        ((*grid, 8, 128), full),
        ((4, 8, width), full),
        ((1, hidden), full),
        ((INBOXES, *plane, *block), low),
        ((count, 2, PLANE, depth, *inner), low),
        ((count, 4 * depth - 2, *inner), low),
        ((count - talls, 2, share, width), full),
        ((talls, *block), full),
        ((HELD, *grid, *block), low),
        ((*grid, 8, 128), full),
        ((*plane, 8, 128), full),
        ((PLANE, depth, 8, 128), full),
        ((depth, 8, 128), full),
        ((depth - 1, 8, 128), full),
        ((8, 128), full),
        ((rows, hidden), low),
        ((rows, hidden), low),
        ((2, *grid, 2, share, width), low),
        ((2, *grid, 2, share * (hidden // width), TILE), low),
        ((rows, width), full),
        ((rows, width), full),
        ((rows, width), full),
        ((rows, width), low),
        ((rows, width), low),
        ((rows, width), low),
        ((rows, width), low),
        ((2, rows, rows), low),
        ((2, rows, rows), low),
        ((rows, rows), full),
        ((4, 8, width), full),
        ((1, hidden), full),
    ]
    outs = pl.pallas_call(
        functools.partial(layer_kernel, depth, units, sums_units),
        out_shape=out_shape,
        in_specs=[anywhere] * 4 + [vmem] * 9 + [anywhere, vmem, smem, smem],
        out_specs=[anywhere] * len(out_shape),
        scratch_shapes=[pltpu.VMEM(shape, dtype) for shape, dtype in scratch]
        + [
            pltpu.SemaphoreType.DMA((2 * count + 2, SLOTS)),
            pltpu.SemaphoreType.DMA((2 * count + 2, SLOTS)),
            pltpu.SemaphoreType.DMA((count + 1,)),
            pltpu.SemaphoreType.DMA((64,)),
            pltpu.SemaphoreType.DMA((24,)),
            pltpu.SemaphoreType.REGULAR((count,)),
        ],
        compiler_params=pltpu.CompilerParams(
            collective_id=0, has_side_effects=True, vmem_limit_bytes=62 << 20
        ),
    )(*halves, *vectors, tokens, cotangent, lengths, codes)
    output, grad_tokens = outs[7:9]
    grads = [o.reshape(-1, o.shape[-1]) for o in outs[9:13]]
    return output, grad_tokens, grads, outs[13]


def deliver_kernel(count, *refs):
    arrays, small = refs[:count], refs[count]
    results, vectors = refs[count + 1 : 2 * count + 1], refs[2 * count + 1 : -count - 2]
    held, came, went = refs[-count - 2 : -2], refs[-2], refs[-1]
    copies = [pltpu.make_async_copy(arrays[k], held[k], came.at[k]) for k in range(count)]
    onward = [pltpu.make_async_copy(held[k], results[k], went.at[k]) for k in range(count)]
    for copy in copies:
        copy.start()
    narrow = vectors[0].shape[0]
    vectors[-1][...] = small[0:1, :].reshape(128)
    for k, vector in enumerate(vectors[:-1]):
        line = small[1 + k // 4 : 2 + k // 4, :]
        if k % 4:
            line = pltpu.roll(line, 128 - narrow * (k % 4), 1)
        vector[...] = line[:, 0:narrow].reshape(narrow)
    for first, second in zip(copies, onward):
        first.wait()
        second.start()
    for copy in onward:
        copy.wait()


def deliver(arrays, small, narrow, wide):
    anywhere = pl.BlockSpec(memory_space=pl.ANY)
    vmem = pl.BlockSpec(memory_space=pltpu.VMEM)
    sizes = [narrow] * 8 + [wide]
    return pl.pallas_call(
        functools.partial(deliver_kernel, len(arrays)),
        out_shape=[jax.ShapeDtypeStruct(a.shape, a.dtype) for a in arrays]
        + [jax.ShapeDtypeStruct((size,), jnp.float32) for size in sizes],
        in_specs=[anywhere] * len(arrays) + [vmem],
        out_specs=[anywhere] * len(arrays) + [vmem] * len(sizes),
        scratch_shapes=[pltpu.VMEM(a.shape, a.dtype) for a in arrays]
        + [pltpu.SemaphoreType.DMA((len(arrays),))] * 2,
        compiler_params=pltpu.CompilerParams(vmem_limit_bytes=62 << 20),
    )(*arrays, small)


def grid_body(mesh, tokens, cotangent, lengths, scale_codes, *params):
    matrices = params[:4]
    (gain_one, shift_one, bias_query, bias_value, bias_out, gain_two, shift_two, bias_up, bias_down) = params[4:]
    vectors = (gain_one, shift_one, bias_query, bias_value, bias_out, gain_two, shift_two, bias_down, bias_up)
    output, grad_tokens, grads, small = run_layer(
        mesh, tokens, cotangent, lengths, scale_codes, matrices, vectors
    )
    wide, narrow = params[11].shape[0], params[4].shape[0]
    results = deliver([output, grad_tokens, *grads], small, narrow, wide)
    output, grad_tokens, *grads = results[:6]
    *small, grad_up_bias = results[6:]
    return (output, grad_tokens, *grads, *small[:7], grad_up_bias, small[7])


def solution(mesh):
    placed = (
        P(("dp", "fsdp"), None),
        P(("dp", "fsdp"), None),
        P(("dp", "fsdp"), None),
        P(("dp", "fsdp"), None),
        P(("dp", "fsdp"), None),
        P(("dp", "fsdp"), None),
        P(("dp", "fsdp"), None),
        P(("dp", "fsdp"), None),
        P(("dp", "fsdp")),
        P(("dp", "fsdp")),
        P(("dp", "fsdp")),
        P(("dp", "fsdp")),
        P(("dp", "fsdp")),
        P(("dp", "fsdp")),
        P(("dp", "fsdp")),
        P(("dp", "fsdp")),
        P(("dp", "fsdp")),
    )
    per_device = body
    if mesh.shape["dp"] == PLANE * PLANE and mesh.shape["fsdp"] == 4 * CORES:
        per_device = functools.partial(grid_body, mesh)
    return jax.shard_map(
        per_device,
        mesh=mesh,
        in_specs=placed,
        out_specs=(
            P(("dp", "fsdp"), None),
            P(("dp", "fsdp"), None),
            P(("dp", "fsdp"), None),
            P(("dp", "fsdp"), None),
            P(("dp", "fsdp"), None),
            P(("dp", "fsdp"), None),
            P(("dp", "fsdp")),
            P(("dp", "fsdp")),
            P(("dp", "fsdp")),
            P(("dp", "fsdp")),
            P(("dp", "fsdp")),
            P(("dp", "fsdp")),
            P(("dp", "fsdp")),
            P(("dp", "fsdp")),
            P(("dp", "fsdp")),
        ),
        check_vma=False,
    )
```
